128 devices in a mesh: gx: 16 (over z, y_lo, core), gy: 8 (over x, y_hi).
Axes of the slice: x: 4, y: 4 (y_hi: 2, y_lo: 2; y = y_hi * 2 + y_lo), z: 4, core: 2. Of those that a mesh axis runs over, the one named last changes fastest.
Arguments:
- phi: bfloat16 [2048, 80, 4, 256], P('gx', 'gy'), may hold values from -1 to 1, as said below
- potential: float32 [80, 4, 256], P('gy'), may hold values from 0 to 2
- kernel: bfloat16 [2048, 2048], P('gx'), may hold values from -0.25 to 0.25
- mask_s: int32 [32, 32], P('gx'), may hold values from 0 to 1, as said below
- mask_k: int32 [32, 32], P('gx'), may hold values from 0 to 1, as said below
Outputs:
- kernel_next: float32 [2048, 2048], P('gx', 'gy')
The draws below stay inside these ranges and needn't reach their ends.
Inputs may be any that keep to these rules, and one draw needn't show every extreme that they name: `phi`: each block of 64 NGWFs has a box of 2 * max(13, 1) + 1 planes along the first grid dimension (periodic) around its centre; every NGWF is zero outside its block's box. mask_s[a, b] is 1 exactly where the periodic distance of the box centres of blocks a and b is at most h + h // 2, with h = max(13, 1); it is symmetric with ones on the diagonal. mask_k is symmetric, 1 wherever the centre distance is at most 3 h, and 1 for some further pairs.
All inputs are finite; a program needn't handle non-finite values.
Results may differ from the reference program's by a relative error of at most 0.0046.
Values may be sent and summed in bfloat16 or wider, within the bound.
No kernel may reach another device: no remote copies, remote signals or barrier semaphores. Data moves between devices by JAX's collectives and lax.ppermute only.
A program may use at most 192 MiB of HBM per device.

```python
import jax
import jax.numpy as jnp

BLOCK = 64
CY = 4
CZ = 256
F = 2048
NXG = 80
NB = 32


def box_half():
    return max(NXG // 6, 1)


def block_centres(key):
    order = jax.random.permutation(jax.random.fold_in(key, 101), NB)
    jitter = jax.random.randint(jax.random.fold_in(key, 102), (NB,), 0, max(NXG // NB, 1))
    return (order * NXG // NB + jitter) % NXG


def centre_distance(key):
    centres = block_centres(key)
    apart = jnp.abs(centres[:, None] - centres[None, :])
    return jnp.minimum(apart, NXG - apart)


def draw_phi(key, part):
    centres = jnp.repeat(block_centres(key), BLOCK)
    key = jax.random.fold_in(key, 11)
    shape = (F, NXG, CY, CZ)
    noise = jnp.clip(jax.random.normal(key, shape, jnp.float32), -4.0, 4.0)
    mixed = noise + 0.6 * jnp.roll(noise, 1, 0) + 0.5 * jnp.roll(noise, 2, 0)
    planes = jnp.arange(NXG, dtype=jnp.int32)
    apart = jnp.abs(planes[None, :] - centres[:, None])
    apart = jnp.minimum(apart, NXG - apart)
    inside = (apart <= box_half()).astype(jnp.float32)
    scale = ((2 * box_half() + 1) * CY * CZ) ** (-0.5)
    return (mixed * inside[:, :, None, None] * scale).astype(jnp.bfloat16)


def draw_mask_s(key, part):
    distance = centre_distance(key)
    half = box_half()
    return (distance <= half + half // 2).astype(jnp.int32)


def draw_mask_k(key, part):
    distance = centre_distance(key)
    key = jax.random.fold_in(key, 13)
    picks = jax.random.randint(key, (NB, NB), 0, 8)
    far = (picks == 0) | (picks.T == 0)
    return ((distance <= 3 * box_half()) | far).astype(jnp.int32)


def steps_of(key, dims, cuts, least, high):
    factor_of, own = 1.0, jax.random.fold_in(key, 6)
    for axis_at, blocks in cuts:
        steps = jnp.exp(jax.random.uniform(jax.random.fold_in(own, axis_at), (blocks,), jnp.float32, least / len(cuts), high / len(cuts)))
        factor_of = factor_of * jnp.repeat(steps, dims[axis_at] // blocks).reshape([-1 if axis == axis_at else 1 for axis in range(len(dims))])
    return factor_of


def bell_draw(key, extent, deviation, reach, shards=(), held_as=jnp.bfloat16):
    array = jax.random.normal(key, extent, jnp.float32) * deviation
    if len(shards) > 0:
        array = steps_of(key, extent, shards, -0.22, 0.18) * array
    return jnp.clip(array, min=-reach, max=reach).astype(held_as)


def setup_inputs(seed: int = 0) -> dict:
    keys = jax.random.split(jax.random.key(seed), 6)
    return {
        "phi": draw_phi(jax.random.fold_in(keys[5], 71), 0),
        "potential": jnp.clip(2.0 * jax.random.uniform(keys[1], (NXG, CY, CZ), jnp.float32) ** steps_of(keys[1], (NXG, CY, CZ), ((0, 8),), -0.2, 0.2), 0.0, 2.0),
        "kernel": bell_draw(keys[2], (F, F), (F // 4) ** -0.5, 0.25, ((0, 16),)),
        "mask_s": draw_mask_s(jax.random.fold_in(keys[5], 71), 0),
        "mask_k": draw_mask_k(jax.random.fold_in(keys[5], 71), 0),
    }


def spread(values, mask):
    rows, cols = values.shape[-2], values.shape[-1]
    grid = values.reshape(values.shape[:-2] + (rows // BLOCK, BLOCK, cols // BLOCK, BLOCK))
    return (grid * mask.astype(values.dtype)[:, None, :, None]).reshape(values.shape)


def hamiltonian(phi, potential):
    field = phi.astype(jnp.float32)
    lap = -6.0 * field
    for axis in (1, 2, 3):
        lap = lap + jnp.roll(field, 1, axis) + jnp.roll(field, -1, axis)
    return (-0.5 * lap + potential[None] * field).astype(jnp.bfloat16)


def reference(phi, potential, kernel, mask_s, mask_k):
    flat = phi.reshape(F, -1)
    hflat = hamiltonian(phi, potential).reshape(F, -1)
    intersection = jnp.dot(flat, flat.T, preferred_element_type=jnp.float32)
    ham = jnp.dot(hflat, flat.T, preferred_element_type=jnp.float32)
    s_mat = spread(intersection, mask_s).astype(jnp.bfloat16)
    h_mat = spread(ham, mask_s).astype(jnp.bfloat16)
    k_mat = spread(kernel, mask_k)
    x_mat = jnp.dot(k_mat, s_mat, preferred_element_type=jnp.float32).astype(jnp.bfloat16)
    y_mat = jnp.dot(k_mat, h_mat, preferred_element_type=jnp.float32).astype(jnp.bfloat16)
    p_one = jnp.dot(h_mat, x_mat, preferred_element_type=jnp.float32).astype(jnp.bfloat16)
    p_two = jnp.dot(s_mat, y_mat, preferred_element_type=jnp.float32).astype(jnp.bfloat16)
    z_mat = jnp.dot(s_mat, x_mat, preferred_element_type=jnp.float32).astype(jnp.bfloat16)
    q_mat = (jnp.dot(p_one, x_mat, preferred_element_type=jnp.float32)
             + jnp.dot(z_mat, y_mat, preferred_element_type=jnp.float32)
             + jnp.dot(p_two, x_mat, preferred_element_type=jnp.float32))
    grad = 3.0 * (p_one.astype(jnp.float32) + p_two.astype(jnp.float32)) - 2.0 * q_mat
    return kernel.astype(jnp.float32) - 0.5 * spread(grad, mask_k)
```

```python
import jax
import jax.numpy as jnp
from jax import lax
from jax.experimental import pallas as pl
from jax.experimental.pallas import tpu as pltpu
from jax.sharding import Mesh, PartitionSpec as P

BLOCK = 64
NB = 32
SLOTS = 16
REACH = 8
LANES = 128
ROWS = ("v", "c")
PEERS = ("v", "gy")
BF = jnp.bfloat16
F32 = jnp.float32
I32 = jnp.int32
VMEM_LIMIT = 56 * 1024 * 1024


def iota(shape, dim):
    return lax.broadcasted_iota(I32, shape, dim)


def dot(left, right):
    return lax.dot_general(left, right, (((1,), (0,)), ((), ())), preferred_element_type=F32)


def dot_t(left, right):
    return lax.dot_general(left, right, (((1,), (1,)), ((), ())), preferred_element_type=F32)


def params(**more):
    return pltpu.CompilerParams(vmem_limit_bytes=VMEM_LIMIT, **more)


def pack_kernel(dev, flat, halo, mask_rows, packed, meta):
    rows = flat.shape[0]
    src, dst = iota((512, 512), 0), iota((512, 512), 1)
    wanted = ((dst >> 5) & 3) * 128 + (dst >> 7) * 32 + (dst & 31)
    perm = (src == wanted).astype(F32).astype(BF)
    for x in range(11):
        for half in range(2):
            pieces = []
            for y in range(4):
                at = y * 256 + half * 128
                if x < 10:
                    pieces.append(flat[:, x * 1024 + at : x * 1024 + at + 128])
                else:
                    pieces.append(halo[:, at : at + 128])
            out = dot(jnp.concatenate(pieces, axis=1), perm).astype(BF)
            tile = x if x < 10 else 11
            for j in range(4):
                packed[4 * half + j, :, tile * 128 : tile * 128 + 128] = out[:, j * 128 : j * 128 + 128]
    src, dst = iota((1280, 256), 0), iota((1280, 256), 1)
    plane, lane = src >> 7, src & 127
    low = (dst < 128) & ((lane & 31) == 31) & ((dst & 127) == (lane & 96) + plane)
    high = (dst >= 128) & ((lane & 31) == 0) & ((dst & 127) == (lane & 96) + 16 + plane)
    edges = (low | high).astype(F32).astype(BF)
    found = [dot(packed[v, :, :1280], edges) for v in range(8)]
    for v in range(8):
        tile = found[v][:, :128] + found[(v + 1) % 8][:, 128:]
        packed[v, :, 1280:1408] = tile.astype(BF)
    lane, row = iota((8, LANES), 1), iota((8, LANES), 0)
    total = mask_rows[...]
    start = dev[2] * 10
    for block in range(2):
        for x in range(10):
            part = jnp.abs(flat[block * 64 : block * 64 + 64, x * 1024 : x * 1024 + 1024].astype(F32))
            top = jnp.max(jnp.max(part, axis=0, keepdims=True), axis=1, keepdims=True)
            used = (top > 0.0).astype(F32)
            total = total + jnp.where((row == block) & (lane == start + x), used, 0.0)
    meta[...] = total


def pack(dev, flat, halo, mask_rows):
    vmem = pl.BlockSpec(memory_space=pltpu.VMEM)
    return pl.pallas_call(
        pack_kernel,
        out_shape=(
            jax.ShapeDtypeStruct((8, 128, 1536), BF),
            jax.ShapeDtypeStruct((8, LANES), F32),
        ),
        in_specs=[pl.BlockSpec(memory_space=pltpu.SMEM), vmem, vmem, vmem],
        out_specs=(vmem, vmem),
        compiler_params=params(),
        name="pack",
    )(dev, flat, halo, mask_rows)


def plan_kernel(dev, used_ref, near_ref, table, weights):
    gx, core, gy = dev[0], dev[1], dev[2]
    used = used_ref[...]
    near = near_ref[...]
    square = (LANES, LANES)
    zeros = jnp.zeros((96, LANES), F32)
    tall_used = jnp.concatenate([used, zeros], axis=0)
    tall_near = jnp.concatenate([near, zeros], axis=0)
    a, b = iota(square, 0), iota(square, 1)
    apart = jnp.abs(a - b)
    apart = jnp.minimum(apart, 80 - apart)
    far = ((a < 80) & (b < 80) & (apart > 13)).astype(F32)
    row, lane = iota((NB, LANES), 0), iota((NB, LANES), 1)
    outside = dot(used, far)
    fits = (outside < 0.5) & (lane < 80)
    centre = jnp.min(jnp.where(fits, lane.astype(F32), 127.0), axis=1, keepdims=True)
    key_col = centre * 32.0 + row[:, :1].astype(F32)
    key_row = jnp.sum(jnp.where(row == lane, key_col, 0.0), axis=0, keepdims=True)
    rank_col = jnp.sum(((lane < NB) & (key_row < key_col)).astype(F32), axis=1, keepdims=True)
    rank_row = jnp.sum((key_col < key_row).astype(F32), axis=0, keepdims=True)
    lane_f = lane.astype(F32)
    block_row = jnp.sum(jnp.where(rank_col == lane_f, row.astype(F32), 0.0), axis=0, keepdims=True)
    order = ((rank_row == a.astype(F32)) & (b < NB) & (a < NB)).astype(F32)
    order_rows = order[:NB]
    d8, l8 = iota((8, LANES), 0), iota((8, LANES), 1)
    ahead = l8 - 10 * d8
    ahead = jnp.where(ahead < 0, ahead + 80, ahead)
    touch = ((ahead <= 10) & (l8 < 80)).astype(F32)
    flags = (dot_t(touch, tall_used) > 0.5).astype(F32)
    flags = dot_t(flags, order)
    upper = jnp.where(l8 < SLOTS, pltpu.roll(flags, LANES - SLOTS, 1), 0.0)
    clash = jnp.max(upper * flags)
    sorted_near = dot_t(dot(order_rows, tall_near), order)
    gap = (lane - row) & 31
    stray = (sorted_near > 0.5) & (lane < NB) & (gap > REACH) & (gap < NB - REACH)
    good = (clash < 0.5) & (jnp.max(stray.astype(F32)) < 0.5)
    shift = b - core
    pick = ((a == ((gx + shift) & 15)) & (a < SLOTS)).astype(F32)
    col_half = dot(upper, pick)
    row_half = jnp.sum(jnp.where(l8 == gx, upper, 0.0), axis=1, keepdims=True)
    step = l8 - core
    allowed = ((step >= 0) & (step <= REACH)).astype(F32)
    j, lanes = iota((LANES, 1280), 0), iota((LANES, 1280), 1)
    lanes = jnp.where(lanes >= 640, lanes - 640, lanes)
    widen = ((lanes >> 6) == j).astype(F32)
    for half in range(2):
        mine = gx + 16 * half
        line = jnp.sum(jnp.where(row == mine, sorted_near, 0.0), axis=0, keepdims=True)
        pick = ((a == ((mine + shift) & 31)) & (a < NB)).astype(F32)
        line = dot(jnp.broadcast_to(line, (8, LANES)), pick)
        other = (((mine + step) & 31) >> 4).astype(F32)
        same = (row_half == float(half)) & (col_half == other)
        small = jnp.where(same, line * allowed, 0.0)
        weights[8 * half : 8 * half + 8, :] = dot(small, widen)
    own = jnp.sum(jnp.where(d8 == gy, upper, 0.0), axis=0, keepdims=True)
    source = jnp.where(own > 0.5, pltpu.roll(block_row, LANES - SLOTS, 1), block_row)
    ok = jnp.where(good, 1.0, 0.0)
    out = jnp.where(d8 == 0, source, 0.0) + jnp.where(d8 == 1, block_row, 0.0)
    out = out + jnp.where(d8 == 2, rank_row, 0.0) + jnp.where(d8 == 3, ok, 0.0)
    table[...] = jnp.where(l8 < NB, out, 0.0).astype(I32)


def plan(dev, used, near):
    vmem = pl.BlockSpec(memory_space=pltpu.VMEM)
    return pl.pallas_call(
        plan_kernel,
        out_shape=(
            jax.ShapeDtypeStruct((8, LANES), I32),
            jax.ShapeDtypeStruct((16, 1280), F32),
        ),
        in_specs=[pl.BlockSpec(memory_space=pltpu.SMEM), vmem, vmem],
        out_specs=(vmem, vmem),
        compiler_params=params(),
        name="plan",
    )(dev, used, near)


def sort_columns_kernel(table, mask, kernel, out):
    lane = iota((64, LANES), 1)
    for tile in range(16):
        for rows in range(2):
            halves = []
            for half in range(2):
                block = table[1, 2 * tile + half]
                at = pl.multiple_of((block >> 1) * 128, 128)
                part = kernel[rows * 64 : rows * 64 + 64, pl.ds(at, 128)].astype(F32)
                turned = pltpu.roll(part, 64, 1)
                part = jnp.where((block & 1) == half, part, turned)
                halves.append(part * mask[rows, block].astype(F32))
            both = jnp.where(lane < 64, halves[0], halves[1])
            out[rows * 64 : rows * 64 + 64, tile * 128 : tile * 128 + 128] = both.astype(BF)


def sort_columns(table, mask, kernel):
    vmem = pl.BlockSpec(memory_space=pltpu.VMEM)
    smem = pl.BlockSpec(memory_space=pltpu.SMEM)
    return pl.pallas_call(
        sort_columns_kernel,
        out_shape=jax.ShapeDtypeStruct((128, 2048), BF),
        in_specs=[smem, smem, vmem],
        out_specs=vmem,
        compiler_params=params(),
        name="sort_columns",
    )(table, mask, kernel)


def integrals_kernel(table, dev, own, other, pot, out, right, left_s, left_h):
    slot = pl.program_id(0)
    core = dev[1]
    block = table[0, slot]
    mine = ((block >> 1) & 1) == core
    data = jnp.where(mine, own[0], other[0])
    at = pl.multiple_of(slot * 64, 64)
    lane = iota((64, LANES), 1)
    edge = data[:, 1280:1408].astype(F32)
    swapped = jnp.where((lane & 31) < 16, pltpu.roll(edge, 112, 1), pltpu.roll(edge, 16, 1))
    right[pl.ds(at, 64), :1280] = data[:, :1280]
    right[pl.ds(at, 64), 1280:1408] = swapped.astype(BF)
    right[pl.ds(at, 64), 1408:1536] = data[:, 1408:1536]
    right[pl.ds(at, 64), 1536:1664] = data[:, 1152:1280]

    @pl.when((slot & 1) == core)
    def _():
        to = pl.multiple_of((slot >> 1) * 64, 64)
        left_s[pl.ds(to, 64), :] = data[:, :1280]
        low, high = (lane & 31) == 0, (lane & 31) == 31
        before = jnp.zeros((64, LANES), F32)
        here = data[:, :128].astype(F32)
        for x in range(10):
            after = data[:, x * 128 + 128 : x * 128 + 256].astype(F32) if x < 9 else jnp.zeros((64, LANES), F32)
            near = before + after
            near = near + pltpu.roll(here, 32, 1) + pltpu.roll(here, 96, 1)
            near = near + jnp.where(low, 0.0, pltpu.roll(here, 1, 1))
            near = near + jnp.where(high, 0.0, pltpu.roll(here, 127, 1))
            value = (3.0 + pot[x : x + 1, :]) * here - 0.5 * near
            left_h[pl.ds(to, 64), x * 128 : x * 128 + 128] = value.astype(BF)
            before, here = here, after
        left_h[pl.ds(to, 64), 1280:1408] = (-0.5 * edge).astype(BF)
        left_h[pl.ds(to, 64), 1408:1536] = (-0.5 * data[:, 1152:1280].astype(F32)).astype(BF)
        left_h[pl.ds(to, 64), 1536:1664] = (-0.5 * data[:, 1408:1536].astype(F32)).astype(BF)

    @pl.when(slot == SLOTS - 1)
    def _():
        for chunk in range(4):
            cols = right[chunk * 256 : chunk * 256 + 256, :]
            found = (dot_t(left_s[...], cols[:, :1280]), dot_t(left_h[...], cols))
            for mat in range(2):
                value = found[mat].astype(BF)
                for rows in range(8):
                    for side in range(2):
                        step = (2 * chunk + side - rows) % 8
                        if step < 5:
                            to = mat * 640 + step * 128
                            out[rows * 64 : rows * 64 + 64, to : to + 128] = value[
                                rows * 64 : rows * 64 + 64, side * 128 : side * 128 + 128
                            ]


def integrals(table, dev, own, other, pot):
    def place(parity):
        def index(slot, table, dev):
            block = table[0, slot]
            same = (((block >> 1) & 1) == dev[1]) == (parity == 0)
            return jnp.where(same, (block >> 2) * 2 + (block & 1), 0), 0, 0

        return index

    return pl.pallas_call(
        integrals_kernel,
        grid_spec=pltpu.PrefetchScalarGridSpec(
            num_scalar_prefetch=2,
            grid=(SLOTS,),
            in_specs=[
                pl.BlockSpec((1, 64, 1536), place(0)),
                pl.BlockSpec((1, 64, 1536), place(1)),
                pl.BlockSpec((16, LANES), lambda slot, table, dev: (0, 0)),
            ],
            out_specs=pl.BlockSpec((512, 1280), lambda slot, table, dev: (0, 0)),
            scratch_shapes=[
                pltpu.VMEM((1024, 1664), BF),
                pltpu.VMEM((512, 1280), BF),
                pltpu.VMEM((512, 1664), BF),
            ],
        ),
        out_shape=jax.ShapeDtypeStruct((512, 1280), BF),
        compiler_params=params(dimension_semantics=("arbitrary",)),
        name="integrals",
    )(table, dev, own.reshape(16, 64, 1536), other.reshape(16, 64, 1536), pot)


def combine_kernel(parts, weights, out):
    lines = [jnp.zeros((8, 1280), F32), jnp.zeros((8, 1280), F32)]
    for domain in range(8):
        total = parts[domain].astype(F32)
        for v in range(1, 8):
            total = total + parts[v * 8 + domain].astype(F32)
        for half in range(2):
            lines[half] = lines[half] + total * weights[8 * half + domain : 8 * half + domain + 1, :]
    out[...] = jnp.concatenate(lines, axis=0).astype(BF)


def combine(parts, weights):
    vmem = pl.BlockSpec(memory_space=pltpu.VMEM)
    return pl.pallas_call(
        combine_kernel,
        out_shape=jax.ShapeDtypeStruct((16, 1280), BF),
        in_specs=[vmem, vmem],
        out_specs=vmem,
        compiler_params=params(),
        name="combine",
    )(parts, weights)


def chain_kernel(table, dev, mask, band, k_rows, k_own, out, full, k_all, rows_i, rows_j, first, second, sems):
    gx, gy = dev[0], dev[2]
    copies = []
    for rank in range(NB):
        source = pl.multiple_of(table[1, rank] * 64, 64)
        copy = pltpu.make_async_copy(
            k_rows.at[pl.ds(source, 64), :], k_all.at[rank * 64 : rank * 64 + 64, :], sems.at[rank]
        )
        copy.start()
        copies.append(copy)
    a, b = iota((256, 256), 0), iota((256, 256), 1)
    same_block = (a >> 6) == (b >> 6)
    eye = (a == b).astype(F32).astype(BF)
    empty = jnp.zeros((128, 128), BF)
    for mat in range(2):
        base = mat * 640
        for quad in range(8):
            at = quad * 256
            top = band[at : at + 128, base : base + 640]
            low = band[at + 128 : at + 256, base : base + 640]
            wide = jnp.concatenate(
                [jnp.concatenate([top, empty], axis=1), jnp.concatenate([empty, low], axis=1)], axis=0
            )
            own = wide[:, :256]
            strict = jnp.where(same_block, 0.0, own.astype(F32)).astype(BF)
            own = (own.astype(F32) + dot_t(eye, strict)).astype(BF)
            full[mat, at : at + 256, at : at + 256] = own
            for step in (1, 2):
                to = ((quad + step) % 8) * 256
                part = wide[:, step * 256 : step * 256 + 256]
                full[mat, at : at + 256, to : to + 256] = part
                full[mat, to : to + 256, at : at + 256] = dot_t(eye, part).astype(BF)
            for step in (3, 4, 5):
                to = ((quad + step) % 8) * 256
                full[mat, at : at + 256, to : to + 256] = jnp.zeros((256, 256), BF)
    for mat in range(2):
        for i in range(2):
            rank = pl.multiple_of(table[2, 2 * gx + i] * 64, 64)
            rows_i[mat * 128 + i * 64 : mat * 128 + i * 64 + 64, :] = full[mat, pl.ds(rank, 64), :]
        for j in range(4):
            rank = pl.multiple_of(table[2, 4 * gy + j] * 64, 64)
            rows_j[mat, j * 64 : j * 64 + 64, :] = full[mat, pl.ds(rank, 64), :]
    for copy in copies:
        copy.wait()
    for n in range(8):
        first[:, n * 256 : n * 256 + 256] = dot(rows_i[...], k_all[:, n * 256 : n * 256 + 256]).astype(BF)
    for quad in range(8):
        at = quad * 256
        both = jnp.zeros((256, 256), F32)
        cross = jnp.zeros((128, 256), F32)
        for step in (-2, -1, 0, 1, 2):
            k = ((quad + step) % 8) * 256
            both = both + dot(first[:, k : k + 256], full[0, k : k + 256, at : at + 256])
            cross = cross + dot(first[:128, k : k + 256], full[1, k : k + 256, at : at + 256])
        second[:128, at : at + 256] = (both[128:] + cross).astype(BF)
        second[128:, at : at + 256] = both[:128].astype(BF)
    pair = dot_t(first[128:, :], rows_j[0]) + dot_t(first[:128, :], rows_j[1])
    for n in range(8):
        first[:, n * 256 : n * 256 + 256] = dot(second[...], k_all[:, n * 256 : n * 256 + 256]).astype(BF)
    cubic = dot_t(first[:128, :], rows_j[0]) + dot_t(first[128:, :], rows_j[1])
    grad = 3.0 * pair - 2.0 * cubic
    kernel = k_own[:, pl.ds(pl.multiple_of(gy * 256, 256), 256)].astype(F32)
    r, l = iota((128, 256), 0), iota((128, 256), 1)
    keep = jnp.zeros((128, 256), F32)
    for i in range(2):
        for j in range(4):
            here = ((r >> 6) == i) & ((l >> 6) == j)
            keep = keep + jnp.where(here, mask[i, 4 * gy + j].astype(F32), 0.0)
    out[...] = kernel - 0.5 * (keep * grad)


def chain(table, dev, mask, band, k_rows, k_own):
    vmem = pl.BlockSpec(memory_space=pltpu.VMEM)
    smem = pl.BlockSpec(memory_space=pltpu.SMEM)
    return pl.pallas_call(
        chain_kernel,
        out_shape=jax.ShapeDtypeStruct((128, 256), F32),
        in_specs=[smem, smem, smem, vmem, pl.BlockSpec(memory_space=pl.ANY), vmem],
        out_specs=vmem,
        scratch_shapes=[
            pltpu.VMEM((2, 2048, 2048), BF),
            pltpu.VMEM((2048, 2048), BF),
            pltpu.VMEM((256, 2048), BF),
            pltpu.VMEM((2, 256, 2048), BF),
            pltpu.VMEM((256, 2048), BF),
            pltpu.VMEM((256, 2048), BF),
            pltpu.SemaphoreType.DMA((NB,)),
        ],
        compiler_params=params(),
        name="chain",
    )(table, dev, mask, band, k_rows, k_own)


def extended(block):
    forward = [(i, (i + 1) % 8) for i in range(8)]
    backward = [(target, source) for source, target in forward]
    low = lax.ppermute(block[:, -1:], "gy", forward)
    high = lax.ppermute(block[:, :1], "gy", backward)
    return jnp.concatenate([low, block, high], axis=1)


def spread(values, mask):
    rows, cols = (values.shape[-2], values.shape[-1])
    grid = values.reshape(values.shape[:-2] + (rows // BLOCK, BLOCK, cols // BLOCK, BLOCK))
    return (grid * mask.astype(values.dtype)[:, None, :, None]).reshape(values.shape)


def matmul(left, right):
    return jnp.dot(left, right, preferred_element_type=F32)


def general(phi, potential, kernel, mask_s, mask_k):
    nrows = phi.shape[0]
    width = kernel.shape[1] // 8
    col_start = lax.axis_index("gy") * width
    padded = extended(phi).astype(F32)
    center = padded[:, 1:-1]
    lap = padded[:, 2:] + padded[:, :-2] - 6.0 * center
    for axis in (2, 3):
        lap = lap + jnp.roll(center, 1, axis) + jnp.roll(center, -1, axis)
    hphi = (-0.5 * lap + potential[None] * center).astype(BF)
    flat_phi = phi.reshape(nrows, -1)
    flat_h = hphi.reshape(nrows, -1)
    piece = lax.all_gather(phi, ROWS, axis=0, tiled=True)
    other = piece.reshape(piece.shape[0], -1)
    s_part = jnp.einsum("ap,bp->ab", flat_phi, other, preferred_element_type=F32)
    h_part = jnp.einsum("ap,bp->ab", flat_h, other, preferred_element_type=F32)
    partial_sums = jnp.stack([s_part, h_part])
    mask_cols = lax.dynamic_slice_in_dim(mask_s, col_start // BLOCK, width // BLOCK, 1)
    local = lax.psum_scatter(partial_sums, "gy", scatter_dimension=2, tiled=True)
    block_pair = spread(local, mask_cols).astype(BF)
    rows = lax.all_gather(block_pair, "gy", axis=2, tiled=True)
    k_mat = spread(kernel, mask_k)
    pieces = lax.all_gather(block_pair, ROWS, axis=1, tiled=True)
    x_acc = matmul(k_mat, pieces[0])
    y_acc = matmul(k_mat, pieces[1])
    pair = jnp.stack([x_acc.astype(BF), y_acc.astype(BF)])
    columns = lax.all_gather(pair, ROWS, axis=1, tiled=True)
    p_one = matmul(rows[1], columns[0])
    p_two = matmul(rows[0], columns[1])
    z_mat = matmul(rows[0], columns[0])
    trio = jnp.stack([p_one, z_mat, p_two]).astype(BF)
    trio_rows = lax.all_gather(trio, "gy", axis=2, tiled=True)
    q_mat = (
        matmul(trio_rows[0], columns[0])
        + matmul(trio_rows[1], columns[1])
        + matmul(trio_rows[2], columns[0])
    )
    grad = 3.0 * (trio[0].astype(F32) + trio[2].astype(F32)) - 2.0 * q_mat
    mask_kcols = lax.dynamic_slice_in_dim(mask_k, col_start // BLOCK, width // BLOCK, 1)
    kernel_cols = lax.dynamic_slice_in_dim(kernel, col_start, width, 1).astype(F32)
    return kernel_cols - 0.5 * spread(grad, mask_kcols)


def sparse(phi, potential, kernel, mask_s, mask_k):
    v, core, gy = lax.axis_index("v"), lax.axis_index("c"), lax.axis_index("gy")
    dev = jnp.stack([2 * v + core, core, gy]).astype(I32)
    swap = [(0, 1), (1, 0)]
    halo = lax.ppermute(phi[:, 0].reshape(128, 1024), "gy", [((i + 1) % 8, i) for i in range(8)])
    mask_rows = jnp.pad(mask_s.astype(F32), ((2, 4), (0, LANES - NB)))
    packed, meta = pack(dev, phi.reshape(128, 10240), halo, mask_rows)
    metas = jnp.max(lax.all_gather(meta, "gy"), axis=0)
    metas = lax.all_gather(metas[:4], ROWS)
    used = metas[:, :2].reshape(NB, LANES)
    near = metas[:, 2:].reshape(NB, LANES)
    own = lax.all_to_all(packed, "v", 0, 0, tiled=True)
    other = lax.ppermute(own, "c", swap)
    pot = lax.dynamic_index_in_dim(potential.reshape(10, 4, 8, 32), v, 2, keepdims=False)
    pot = jnp.pad(pot.reshape(10, LANES), ((0, 6), (0, 0)))
    table, weights = plan(dev, used, near)
    k_rows = lax.all_gather(sort_columns(table, mask_k, kernel), ROWS, axis=0, tiled=True)
    part = integrals(table, dev, own, other, pot)
    parts = lax.all_to_all(part.reshape(64, 8, 1280), PEERS, 0, 0, tiled=True)
    mine = combine(parts, weights)
    mine = lax.all_to_all(jnp.broadcast_to(mine[None], (64, 16, 1280)), PEERS, 0, 0, tiled=True)
    theirs = lax.ppermute(mine, "c", swap)
    even = jnp.where(core == 0, mine, theirs)
    odd = jnp.where(core == 0, theirs, mine)
    band = jnp.stack([even, odd]).reshape(2, 8, 8, 2, 8, 1280)
    band = band.transpose(3, 1, 0, 2, 4, 5).reshape(2048, 1280)
    result = chain(table, dev, mask_k, band, k_rows, kernel)
    return result, table[3, 0] == 1


def shards(*args):
    result, fits = sparse(*args)
    return lax.cond(fits, lambda *_: result, general, *args)


def solution(mesh):
    fine = Mesh(mesh.devices.reshape(8, 2, 8), ("v", "c", "gy"))
    in_specs = (
        P(ROWS, "gy", None, None),
        P("gy", None, None),
        P(ROWS, None),
        P(ROWS, None),
        P(ROWS, None),
    )
    out_specs = P(ROWS, "gy")
    return jax.shard_map(shards, mesh=fine, in_specs=in_specs, out_specs=out_specs, check_vma=False)
```

```python
import jax
import jax.numpy as jnp
from jax import lax
from jax.experimental import pallas as pl
from jax.experimental.pallas import tpu as pltpu
from jax.sharding import Mesh, PartitionSpec as P

BLOCK = 64
NB = 32
SLOTS = 16
REACH = 8
LANES = 128
ROWS = ("v", "c")
GY = ("x", "yh")
PEERS = ("v", "x", "yh")
BF = jnp.bfloat16
F32 = jnp.float32
I32 = jnp.int32
VMEM_LIMIT = 56 * 1024 * 1024


def iota(shape, dim):
    return lax.broadcasted_iota(I32, shape, dim)


def dot(left, right):
    return lax.dot_general(left, right, (((1,), (0,)), ((), ())), preferred_element_type=F32)


def dot_t(left, right):
    return lax.dot_general(left, right, (((1,), (1,)), ((), ())), preferred_element_type=F32)


def exact(left, right):
    return dot(left.astype(BF), right.astype(BF))


def exact_t(left, right):
    return dot_t(left.astype(BF), right.astype(BF))


def params(**more):
    return pltpu.CompilerParams(vmem_limit_bytes=VMEM_LIMIT, **more)


def spare_lanes():
    note, lane = iota((LANES, LANES), 0), iota((LANES, LANES), 1)
    group, at = lane >> 5, lane & 31
    index = group * 12 + jnp.where(at >= 16, at - 20, at - 10)
    spare = ((at & 15) >= 10) & (index < 42)
    wanted = jnp.where(index < 10, index, index + 22)
    return (spare & (note == wanted)).astype(F32)


def pack_kernel(flat, halo, mask_rows, packed):
    rows = flat.shape[0]
    src, dst = iota((512, 512), 0), iota((512, 512), 1)
    wanted = ((dst >> 5) & 3) * 128 + (dst >> 7) * 32 + (dst & 31)
    perm = (src == wanted).astype(F32).astype(BF)
    for x in range(11):
        for half in range(2):
            pieces = []
            for y in range(4):
                at = y * 256 + half * 128
                if x < 10:
                    pieces.append(flat[:, x * 1024 + at : x * 1024 + at + 128])
                else:
                    pieces.append(halo[:, at : at + 128])
            out = dot(jnp.concatenate(pieces, axis=1), perm).astype(BF)
            tile = x if x < 10 else 11
            for j in range(4):
                packed[4 * half + j, :, tile * 128 : tile * 128 + 128] = out[:, j * 128 : j * 128 + 128]
    src, dst = iota((1280, 256), 0), iota((1280, 256), 1)
    plane, lane = src >> 7, src & 127
    low = (dst < 128) & ((lane & 31) == 31) & ((dst & 127) == (lane & 96) + plane)
    high = (dst >= 128) & ((lane & 31) == 0) & ((dst & 127) == (lane & 96) + 16 + plane)
    edges = (low | high).astype(F32).astype(BF)
    lane, row = iota((8, LANES), 1), iota((8, LANES), 0)
    meta = mask_rows[...]
    for block in range(2):
        for x in range(10):
            part = jnp.abs(flat[block * 64 : block * 64 + 64, x * 1024 : x * 1024 + 1024].astype(F32))
            top = jnp.max(jnp.max(part, axis=0, keepdims=True), axis=1, keepdims=True)
            used = (top > 0.0).astype(F32)
            meta = meta + jnp.where((row == block) & (lane == x), used, 0.0)
    meta = dot(meta, spare_lanes())
    row = iota((128, LANES), 0)
    notes = jnp.where(row == 0, meta[0:1], 0.0) + jnp.where(row == 64, meta[1:2], 0.0)
    found = [dot(packed[v, :, :1280], edges) for v in range(8)]
    for v in range(8):
        tile = found[v][:, :128] + found[(v + 1) % 8][:, 128:]
        packed[v, :, 1280:1408] = (tile + notes).astype(BF)


def pack(flat, halo, mask_rows):
    vmem = pl.BlockSpec(memory_space=pltpu.VMEM)
    return pl.pallas_call(
        pack_kernel,
        out_shape=jax.ShapeDtypeStruct((8, 128, 1536), BF),
        in_specs=[vmem, vmem, vmem],
        out_specs=vmem,
        compiler_params=params(),
        name="pack",
    )(flat, halo, mask_rows)


def plan_kernel(dev, notes, table, weights):
    gx, core, gy = dev[0], dev[1], dev[2]
    square = (LANES, LANES)
    zeros = jnp.zeros((96, LANES), F32)
    found = dot_t(notes[...].reshape(256, LANES), spare_lanes().astype(BF))
    lane = iota((16, LANES), 1)
    planes, masks = [], []
    for c in range(2):
        total = jnp.zeros((16, LANES), F32)
        for domain in range(8):
            at = (c * 8 + domain) * 16
            part = jnp.where(lane < 10, found[at : at + 16], 0.0)
            total = total + (pltpu.roll(part, 10 * domain, 1) if domain else part)
        planes.append(total)
        part = pltpu.roll(found[c * 128 : c * 128 + 16], 96, 1)
        masks.append(jnp.where(lane < NB, part, 0.0))
    block, at = iota((NB, NB), 0), iota((NB, NB), 1)
    spot = (block == 4 * ((at & 15) >> 1) + 2 * (at >> 4) + (at & 1)).astype(F32)
    used = exact(spot, jnp.concatenate(planes, axis=0))
    near = exact(spot, jnp.concatenate(masks, axis=0))
    tall_used = jnp.concatenate([used, zeros], axis=0)
    tall_near = jnp.concatenate([near, zeros], axis=0)
    a, b = iota(square, 0), iota(square, 1)
    apart = jnp.abs(a - b)
    apart = jnp.minimum(apart, 80 - apart)
    far = ((a < 80) & (b < 80) & (apart > 13)).astype(F32)
    row, lane = iota((NB, LANES), 0), iota((NB, LANES), 1)
    outside = exact(used, far)
    fits = (outside < 0.5) & (lane < 80)
    centre = jnp.min(jnp.where(fits, lane.astype(F32), 127.0), axis=1, keepdims=True)
    key_col = centre * 32.0 + row[:, :1].astype(F32)
    key_row = jnp.sum(jnp.where(row == lane, key_col, 0.0), axis=0, keepdims=True)
    rank_col = jnp.sum(((lane < NB) & (key_row < key_col)).astype(F32), axis=1, keepdims=True)
    rank_row = jnp.sum((key_col < key_row).astype(F32), axis=0, keepdims=True)
    lane_f = lane.astype(F32)
    block_row = jnp.sum(jnp.where(rank_col == lane_f, row.astype(F32), 0.0), axis=0, keepdims=True)
    order = ((rank_row == a.astype(F32)) & (b < NB) & (a < NB)).astype(F32)
    order_rows = order[:NB]
    d8, l8 = iota((8, LANES), 0), iota((8, LANES), 1)
    ahead = l8 - 10 * d8
    ahead = jnp.where(ahead < 0, ahead + 80, ahead)
    touch = ((ahead <= 10) & (l8 < 80)).astype(F32)
    flags = (exact_t(touch, tall_used) > 0.5).astype(F32)
    flags = exact_t(flags, order)
    upper = jnp.where(l8 < SLOTS, pltpu.roll(flags, LANES - SLOTS, 1), 0.0)
    clash = jnp.max(upper * flags)
    sorted_near = exact_t(exact(order_rows, tall_near), order)
    gap = (lane - row) & 31
    stray = (sorted_near > 0.5) & (lane < NB) & (gap > REACH) & (gap < NB - REACH)
    good = (clash < 0.5) & (jnp.max(stray.astype(F32)) < 0.5)
    shift = b - core
    pick = ((a == ((gx + shift) & 15)) & (a < SLOTS)).astype(F32)
    col_half = exact(upper, pick)
    row_half = jnp.sum(jnp.where(l8 == gx, upper, 0.0), axis=1, keepdims=True)
    step = l8 - core
    allowed = ((step >= 0) & (step <= REACH)).astype(F32)
    j, lanes = iota((LANES, 640), 0), iota((LANES, 640), 1)
    widen = ((lanes >> 6) == j).astype(F32)
    for half in range(2):
        mine = gx + 16 * half
        line = jnp.sum(jnp.where(row == mine, sorted_near, 0.0), axis=0, keepdims=True)
        pick = ((a == ((mine + shift) & 31)) & (a < NB)).astype(F32)
        line = exact(jnp.broadcast_to(line, (8, LANES)), pick)
        other = (((mine + step) & 31) >> 4).astype(F32)
        same = (row_half == float(half)) & (col_half == other)
        small = jnp.where(same, line * allowed, 0.0)
        weights[8 * half : 8 * half + 8, :] = exact(small, widen)
    own = jnp.sum(jnp.where(d8 == gy, upper, 0.0), axis=0, keepdims=True)
    source = jnp.where(own > 0.5, pltpu.roll(block_row, LANES - SLOTS, 1), block_row)
    ok = jnp.where(good, 1.0, 0.0)
    out = jnp.where(d8 == 0, source, 0.0) + jnp.where(d8 == 1, block_row, 0.0)
    out = out + jnp.where(d8 == 2, rank_row, 0.0) + jnp.where(d8 == 3, ok, 0.0)
    table[...] = jnp.where(l8 < NB, out, 0.0).astype(I32)


def plan(dev, notes):
    vmem = pl.BlockSpec(memory_space=pltpu.VMEM)
    return pl.pallas_call(
        plan_kernel,
        out_shape=(
            jax.ShapeDtypeStruct((8, LANES), I32),
            jax.ShapeDtypeStruct((16, 640), F32),
        ),
        in_specs=[pl.BlockSpec(memory_space=pltpu.SMEM), vmem],
        out_specs=(vmem, vmem),
        compiler_params=params(),
        name="plan",
    )(dev, notes)


def trim_kernel(dev, mask, kernel, out):
    lane = iota((64, LANES), 1)
    quarter = dev[2] >> 1
    for rows in range(2):
        for tile in range(4):
            at = pl.multiple_of(quarter * 512 + tile * 128, 128)
            block = quarter * 8 + tile * 2
            part = kernel[rows * 64 : rows * 64 + 64, pl.ds(at, 128)].astype(F32)
            keep = jnp.where(lane < 64, mask[rows, block], mask[rows, block + 1]).astype(F32)
            out[rows * 64 : rows * 64 + 64, tile * 128 : tile * 128 + 128] = (part * keep).astype(BF)


def trim(dev, mask, kernel):
    vmem = pl.BlockSpec(memory_space=pltpu.VMEM)
    smem = pl.BlockSpec(memory_space=pltpu.SMEM)
    return pl.pallas_call(
        trim_kernel,
        out_shape=jax.ShapeDtypeStruct((128, 512), BF),
        in_specs=[smem, smem, vmem],
        out_specs=vmem,
        compiler_params=params(),
        name="trim",
    )(dev, mask, kernel)


def integrals_kernel(table, dev, own, other, pot, out, right, left_s, left_h, sems):
    core = dev[1]
    for slot in range(SLOTS):
        block = table[0, slot]
        at = (block >> 2) * 2 + (block & 1)
        mine = ((block >> 1) & 1) == core
        to = right.at[slot * 64 : slot * 64 + 64, :]

        @pl.when(mine)
        def _():
            pltpu.make_async_copy(own.at[at], to, sems.at[slot]).start()

        @pl.when(jnp.logical_not(mine))
        def _():
            pltpu.make_async_copy(other.at[at], to, sems.at[slot]).start()

    lane = iota((64, LANES), 1)
    low, high = (lane & 31) == 0, (lane & 31) == 31
    for pair in range(8):
        for side in range(2):
            slot = 2 * pair + side
            rows = right.at[slot * 64 : slot * 64 + 64, :]
            pltpu.make_async_copy(own.at[0], rows, sems.at[slot]).wait()
        to = pair * 64
        source = pl.multiple_of((2 * pair + core) * 64, 64)
        data = right[pl.ds(source, 64), :]
        left_s[to : to + 64, :] = data[:, :1280]
        before = jnp.zeros((64, LANES), F32)
        here = data[:, :128].astype(F32)
        for x in range(10):
            after = data[:, x * 128 + 128 : x * 128 + 256].astype(F32) if x < 9 else jnp.zeros((64, LANES), F32)
            near = before + after
            near = near + pltpu.roll(here, 32, 1) + pltpu.roll(here, 96, 1)
            near = near + jnp.where(low, 0.0, pltpu.roll(here, 1, 1))
            near = near + jnp.where(high, 0.0, pltpu.roll(here, 127, 1))
            value = (3.0 + pot[x : x + 1, :]) * here - 0.5 * near
            left_h[to : to + 64, x * 128 : x * 128 + 128] = value.astype(BF)
            before, here = here, after
        edge = jnp.where((lane & 15) < 10, data[:, 1280:1408].astype(F32), 0.0)
        left_h[to : to + 64, 1280:1408] = (-0.5 * edge).astype(BF)
        left_h[to : to + 64, 1408:1536] = (-0.5 * data[:, 1152:1280].astype(F32)).astype(BF)
        left_h[to : to + 64, 1536:1664] = (-0.5 * data[:, 1408:1536].astype(F32)).astype(BF)
        for side in range(2):
            at = (2 * pair + side) * 64
            edge = right[at : at + 64, 1280:1408].astype(F32)
            edge = jnp.where((lane & 31) < 16, pltpu.roll(edge, 112, 1), pltpu.roll(edge, 16, 1))
            edge = jnp.where((lane & 15) < 10, edge, 0.0)
            right[at : at + 64, 1280:1408] = edge.astype(BF)
    for chunk in range(4):
        cols = right[chunk * 256 : chunk * 256 + 256, :]
        found = (
            dot_t(left_s[...], cols[:, :1280]),
            dot_t(left_h[:, :1536], cols) + dot_t(left_h[:, 1536:], cols[:, 1152:1280]),
        )
        for mat in range(2):
            value = found[mat].astype(BF)
            for rows in range(8):
                for side in range(2):
                    step = (2 * chunk + side - rows) % 8
                    if step < 5:
                        for part in range(4):
                            at = rows * 64 + part * 16
                            out[rows * 8 + mat * 4 + part, :, step * 128 : step * 128 + 128] = value[
                                at : at + 16, side * 128 : side * 128 + 128
                            ]


def integrals(table, dev, own, other, pot):
    vmem = pl.BlockSpec(memory_space=pltpu.VMEM)
    smem = pl.BlockSpec(memory_space=pltpu.SMEM)
    anywhere = pl.BlockSpec(memory_space=pl.ANY)
    return pl.pallas_call(
        integrals_kernel,
        out_shape=jax.ShapeDtypeStruct((64, 16, 640), BF),
        in_specs=[smem, smem, anywhere, anywhere, vmem],
        out_specs=vmem,
        scratch_shapes=[
            pltpu.VMEM((1024, 1536), BF),
            pltpu.VMEM((512, 1280), BF),
            pltpu.VMEM((512, 1664), BF),
            pltpu.SemaphoreType.DMA((SLOTS,)),
        ],
        compiler_params=params(),
        name="integrals",
    )(table, dev, own.reshape(16, 64, 1536), other.reshape(16, 64, 1536), pot)


def combine_kernel(parts, weights, out):
    lines = [jnp.zeros((16, 640), F32), jnp.zeros((16, 640), F32)]
    for domain in range(8):
        total = parts[domain].astype(F32)
        for v in range(1, 8):
            total = total + parts[v * 8 + domain].astype(F32)
        for half in range(2):
            lines[half] = lines[half] + total * weights[8 * half + domain : 8 * half + domain + 1, :]
    out[...] = jnp.concatenate(lines, axis=0).astype(BF)


def combine(parts, weights):
    vmem = pl.BlockSpec(memory_space=pltpu.VMEM)
    return pl.pallas_call(
        combine_kernel,
        out_shape=jax.ShapeDtypeStruct((32, 640), BF),
        in_specs=[vmem, vmem],
        out_specs=vmem,
        compiler_params=params(),
        name="combine",
    )(parts, weights)


def regroup(table, source, target):
    lane = iota((256, LANES), 1)
    for tile in range(16):
        halves = []
        for half in range(2):
            block = table[1, 2 * tile + half]
            part = source[:, pl.ds(pl.multiple_of((block >> 1) * 128, 128), 128)].astype(F32)
            halves.append(jnp.where((block & 1) == half, part, pltpu.roll(part, 64, 1)))
        both = jnp.where(lane < 64, halves[0], halves[1])
        target[:, tile * 128 : tile * 128 + 128] = both.astype(BF)


def chain_kernel(
    table, dev, mask, mine, theirs, k_mine, k_theirs, k_own, out, band, full, k_all, rows_i, rows_j, raw, first, second, sems
):
    gx, core, gy = dev[0], dev[1], dev[2]
    copies = []
    for rank in range(NB):
        source = pl.multiple_of(table[1, rank] * 64, 64)
        for held, half in ((k_mine, core), (k_theirs, 1 - core)):
            copy = pltpu.make_async_copy(
                held.at[:, pl.ds(source, 64), :],
                k_all.at[half, :, rank * 64 : rank * 64 + 64, :],
                sems.at[len(copies)],
            )
            copy.start()
            copies.append(copy)
    a, b = iota((256, 256), 0), iota((256, 256), 1)
    same_block = (a >> 6) == (b >> 6)
    eye = (a == b).astype(F32).astype(BF)
    empty = jnp.zeros((128, 128), BF)
    for held, parity in ((mine, core), (theirs, 1 - core)):
        for v in range(8):
            for half in range(2):
                at = (16 * half + 2 * v + parity) * 64
                for part in range(8):
                    to = pl.multiple_of(at + 16 * (part % 4), 16)
                    band[part // 4, pl.ds(to, 16), :] = held[v * 8 + part, 16 * half : 16 * half + 16, :]
    for mat in range(2):
        for quad in range(8):
            at = quad * 256
            top = band[mat, at : at + 128, :]
            low = band[mat, at + 128 : at + 256, :]
            wide = jnp.concatenate(
                [jnp.concatenate([top, empty], axis=1), jnp.concatenate([empty, low], axis=1)], axis=0
            )
            own = wide[:, :256]
            strict = jnp.where(same_block, 0.0, own.astype(F32)).astype(BF)
            own = (own.astype(F32) + dot_t(eye, strict)).astype(BF)
            full[mat, at : at + 256, at : at + 256] = own
            for step in (1, 2):
                to = ((quad + step) % 8) * 256
                part = wide[:, step * 256 : step * 256 + 256]
                full[mat, at : at + 256, to : to + 256] = part
                full[mat, to : to + 256, at : at + 256] = dot_t(eye, part).astype(BF)
            for step in (3, 4, 5):
                to = ((quad + step) % 8) * 256
                full[mat, at : at + 256, to : to + 256] = jnp.zeros((256, 256), BF)
    for mat in range(2):
        for i in range(2):
            rank = pl.multiple_of(table[2, 2 * gx + i] * 64, 64)
            rows_i[mat * 128 + i * 64 : mat * 128 + i * 64 + 64, :] = full[mat, pl.ds(rank, 64), :]
        for j in range(4):
            rank = pl.multiple_of(table[2, 4 * gy + j] * 64, 64)
            rows_j[mat, j * 64 : j * 64 + 64, :] = full[mat, pl.ds(rank, 64), :]
    for copy in copies:
        copy.wait()
    for n in range(8):
        raw[:, n * 256 : n * 256 + 256] = dot(rows_i[...], k_all[n % 2, n // 2]).astype(BF)
    regroup(table, raw, first)
    for quad in range(8):
        at = quad * 256
        both = jnp.zeros((256, 256), F32)
        cross = jnp.zeros((128, 256), F32)
        for step in (-2, -1, 0, 1, 2):
            k = ((quad + step) % 8) * 256
            both = both + dot(first[:, k : k + 256], full[0, k : k + 256, at : at + 256])
            cross = cross + dot(first[:128, k : k + 256], full[1, k : k + 256, at : at + 256])
        second[:128, at : at + 256] = (both[128:] + cross).astype(BF)
        second[128:, at : at + 256] = both[:128].astype(BF)
    pair = dot_t(first[128:, :], rows_j[0]) + dot_t(first[:128, :], rows_j[1])
    for n in range(8):
        raw[:, n * 256 : n * 256 + 256] = dot(second[...], k_all[n % 2, n // 2]).astype(BF)
    regroup(table, raw, first)
    cubic = dot_t(first[:128, :], rows_j[0]) + dot_t(first[128:, :], rows_j[1])
    grad = 3.0 * pair - 2.0 * cubic
    kernel = k_own[:, pl.ds(pl.multiple_of(gy * 256, 256), 256)].astype(F32)
    r, l = iota((128, 256), 0), iota((128, 256), 1)
    keep = jnp.zeros((128, 256), F32)
    for i in range(2):
        for j in range(4):
            here = ((r >> 6) == i) & ((l >> 6) == j)
            keep = keep + jnp.where(here, mask[i, 4 * gy + j].astype(F32), 0.0)
    out[...] = kernel - 0.5 * (keep * grad)


def chain(table, dev, mask, mine, theirs, k_mine, k_theirs, k_own):
    vmem = pl.BlockSpec(memory_space=pltpu.VMEM)
    smem = pl.BlockSpec(memory_space=pltpu.SMEM)
    anywhere = pl.BlockSpec(memory_space=pl.ANY)
    return pl.pallas_call(
        chain_kernel,
        out_shape=jax.ShapeDtypeStruct((128, 256), F32),
        in_specs=[smem, smem, smem, vmem, vmem, anywhere, anywhere, vmem],
        out_specs=vmem,
        scratch_shapes=[
            pltpu.VMEM((2, 2048, 640), BF),
            pltpu.VMEM((2, 2048, 2048), BF),
            pltpu.VMEM((2, 4, 2048, 256), BF),
            pltpu.VMEM((256, 2048), BF),
            pltpu.VMEM((2, 256, 2048), BF),
            pltpu.VMEM((256, 2048), BF),
            pltpu.VMEM((256, 2048), BF),
            pltpu.VMEM((256, 2048), BF),
            pltpu.SemaphoreType.DMA((2 * NB,)),
        ],
        compiler_params=params(),
        name="chain",
    )(table, dev, mask, mine, theirs, k_mine, k_theirs, k_own)


def extended(block):
    forward = [(i, (i + 1) % 8) for i in range(8)]
    backward = [(target, source) for source, target in forward]
    low = lax.ppermute(block[:, -1:], GY, forward)
    high = lax.ppermute(block[:, :1], GY, backward)
    return jnp.concatenate([low, block, high], axis=1)


def spread(values, mask):
    rows, cols = (values.shape[-2], values.shape[-1])
    grid = values.reshape(values.shape[:-2] + (rows // BLOCK, BLOCK, cols // BLOCK, BLOCK))
    return (grid * mask.astype(values.dtype)[:, None, :, None]).reshape(values.shape)


def matmul(left, right):
    return jnp.dot(left, right, preferred_element_type=F32)


def general(phi, potential, kernel, mask_s, mask_k):
    nrows = phi.shape[0]
    width = kernel.shape[1] // 8
    col_start = lax.axis_index(GY) * width
    padded = extended(phi).astype(F32)
    center = padded[:, 1:-1]
    lap = padded[:, 2:] + padded[:, :-2] - 6.0 * center
    for axis in (2, 3):
        lap = lap + jnp.roll(center, 1, axis) + jnp.roll(center, -1, axis)
    hphi = (-0.5 * lap + potential[None] * center).astype(BF)
    flat_phi = phi.reshape(nrows, -1)
    flat_h = hphi.reshape(nrows, -1)
    piece = lax.all_gather(phi, ROWS, axis=0, tiled=True)
    other = piece.reshape(piece.shape[0], -1)
    s_part = jnp.einsum("ap,bp->ab", flat_phi, other, preferred_element_type=F32)
    h_part = jnp.einsum("ap,bp->ab", flat_h, other, preferred_element_type=F32)
    partial_sums = jnp.stack([s_part, h_part])
    mask_cols = lax.dynamic_slice_in_dim(mask_s, col_start // BLOCK, width // BLOCK, 1)
    local = lax.psum_scatter(partial_sums, GY, scatter_dimension=2, tiled=True)
    block_pair = spread(local, mask_cols).astype(BF)
    rows = lax.all_gather(block_pair, GY, axis=2, tiled=True)
    k_mat = spread(kernel, mask_k)
    pieces = lax.all_gather(block_pair, ROWS, axis=1, tiled=True)
    x_acc = matmul(k_mat, pieces[0])
    y_acc = matmul(k_mat, pieces[1])
    pair = jnp.stack([x_acc.astype(BF), y_acc.astype(BF)])
    columns = lax.all_gather(pair, ROWS, axis=1, tiled=True)
    p_one = matmul(rows[1], columns[0])
    p_two = matmul(rows[0], columns[1])
    z_mat = matmul(rows[0], columns[0])
    trio = jnp.stack([p_one, z_mat, p_two]).astype(BF)
    trio_rows = lax.all_gather(trio, GY, axis=2, tiled=True)
    q_mat = (
        matmul(trio_rows[0], columns[0])
        + matmul(trio_rows[1], columns[1])
        + matmul(trio_rows[2], columns[0])
    )
    grad = 3.0 * (trio[0].astype(F32) + trio[2].astype(F32)) - 2.0 * q_mat
    mask_kcols = lax.dynamic_slice_in_dim(mask_k, col_start // BLOCK, width // BLOCK, 1)
    kernel_cols = lax.dynamic_slice_in_dim(kernel, col_start, width, 1).astype(F32)
    return kernel_cols - 0.5 * spread(grad, mask_kcols)


def sparse(phi, potential, kernel, mask_s, mask_k):
    v, core, gy = lax.axis_index("v"), lax.axis_index("c"), lax.axis_index(GY)
    dev = jnp.stack([2 * v + core, core, gy]).astype(I32)
    swap = [(0, 1), (1, 0)]
    halo = lax.ppermute(phi[:, 0].reshape(128, 1024), GY, [((i + 1) % 8, i) for i in range(8)])
    quarter = lax.all_gather(trim(dev, mask_k, kernel), ROWS, axis=0, tiled=True)
    mask_rows = jnp.pad(mask_s.astype(F32), ((0, 6), (NB, LANES - 2 * NB)))
    packed = pack(phi.reshape(128, 10240), halo, mask_rows)
    own = lax.all_to_all(packed, "v", 0, 0, tiled=True)
    own, quarter = lax.optimization_barrier((own, quarter))
    other = lax.ppermute(own, "c", swap)
    eighth = lax.dynamic_slice_in_dim(quarter, 256 * core, 256, 1)
    k_mine = lax.all_gather(eighth, "x")
    notes = own.reshape(16, 64, 1536)[:, 0, 1280:1408]
    notes = lax.all_to_all(jnp.broadcast_to(notes[None], (16, 16, LANES)), ("c", "x", "yh"), 0, 0, tiled=True)
    pot = lax.dynamic_index_in_dim(potential.reshape(10, 4, 8, 32), v, 2, keepdims=False)
    pot = jnp.pad(pot.reshape(10, LANES), ((0, 6), (0, 0)))
    table, weights = plan(dev, notes)
    part = integrals(table, dev, own, other, pot)
    parts = lax.all_to_all(part, PEERS, 0, 0, tiled=True)
    parts, k_mine = lax.optimization_barrier((parts, k_mine))
    k_theirs = lax.ppermute(k_mine, "c", swap)
    mine = combine(parts, weights)
    mine = lax.all_to_all(jnp.broadcast_to(mine[None], (64, 32, 640)), PEERS, 0, 0, tiled=True)
    theirs = lax.ppermute(mine, "c", swap)
    result = chain(table, dev, mask_k, mine, theirs, k_mine, k_theirs, kernel)
    return result, table[3, 0] == 1


def shards(*args):
    result, fits = sparse(*args)
    return lax.cond(fits, lambda *_: result, general, *args)


def solution(mesh):
    fine = Mesh(mesh.devices.reshape(8, 2, 4, 2), ("v", "c", "x", "yh"))
    in_specs = (
        P(ROWS, GY, None, None),
        P(GY, None, None),
        P(ROWS, None),
        P(ROWS, None),
        P(ROWS, None),
    )
    out_specs = P(ROWS, GY)
    return jax.shard_map(shards, mesh=fine, in_specs=in_specs, out_specs=out_specs, check_vma=False)
```

```python
import jax
import jax.numpy as jnp
from jax import lax
from jax.experimental import pallas as pl
from jax.experimental.pallas import tpu as pltpu
from jax.sharding import Mesh, PartitionSpec as P

BLOCK = 64
NB = 32
SLOTS = 16
REACH = 8
LANES = 128
ROWS = ("v", "c")
GY = ("x", "yh")
PEERS = ("v", "x", "yh")
BF = jnp.bfloat16
F32 = jnp.float32
I32 = jnp.int32
VMEM_LIMIT = 56 * 1024 * 1024


def iota(shape, dim):
    return lax.broadcasted_iota(I32, shape, dim)


def dot(left, right):
    return lax.dot_general(left, right, (((1,), (0,)), ((), ())), preferred_element_type=F32)


def dot_t(left, right):
    return lax.dot_general(left, right, (((1,), (1,)), ((), ())), preferred_element_type=F32)


def exact(left, right):
    return dot(left.astype(BF), right.astype(BF))


def exact_t(left, right):
    return dot_t(left.astype(BF), right.astype(BF))


def place():
    core = lax.axis_index("c")
    return 2 * lax.axis_index("v") + core, core, 2 * lax.axis_index("x") + lax.axis_index("yh")


def params(**more):
    return pltpu.CompilerParams(vmem_limit_bytes=VMEM_LIMIT, **more)


def spare_lanes():
    note, lane = iota((LANES, LANES), 0), iota((LANES, LANES), 1)
    group, at = lane >> 5, lane & 31
    index = group * 12 + jnp.where(at >= 16, at - 20, at - 10)
    spare = ((at & 15) >= 10) & (index < 42)
    wanted = jnp.where(index < 10, index, index + 22)
    return (spare & (note == wanted)).astype(F32)


def pack_kernel(flat, halo, mask, packed):
    rows = flat.shape[0]
    src, dst = iota((512, 512), 0), iota((512, 512), 1)
    wanted = ((dst >> 5) & 3) * 128 + (dst >> 7) * 32 + (dst & 31)
    perm = (src == wanted).astype(F32).astype(BF)
    for x in range(11):
        for half in range(2):
            pieces = []
            for y in range(4):
                at = y * 256 + half * 128
                if x < 10:
                    pieces.append(flat[:, x * 1024 + at : x * 1024 + at + 128])
                else:
                    pieces.append(halo[:, at : at + 128])
            out = dot(jnp.concatenate(pieces, axis=1), perm).astype(BF)
            tile = x if x < 10 else 11
            for j in range(4):
                packed[4 * half + j, :, tile * 128 : tile * 128 + 128] = out[:, j * 128 : j * 128 + 128]
    src, dst = iota((1280, 256), 0), iota((1280, 256), 1)
    plane, lane = src >> 7, src & 127
    low = (dst < 128) & ((lane & 31) == 31) & ((dst & 127) == (lane & 96) + plane)
    high = (dst >= 128) & ((lane & 31) == 0) & ((dst & 127) == (lane & 96) + 16 + plane)
    edges = (low | high).astype(F32).astype(BF)
    lane, row = iota((2, LANES), 1), iota((2, LANES), 0)
    meta = jnp.zeros((2, LANES), F32)
    for block in range(2):
        for x in range(10):
            part = jnp.abs(flat[block * 64 : block * 64 + 64, x * 1024 : x * 1024 + 1024].astype(F32))
            top = jnp.max(jnp.max(part, axis=0, keepdims=True), axis=1, keepdims=True)
            used = (top > 0.0).astype(F32)
            meta = meta + jnp.where((row == block) & (lane == x), used, 0.0)
    spare = spare_lanes()
    meta = exact(meta, spare) + exact(mask[...].astype(F32), spare[NB : 2 * NB])
    row = iota((128, LANES), 0)
    notes = jnp.where(row == 0, meta[0:1], 0.0) + jnp.where(row == 64, meta[1:2], 0.0)
    found = [dot(packed[v, :, :1280], edges) for v in range(8)]
    for v in range(8):
        tile = found[v][:, :128] + found[(v + 1) % 8][:, 128:]
        packed[v, :, 1280:1408] = (tile + notes).astype(BF)


def pack(flat, halo, mask):
    vmem = pl.BlockSpec(memory_space=pltpu.VMEM)
    return pl.pallas_call(
        pack_kernel,
        out_shape=jax.ShapeDtypeStruct((8, 128, 1536), BF),
        in_specs=[vmem, vmem, vmem],
        out_specs=vmem,
        compiler_params=params(),
        name="pack",
    )(flat, halo, mask)


def plan_kernel(notes, table, weights):
    gx, core, gy = place()
    square = (LANES, LANES)
    zeros = jnp.zeros((96, LANES), F32)
    found = dot_t(notes[...].reshape(256, LANES), spare_lanes().astype(BF))
    lane = iota((16, LANES), 1)
    planes, masks = [], []
    for c in range(2):
        total = jnp.zeros((16, LANES), F32)
        for domain in range(8):
            at = (c * 8 + domain) * 16
            part = jnp.where(lane < 10, found[at : at + 16], 0.0)
            total = total + (pltpu.roll(part, 10 * domain, 1) if domain else part)
        planes.append(total)
        part = pltpu.roll(found[c * 128 : c * 128 + 16], 96, 1)
        masks.append(jnp.where(lane < NB, part, 0.0))
    block, at = iota((NB, NB), 0), iota((NB, NB), 1)
    spot = (block == 4 * ((at & 15) >> 1) + 2 * (at >> 4) + (at & 1)).astype(F32)
    used = exact(spot, jnp.concatenate(planes, axis=0))
    near = exact(spot, jnp.concatenate(masks, axis=0))
    tall_used = jnp.concatenate([used, zeros], axis=0)
    tall_near = jnp.concatenate([near, zeros], axis=0)
    a, b = iota(square, 0), iota(square, 1)
    apart = jnp.abs(a - b)
    apart = jnp.minimum(apart, 80 - apart)
    far = ((a < 80) & (b < 80) & (apart > 13)).astype(F32)
    row, lane = iota((NB, LANES), 0), iota((NB, LANES), 1)
    outside = exact(used, far)
    fits = (outside < 0.5) & (lane < 80)
    centre = jnp.min(jnp.where(fits, lane.astype(F32), 127.0), axis=1, keepdims=True)
    key_col = centre * 32.0 + row[:, :1].astype(F32)
    key_row = jnp.sum(jnp.where(row == lane, key_col, 0.0), axis=0, keepdims=True)
    rank_col = jnp.sum(((lane < NB) & (key_row < key_col)).astype(F32), axis=1, keepdims=True)
    rank_row = jnp.sum((key_col < key_row).astype(F32), axis=0, keepdims=True)
    lane_f = lane.astype(F32)
    block_row = jnp.sum(jnp.where(rank_col == lane_f, row.astype(F32), 0.0), axis=0, keepdims=True)
    order = ((rank_row == a.astype(F32)) & (b < NB) & (a < NB)).astype(F32)
    order_rows = order[:NB]
    d8, l8 = iota((8, LANES), 0), iota((8, LANES), 1)
    ahead = l8 - 10 * d8
    ahead = jnp.where(ahead < 0, ahead + 80, ahead)
    touch = ((ahead <= 10) & (l8 < 80)).astype(F32)
    flags = (exact_t(touch, tall_used) > 0.5).astype(F32)
    flags = exact_t(flags, order)
    upper = jnp.where(l8 < SLOTS, pltpu.roll(flags, LANES - SLOTS, 1), 0.0)
    clash = jnp.max(upper * flags)
    sorted_near = exact_t(exact(order_rows, tall_near), order)
    gap = (lane - row) & 31
    stray = (sorted_near > 0.5) & (lane < NB) & (gap > REACH) & (gap < NB - REACH)
    good = (clash < 0.5) & (jnp.max(stray.astype(F32)) < 0.5)
    shift = b - core
    pick = ((a == ((gx + shift) & 15)) & (a < SLOTS)).astype(F32)
    col_half = exact(upper, pick)
    row_half = jnp.sum(jnp.where(l8 == gx, upper, 0.0), axis=1, keepdims=True)
    step = l8 - core
    allowed = ((step >= 0) & (step <= REACH)).astype(F32)
    j, lanes = iota((LANES, 640), 0), iota((LANES, 640), 1)
    widen = ((lanes >> 6) == j).astype(F32)
    for half in range(2):
        mine = gx + 16 * half
        line = jnp.sum(jnp.where(row == mine, sorted_near, 0.0), axis=0, keepdims=True)
        pick = ((a == ((mine + shift) & 31)) & (a < NB)).astype(F32)
        line = exact(jnp.broadcast_to(line, (8, LANES)), pick)
        other = (((mine + step) & 31) >> 4).astype(F32)
        same = (row_half == float(half)) & (col_half == other)
        small = jnp.where(same, line * allowed, 0.0)
        weights[8 * half : 8 * half + 8, :] = exact(small, widen)
    own = jnp.sum(jnp.where(d8 == gy, upper, 0.0), axis=0, keepdims=True)
    source = jnp.where(own > 0.5, pltpu.roll(block_row, LANES - SLOTS, 1), block_row)
    ok = jnp.where(good, 1.0, 0.0)
    out = jnp.where(d8 == 0, source, 0.0) + jnp.where(d8 == 1, block_row, 0.0)
    out = out + jnp.where(d8 == 2, rank_row, 0.0) + jnp.where(d8 == 3, ok, 0.0)
    table[...] = jnp.where(l8 < NB, out, 0.0).astype(I32)


def plan(notes):
    vmem = pl.BlockSpec(memory_space=pltpu.VMEM)
    return pl.pallas_call(
        plan_kernel,
        out_shape=(
            jax.ShapeDtypeStruct((8, LANES), I32),
            jax.ShapeDtypeStruct((16, 640), F32),
        ),
        in_specs=[vmem],
        out_specs=(vmem, vmem),
        compiler_params=params(),
        name="plan",
    )(notes)


def trim_kernel(mask, kernel, *halves):
    lane = iota((64, LANES), 1)
    for rows in range(2):
        for tile in range(16):
            part = kernel[rows * 64 : rows * 64 + 64, tile * 128 : tile * 128 + 128].astype(F32)
            keep = jnp.where(lane < 64, mask[rows, 2 * tile], mask[rows, 2 * tile + 1]).astype(F32)
            at = tile % 8 * 128
            halves[tile // 8][rows * 64 : rows * 64 + 64, at : at + 128] = (part * keep).astype(BF)


def trim(mask, kernel):
    vmem = pl.BlockSpec(memory_space=pltpu.VMEM)
    smem = pl.BlockSpec(memory_space=pltpu.SMEM)
    half = jax.ShapeDtypeStruct((128, 1024), BF)
    return pl.pallas_call(
        trim_kernel,
        out_shape=(half, half),
        in_specs=[smem, vmem],
        out_specs=(vmem, vmem),
        compiler_params=params(),
        name="trim",
    )(mask, kernel)


def integrals_kernel(table, own, other, pot, out, right, left_s, left_h, sems):
    _, core, _ = place()
    for slot in range(SLOTS):
        block = table[0, slot]
        at = (block >> 2) * 2 + (block & 1)
        mine = ((block >> 1) & 1) == core
        to = right.at[slot * 64 : slot * 64 + 64, :]

        @pl.when(mine)
        def _():
            pltpu.make_async_copy(own.at[at], to, sems.at[slot]).start()

        @pl.when(jnp.logical_not(mine))
        def _():
            pltpu.make_async_copy(other.at[at], to, sems.at[slot]).start()

    lane = iota((64, LANES), 1)
    low, high = (lane & 31) == 0, (lane & 31) == 31
    for pair in range(8):
        for side in range(2):
            slot = 2 * pair + side
            rows = right.at[slot * 64 : slot * 64 + 64, :]
            pltpu.make_async_copy(own.at[0], rows, sems.at[slot]).wait()
        to = pair * 64
        source = pl.multiple_of((2 * pair + core) * 64, 64)
        data = right[pl.ds(source, 64), :]
        left_s[to : to + 64, :] = data[:, :1280]
        before = jnp.zeros((64, LANES), F32)
        here = data[:, :128].astype(F32)
        for x in range(10):
            after = data[:, x * 128 + 128 : x * 128 + 256].astype(F32) if x < 9 else jnp.zeros((64, LANES), F32)
            near = before + after
            near = near + pltpu.roll(here, 32, 1) + pltpu.roll(here, 96, 1)
            near = near + jnp.where(low, 0.0, pltpu.roll(here, 1, 1))
            near = near + jnp.where(high, 0.0, pltpu.roll(here, 127, 1))
            value = (3.0 + pot[x : x + 1, :]) * here - 0.5 * near
            left_h[to : to + 64, x * 128 : x * 128 + 128] = value.astype(BF)
            before, here = here, after
        edge = jnp.where((lane & 15) < 10, data[:, 1280:1408].astype(F32), 0.0)
        left_h[to : to + 64, 1280:1408] = (-0.5 * edge).astype(BF)
        left_h[to : to + 64, 1408:1536] = (-0.5 * data[:, 1152:1280].astype(F32)).astype(BF)
        left_h[to : to + 64, 1536:1664] = (-0.5 * data[:, 1408:1536].astype(F32)).astype(BF)
        for side in range(2):
            at = (2 * pair + side) * 64
            edge = right[at : at + 64, 1280:1408].astype(F32)
            edge = jnp.where((lane & 31) < 16, pltpu.roll(edge, 112, 1), pltpu.roll(edge, 16, 1))
            edge = jnp.where((lane & 15) < 10, edge, 0.0)
            right[at : at + 64, 1280:1408] = edge.astype(BF)
    for chunk in range(4):
        cols = right[chunk * 256 : chunk * 256 + 256, :]
        found = (
            dot_t(left_s[...], cols[:, :1280]),
            dot_t(left_h[:, :1536], cols) + dot_t(left_h[:, 1536:], cols[:, 1152:1280]),
        )
        for mat in range(2):
            value = found[mat].astype(BF)
            for rows in range(8):
                for side in range(2):
                    step = (2 * chunk + side - rows) % 8
                    if step < 5:
                        for part in range(4):
                            at = rows * 64 + part * 16
                            out[rows * 8 + mat * 4 + part, :, step * 128 : step * 128 + 128] = value[
                                at : at + 16, side * 128 : side * 128 + 128
                            ]


def integrals(table, own, other, pot):
    vmem = pl.BlockSpec(memory_space=pltpu.VMEM)
    smem = pl.BlockSpec(memory_space=pltpu.SMEM)
    anywhere = pl.BlockSpec(memory_space=pl.ANY)
    return pl.pallas_call(
        integrals_kernel,
        out_shape=jax.ShapeDtypeStruct((64, 16, 640), BF),
        in_specs=[smem, anywhere, anywhere, vmem],
        out_specs=vmem,
        scratch_shapes=[
            pltpu.VMEM((1024, 1536), BF),
            pltpu.VMEM((512, 1280), BF),
            pltpu.VMEM((512, 1664), BF),
            pltpu.SemaphoreType.DMA((SLOTS,)),
        ],
        compiler_params=params(),
        name="integrals",
    )(table, own.reshape(16, 64, 1536), other.reshape(16, 64, 1536), pot)


def combine_kernel(parts, weights, out, lines_all, sems):
    lines = [jnp.zeros((16, 640), F32), jnp.zeros((16, 640), F32)]
    for domain in range(8):
        total = parts[domain].astype(F32)
        for v in range(1, 8):
            total = total + parts[v * 8 + domain].astype(F32)
        for half in range(2):
            lines[half] = lines[half] + total * weights[8 * half + domain : 8 * half + domain + 1, :]
    lines_all[...] = jnp.concatenate(lines, axis=0).astype(BF)
    copies = [pltpu.make_async_copy(lines_all, out.at[peer], sems.at[peer]) for peer in range(64)]
    for copy in copies:
        copy.start()
    for copy in copies:
        copy.wait()


def combine(parts, weights):
    vmem = pl.BlockSpec(memory_space=pltpu.VMEM)
    return pl.pallas_call(
        combine_kernel,
        out_shape=jax.ShapeDtypeStruct((64, 32, 640), BF),
        in_specs=[vmem, vmem],
        out_specs=pl.BlockSpec(memory_space=pl.ANY),
        scratch_shapes=[pltpu.VMEM((32, 640), BF), pltpu.SemaphoreType.DMA((64,))],
        compiler_params=params(),
        name="combine",
    )(parts, weights)


def regroup(table, source, target):
    lane = iota((256, LANES), 1)
    for tile in range(16):
        halves = []
        for half in range(2):
            block = table[1, 2 * tile + half]
            part = source[:, pl.ds(pl.multiple_of((block >> 1) * 128, 128), 128)].astype(F32)
            halves.append(jnp.where((block & 1) == half, part, pltpu.roll(part, 64, 1)))
        both = jnp.where(lane < 64, halves[0], halves[1])
        target[:, tile * 128 : tile * 128 + 128] = both.astype(BF)


def chain_kernel(
    table, mask, mine, theirs, k_low, k_high, k_own, out, band, full, k_all, rows_i, rows_j, raw, first, second, sems
):
    gx, core, gy = place()
    copies = []
    for rank in range(NB):
        source = pl.multiple_of(table[1, rank] * 64, 64)
        for half, held in enumerate((k_low, k_high)):
            copy = pltpu.make_async_copy(
                held.at[pl.ds(source, 64), :],
                k_all.at[half, rank * 64 : rank * 64 + 64, :],
                sems.at[len(copies)],
            )
            copy.start()
            copies.append(copy)
    a, b = iota((256, 256), 0), iota((256, 256), 1)
    same_block = (a >> 6) == (b >> 6)
    eye = (a == b).astype(F32).astype(BF)
    empty = jnp.zeros((128, 128), BF)
    for held, parity in ((mine, core), (theirs, 1 - core)):
        for v in range(8):
            for half in range(2):
                at = (16 * half + 2 * v + parity) * 64
                for part in range(8):
                    to = pl.multiple_of(at + 16 * (part % 4), 16)
                    band[part // 4, pl.ds(to, 16), :] = held[v * 8 + part, 16 * half : 16 * half + 16, :]
    for mat in range(2):
        for quad in range(8):
            at = quad * 256
            top = band[mat, at : at + 128, :]
            low = band[mat, at + 128 : at + 256, :]
            wide = jnp.concatenate(
                [jnp.concatenate([top, empty], axis=1), jnp.concatenate([empty, low], axis=1)], axis=0
            )
            own = wide[:, :256]
            strict = jnp.where(same_block, 0.0, own.astype(F32)).astype(BF)
            own = (own.astype(F32) + dot_t(eye, strict)).astype(BF)
            full[mat, at : at + 256, at : at + 256] = own
            for step in (1, 2):
                to = ((quad + step) % 8) * 256
                part = wide[:, step * 256 : step * 256 + 256]
                full[mat, at : at + 256, to : to + 256] = part
                full[mat, to : to + 256, at : at + 256] = dot_t(eye, part).astype(BF)
            for step in (3, 4, 5):
                to = ((quad + step) % 8) * 256
                full[mat, at : at + 256, to : to + 256] = jnp.zeros((256, 256), BF)
    for mat in range(2):
        for i in range(2):
            rank = pl.multiple_of(table[2, 2 * gx + i] * 64, 64)
            rows_i[mat * 128 + i * 64 : mat * 128 + i * 64 + 64, :] = full[mat, pl.ds(rank, 64), :]
        for j in range(4):
            rank = pl.multiple_of(table[2, 4 * gy + j] * 64, 64)
            rows_j[mat, j * 64 : j * 64 + 64, :] = full[mat, pl.ds(rank, 64), :]
    for copy in copies:
        copy.wait()
    for n in range(8):
        raw[:, n * 256 : n * 256 + 256] = dot(rows_i[...], k_all[n // 4, :, n % 4 * 256 : n % 4 * 256 + 256]).astype(BF)
    regroup(table, raw, first)
    for quad in range(8):
        at = quad * 256
        both = jnp.zeros((256, 256), F32)
        cross = jnp.zeros((128, 256), F32)
        for step in (-2, -1, 0, 1, 2):
            k = ((quad + step) % 8) * 256
            both = both + dot(first[:, k : k + 256], full[0, k : k + 256, at : at + 256])
            cross = cross + dot(first[:128, k : k + 256], full[1, k : k + 256, at : at + 256])
        second[:128, at : at + 256] = (both[128:] + cross).astype(BF)
        second[128:, at : at + 256] = both[:128].astype(BF)
    pair = dot_t(first[128:, :], rows_j[0]) + dot_t(first[:128, :], rows_j[1])
    for n in range(8):
        raw[:, n * 256 : n * 256 + 256] = dot(second[...], k_all[n // 4, :, n % 4 * 256 : n % 4 * 256 + 256]).astype(BF)
    regroup(table, raw, first)
    cubic = dot_t(first[:128, :], rows_j[0]) + dot_t(first[128:, :], rows_j[1])
    grad = 3.0 * pair - 2.0 * cubic
    kernel = k_own[:, pl.ds(pl.multiple_of(gy * 256, 256), 256)].astype(F32)
    r, l = iota((128, 256), 0), iota((128, 256), 1)
    keep = jnp.zeros((128, 256), F32)
    for i in range(2):
        for j in range(4):
            here = ((r >> 6) == i) & ((l >> 6) == j)
            keep = keep + jnp.where(here, mask[i, 4 * gy + j].astype(F32), 0.0)
    out[...] = kernel - 0.5 * (keep * grad)


def chain(table, mask, mine, theirs, k_low, k_high, k_own):
    vmem = pl.BlockSpec(memory_space=pltpu.VMEM)
    smem = pl.BlockSpec(memory_space=pltpu.SMEM)
    anywhere = pl.BlockSpec(memory_space=pl.ANY)
    return pl.pallas_call(
        chain_kernel,
        out_shape=jax.ShapeDtypeStruct((128, 256), F32),
        in_specs=[smem, smem, vmem, vmem, anywhere, anywhere, vmem],
        out_specs=vmem,
        scratch_shapes=[
            pltpu.VMEM((2, 2048, 640), BF),
            pltpu.VMEM((2, 2048, 2048), BF),
            pltpu.VMEM((2, 2048, 1024), BF),
            pltpu.VMEM((256, 2048), BF),
            pltpu.VMEM((2, 256, 2048), BF),
            pltpu.VMEM((256, 2048), BF),
            pltpu.VMEM((256, 2048), BF),
            pltpu.VMEM((256, 2048), BF),
            pltpu.SemaphoreType.DMA((2 * NB,)),
        ],
        compiler_params=params(),
        name="chain",
    )(table, mask, mine, theirs, k_low, k_high, k_own)


def extended(block):
    forward = [(i, (i + 1) % 8) for i in range(8)]
    backward = [(target, source) for source, target in forward]
    low = lax.ppermute(block[:, -1:], GY, forward)
    high = lax.ppermute(block[:, :1], GY, backward)
    return jnp.concatenate([low, block, high], axis=1)


def spread(values, mask):
    rows, cols = (values.shape[-2], values.shape[-1])
    grid = values.reshape(values.shape[:-2] + (rows // BLOCK, BLOCK, cols // BLOCK, BLOCK))
    return (grid * mask.astype(values.dtype)[:, None, :, None]).reshape(values.shape)


def matmul(left, right):
    return jnp.dot(left, right, preferred_element_type=F32)


def general(phi, potential, kernel, mask_s, mask_k):
    nrows = phi.shape[0]
    width = kernel.shape[1] // 8
    col_start = lax.axis_index(GY) * width
    padded = extended(phi).astype(F32)
    center = padded[:, 1:-1]
    lap = padded[:, 2:] + padded[:, :-2] - 6.0 * center
    for axis in (2, 3):
        lap = lap + jnp.roll(center, 1, axis) + jnp.roll(center, -1, axis)
    hphi = (-0.5 * lap + potential[None] * center).astype(BF)
    flat_phi = phi.reshape(nrows, -1)
    flat_h = hphi.reshape(nrows, -1)
    piece = lax.all_gather(phi, ROWS, axis=0, tiled=True)
    other = piece.reshape(piece.shape[0], -1)
    s_part = jnp.einsum("ap,bp->ab", flat_phi, other, preferred_element_type=F32)
    h_part = jnp.einsum("ap,bp->ab", flat_h, other, preferred_element_type=F32)
    partial_sums = jnp.stack([s_part, h_part])
    mask_cols = lax.dynamic_slice_in_dim(mask_s, col_start // BLOCK, width // BLOCK, 1)
    local = lax.psum_scatter(partial_sums, GY, scatter_dimension=2, tiled=True)
    block_pair = spread(local, mask_cols).astype(BF)
    rows = lax.all_gather(block_pair, GY, axis=2, tiled=True)
    k_mat = spread(kernel, mask_k)
    pieces = lax.all_gather(block_pair, ROWS, axis=1, tiled=True)
    x_acc = matmul(k_mat, pieces[0])
    y_acc = matmul(k_mat, pieces[1])
    pair = jnp.stack([x_acc.astype(BF), y_acc.astype(BF)])
    columns = lax.all_gather(pair, ROWS, axis=1, tiled=True)
    p_one = matmul(rows[1], columns[0])
    p_two = matmul(rows[0], columns[1])
    z_mat = matmul(rows[0], columns[0])
    trio = jnp.stack([p_one, z_mat, p_two]).astype(BF)
    trio_rows = lax.all_gather(trio, GY, axis=2, tiled=True)
    q_mat = (
        matmul(trio_rows[0], columns[0])
        + matmul(trio_rows[1], columns[1])
        + matmul(trio_rows[2], columns[0])
    )
    grad = 3.0 * (trio[0].astype(F32) + trio[2].astype(F32)) - 2.0 * q_mat
    mask_kcols = lax.dynamic_slice_in_dim(mask_k, col_start // BLOCK, width // BLOCK, 1)
    kernel_cols = lax.dynamic_slice_in_dim(kernel, col_start, width, 1).astype(F32)
    return kernel_cols - 0.5 * spread(grad, mask_kcols)


def sparse(phi, potential, kernel, mask_s, mask_k):
    swap = [(0, 1), (1, 0)]
    k_low, k_high = trim(mask_k, kernel)
    k_low = lax.all_gather(k_low, ROWS, axis=0, tiled=True)
    halo = lax.ppermute(phi[:, 0].reshape(128, 1024), GY, [((i + 1) % 8, i) for i in range(8)])
    packed = pack(phi.reshape(128, 10240), halo, mask_s)
    own = lax.all_to_all(packed, "v", 0, 0, tiled=True)
    own, k_high = lax.optimization_barrier((own, k_high))
    k_high = lax.all_gather(k_high, ROWS, axis=0, tiled=True)
    other = lax.ppermute(own, "c", swap)
    notes = own.reshape(16, 64, 1536)[:, 0, 1280:1408]
    notes = lax.all_to_all(jnp.broadcast_to(notes[None], (16, 16, LANES)), ("c",) + GY, 0, 0, tiled=True)
    pot = lax.dynamic_index_in_dim(potential.reshape(10, 4, 8, 32), lax.axis_index("v"), 2, keepdims=False)
    pot = jnp.pad(pot.reshape(10, LANES), ((0, 6), (0, 0)))
    table, weights = plan(notes)
    part = integrals(table, own, other, pot)
    parts = lax.all_to_all(part, PEERS, 0, 0, tiled=True)
    mine = lax.all_to_all(combine(parts, weights), PEERS, 0, 0, tiled=True)
    theirs = lax.ppermute(mine, "c", swap)
    result = chain(table, mask_k, mine, theirs, k_low, k_high, kernel)
    return result, table[3, 0] == 1


def shards(*args):
    result, fits = sparse(*args)
    return lax.cond(fits, lambda *_: result, general, *args)


def solution(mesh):
    fine = Mesh(mesh.devices.reshape(8, 2, 4, 2), ("v", "c", "x", "yh"))
    in_specs = (
        P(ROWS, GY, None, None),
        P(GY, None, None),
        P(ROWS, None),
        P(ROWS, None),
        P(ROWS, None),
    )
    out_specs = P(ROWS, GY)
    return jax.shard_map(shards, mesh=fine, in_specs=in_specs, out_specs=out_specs, check_vma=False)
```

```python
import jax
import jax.numpy as jnp
from jax import lax
from jax.experimental import pallas as pl
from jax.experimental.pallas import tpu as pltpu
from jax.sharding import Mesh, PartitionSpec as P

BLOCK = 64
NB = 32
SLOTS = 16
REACH = 8
CUT = 512
LANES = 128
ROWS = ("v", "c")
GY = ("x", "yh")
PEERS = ("v", "x", "yh")
BF = jnp.bfloat16
F32 = jnp.float32
I32 = jnp.int32
VMEM_LIMIT = 56 * 1024 * 1024


def iota(shape, dim):
    return lax.broadcasted_iota(I32, shape, dim)


def dot(left, right):
    return lax.dot_general(left, right, (((1,), (0,)), ((), ())), preferred_element_type=F32)


def dot_t(left, right):
    return lax.dot_general(left, right, (((1,), (1,)), ((), ())), preferred_element_type=F32)


def exact(left, right):
    return dot(left.astype(BF), right.astype(BF))


def exact_t(left, right):
    return dot_t(left.astype(BF), right.astype(BF))


def place():
    core = lax.axis_index("c")
    return 2 * lax.axis_index("v") + core, core, 2 * lax.axis_index("x") + lax.axis_index("yh")


def params(**more):
    return pltpu.CompilerParams(vmem_limit_bytes=VMEM_LIMIT, **more)


def spare_lanes():
    note, lane = iota((LANES, LANES), 0), iota((LANES, LANES), 1)
    group, at = lane >> 5, lane & 31
    index = group * 12 + jnp.where(at >= 16, at - 20, at - 10)
    spare = ((at & 15) >= 10) & (index < 42)
    wanted = jnp.where(index < 10, index, index + 22)
    return (spare & (note == wanted)).astype(F32)


def pack_kernel(flat, mask, packed):
    src, dst = iota((512, 512), 0), iota((512, 512), 1)
    wanted = ((dst >> 5) & 3) * 128 + (dst >> 7) * 32 + (dst & 31)
    perm = (src == wanted).astype(F32).astype(BF)
    for x in range(10):
        for half in range(2):
            pieces = []
            for y in range(4):
                at = y * 256 + half * 128
                pieces.append(flat[:, x * 1024 + at : x * 1024 + at + 128])
            out = dot(jnp.concatenate(pieces, axis=1), perm).astype(BF)
            for j in range(4):
                packed[4 * half + j, :, x * 128 : x * 128 + 128] = out[:, j * 128 : j * 128 + 128]
    src, dst = iota((1280, 256), 0), iota((1280, 256), 1)
    plane, lane = src >> 7, src & 127
    low = (dst < 128) & ((lane & 31) == 31) & ((dst & 127) == (lane & 96) + plane)
    high = (dst >= 128) & ((lane & 31) == 0) & ((dst & 127) == (lane & 96) + 16 + plane)
    edges = (low | high).astype(F32).astype(BF)
    lane, row = iota((2, LANES), 1), iota((2, LANES), 0)
    meta = jnp.zeros((2, LANES), F32)
    for block in range(2):
        for x in range(10):
            part = jnp.abs(flat[block * 64 : block * 64 + 64, x * 1024 : x * 1024 + 1024].astype(F32))
            top = jnp.max(jnp.max(part, axis=0, keepdims=True), axis=1, keepdims=True)
            used = (top > 0.0).astype(F32)
            meta = meta + jnp.where((row == block) & (lane == x), used, 0.0)
    spare = spare_lanes()
    meta = exact(meta, spare) + exact(mask[...].astype(F32), spare[NB : 2 * NB])
    row = iota((128, LANES), 0)
    notes = jnp.where(row == 0, meta[0:1], 0.0) + jnp.where(row == 64, meta[1:2], 0.0)
    found = [dot(packed[v, :, :1280], edges) for v in range(8)]
    for v in range(8):
        tile = found[v][:, :128] + found[(v + 1) % 8][:, 128:]
        packed[v, :, 1280:1408] = (tile + notes).astype(BF)


def pack(flat, mask):
    vmem = pl.BlockSpec(memory_space=pltpu.VMEM)
    return pl.pallas_call(
        pack_kernel,
        out_shape=jax.ShapeDtypeStruct((8, 128, 1408), BF),
        in_specs=[vmem, vmem],
        out_specs=vmem,
        compiler_params=params(),
        name="pack",
    )(flat, mask)


def plan_kernel(notes, table, weights):
    gx, core, gy = place()
    square = (LANES, LANES)
    zeros = jnp.zeros((96, LANES), F32)
    found = dot_t(notes[...].reshape(256, LANES), spare_lanes().astype(BF))
    lane = iota((16, LANES), 1)
    planes, masks = [], []
    for c in range(2):
        total = jnp.zeros((16, LANES), F32)
        for domain in range(8):
            at = (c * 8 + domain) * 16
            part = jnp.where(lane < 10, found[at : at + 16], 0.0)
            total = total + (pltpu.roll(part, 10 * domain, 1) if domain else part)
        planes.append(total)
        part = pltpu.roll(found[c * 128 : c * 128 + 16], 96, 1)
        masks.append(jnp.where(lane < NB, part, 0.0))
    block, at = iota((NB, NB), 0), iota((NB, NB), 1)
    spot = (block == 4 * ((at & 15) >> 1) + 2 * (at >> 4) + (at & 1)).astype(F32)
    used = exact(spot, jnp.concatenate(planes, axis=0))
    near = exact(spot, jnp.concatenate(masks, axis=0))
    tall_used = jnp.concatenate([used, zeros], axis=0)
    tall_near = jnp.concatenate([near, zeros], axis=0)
    a, b = iota(square, 0), iota(square, 1)
    apart = jnp.abs(a - b)
    apart = jnp.minimum(apart, 80 - apart)
    far = ((a < 80) & (b < 80) & (apart > 13)).astype(F32)
    row, lane = iota((NB, LANES), 0), iota((NB, LANES), 1)
    outside = exact(used, far)
    fits = (outside < 0.5) & (lane < 80)
    centre = jnp.min(jnp.where(fits, lane.astype(F32), 127.0), axis=1, keepdims=True)
    key_col = centre * 32.0 + row[:, :1].astype(F32)
    key_row = jnp.sum(jnp.where(row == lane, key_col, 0.0), axis=0, keepdims=True)
    rank_col = jnp.sum(((lane < NB) & (key_row < key_col)).astype(F32), axis=1, keepdims=True)
    rank_row = jnp.sum((key_col < key_row).astype(F32), axis=0, keepdims=True)
    lane_f = lane.astype(F32)
    block_row = jnp.sum(jnp.where(rank_col == lane_f, row.astype(F32), 0.0), axis=0, keepdims=True)
    order = ((rank_row == a.astype(F32)) & (b < NB) & (a < NB)).astype(F32)
    order_rows = order[:NB]
    d8, l8 = iota((8, LANES), 0), iota((8, LANES), 1)
    ahead = l8 - 10 * d8
    ahead = jnp.where(ahead < 0, ahead + 80, ahead)
    touch = ((ahead <= 10) & (l8 < 80)).astype(F32)
    flags = (exact_t(touch, tall_used) > 0.5).astype(F32)
    flags = exact_t(flags, order)
    upper = jnp.where(l8 < SLOTS, pltpu.roll(flags, LANES - SLOTS, 1), 0.0)
    clash = jnp.max(upper * flags)
    sorted_near = exact_t(exact(order_rows, tall_near), order)
    gap = (lane - row) & 31
    stray = (sorted_near > 0.5) & (lane < NB) & (gap > REACH) & (gap < NB - REACH)
    good = (clash < 0.5) & (jnp.max(stray.astype(F32)) < 0.5)
    shift = b - core
    pick = ((a == ((gx + shift) & 15)) & (a < SLOTS)).astype(F32)
    col_half = exact(upper, pick)
    row_half = jnp.sum(jnp.where(l8 == gx, upper, 0.0), axis=1, keepdims=True)
    step = l8 - core
    allowed = ((step >= 0) & (step <= REACH)).astype(F32)
    j, lanes = iota((LANES, 640), 0), iota((LANES, 640), 1)
    widen = ((lanes >> 6) == j).astype(F32)
    for half in range(2):
        mine = gx + 16 * half
        line = jnp.sum(jnp.where(row == mine, sorted_near, 0.0), axis=0, keepdims=True)
        pick = ((a == ((mine + shift) & 31)) & (a < NB)).astype(F32)
        line = exact(jnp.broadcast_to(line, (8, LANES)), pick)
        other = (((mine + step) & 31) >> 4).astype(F32)
        same = (row_half == float(half)) & (col_half == other)
        small = jnp.where(same, line * allowed, 0.0)
        weights[8 * half : 8 * half + 8, :] = exact(small, widen)
    own = jnp.sum(jnp.where(d8 == gy, upper, 0.0), axis=0, keepdims=True)
    source = jnp.where(own > 0.5, pltpu.roll(block_row, LANES - SLOTS, 1), block_row)
    ok = jnp.where(good, 1.0, 0.0)
    out = jnp.where(d8 == 0, source, 0.0) + jnp.where(d8 == 1, block_row, 0.0)
    out = out + jnp.where(d8 == 2, rank_row, 0.0) + jnp.where(d8 == 3, ok, 0.0)
    table[...] = jnp.where(l8 < NB, out, 0.0).astype(I32)


def plan(notes):
    vmem = pl.BlockSpec(memory_space=pltpu.VMEM)
    return pl.pallas_call(
        plan_kernel,
        out_shape=(
            jax.ShapeDtypeStruct((8, LANES), I32),
            jax.ShapeDtypeStruct((16, 640), F32),
        ),
        in_specs=[vmem],
        out_specs=(vmem, vmem),
        compiler_params=params(),
        name="plan",
    )(notes)


def trim_kernel(mask, kernel, *parts):
    lane = iota((64, LANES), 1)
    for rows in range(2):
        for tile in range(16):
            part = kernel[rows * 64 : rows * 64 + 64, tile * 128 : tile * 128 + 128].astype(F32)
            keep = jnp.where(lane < 64, mask[rows, 2 * tile], mask[rows, 2 * tile + 1]).astype(F32)
            at = tile * 128 - (0 if tile * 128 < CUT else CUT)
            parts[tile * 128 >= CUT][rows * 64 : rows * 64 + 64, at : at + 128] = (part * keep).astype(BF)


def trim(mask, kernel):
    vmem = pl.BlockSpec(memory_space=pltpu.VMEM)
    smem = pl.BlockSpec(memory_space=pltpu.SMEM)
    return pl.pallas_call(
        trim_kernel,
        out_shape=tuple(jax.ShapeDtypeStruct((128, width), BF) for width in (CUT, 2048 - CUT)),
        in_specs=[smem, vmem],
        out_specs=(vmem, vmem),
        compiler_params=params(),
        name="trim",
    )(mask, kernel)


def integrals_kernel(
    table, own, other, own_next, other_next, pot, out, right, left_s, left_h, sems, next_sems
):
    _, core, _ = place()
    for slot in range(SLOTS):
        block = table[0, slot]
        at = (block >> 2) * 2 + (block & 1)
        mine = ((block >> 1) & 1) == core
        to = right.at[slot * 64 : slot * 64 + 64, :1408]
        after = right.at[slot * 64 : slot * 64 + 64, 1408:]

        @pl.when(mine)
        def _():
            pltpu.make_async_copy(own.at[at], to, sems.at[slot]).start()
            pltpu.make_async_copy(own_next.at[at], after, next_sems.at[slot]).start()

        @pl.when(jnp.logical_not(mine))
        def _():
            pltpu.make_async_copy(other.at[at], to, sems.at[slot]).start()
            pltpu.make_async_copy(other_next.at[at], after, next_sems.at[slot]).start()

    lane = iota((64, LANES), 1)
    low, high = (lane & 31) == 0, (lane & 31) == 31
    for pair in range(8):
        for side in range(2):
            slot = 2 * pair + side
            rows = right.at[slot * 64 : slot * 64 + 64, :1408]
            after = right.at[slot * 64 : slot * 64 + 64, 1408:]
            pltpu.make_async_copy(own.at[0], rows, sems.at[slot]).wait()
            pltpu.make_async_copy(own_next.at[0], after, next_sems.at[slot]).wait()
        to = pair * 64
        source = pl.multiple_of((2 * pair + core) * 64, 64)
        data = right[pl.ds(source, 64), :]
        left_s[to : to + 64, :] = data[:, :1280]
        before = jnp.zeros((64, LANES), F32)
        here = data[:, :128].astype(F32)
        for x in range(10):
            after = data[:, x * 128 + 128 : x * 128 + 256].astype(F32) if x < 9 else jnp.zeros((64, LANES), F32)
            near = before + after
            near = near + pltpu.roll(here, 32, 1) + pltpu.roll(here, 96, 1)
            near = near + jnp.where(low, 0.0, pltpu.roll(here, 1, 1))
            near = near + jnp.where(high, 0.0, pltpu.roll(here, 127, 1))
            value = (3.0 + pot[x : x + 1, :]) * here - 0.5 * near
            left_h[to : to + 64, x * 128 : x * 128 + 128] = value.astype(BF)
            before, here = here, after
        edge = jnp.where((lane & 15) < 10, data[:, 1280:1408].astype(F32), 0.0)
        left_h[to : to + 64, 1280:1408] = (-0.5 * edge).astype(BF)
        left_h[to : to + 64, 1408:1536] = (-0.5 * data[:, 1152:1280].astype(F32)).astype(BF)
        left_h[to : to + 64, 1536:1664] = (-0.5 * data[:, 1408:1536].astype(F32)).astype(BF)
        for side in range(2):
            at = (2 * pair + side) * 64
            edge = right[at : at + 64, 1280:1408].astype(F32)
            edge = jnp.where((lane & 31) < 16, pltpu.roll(edge, 112, 1), pltpu.roll(edge, 16, 1))
            edge = jnp.where((lane & 15) < 10, edge, 0.0)
            right[at : at + 64, 1280:1408] = edge.astype(BF)
    for chunk in range(4):
        cols = right[chunk * 256 : chunk * 256 + 256, :]
        found = (
            dot_t(left_s[...], cols[:, :1280]),
            dot_t(left_h[:, :1536], cols) + dot_t(left_h[:, 1536:], cols[:, 1152:1280]),
        )
        for mat in range(2):
            value = found[mat].astype(BF)
            for rows in range(8):
                for side in range(2):
                    step = (2 * chunk + side - rows) % 8
                    if step < 5:
                        for part in range(4):
                            at = rows * 64 + part * 16
                            out[rows * 8 + mat * 4 + part, :, step * 128 : step * 128 + 128] = value[
                                at : at + 16, side * 128 : side * 128 + 128
                            ]


def integrals(table, own, other, own_next, other_next, pot):
    vmem = pl.BlockSpec(memory_space=pltpu.VMEM)
    anywhere = pl.BlockSpec(memory_space=pl.ANY)
    return pl.pallas_call(
        integrals_kernel,
        out_shape=jax.ShapeDtypeStruct((64, 16, 640), BF),
        in_specs=[pl.BlockSpec(memory_space=pltpu.SMEM), anywhere, anywhere, anywhere, anywhere, vmem],
        out_specs=vmem,
        scratch_shapes=[
            pltpu.VMEM((1024, 1536), BF),
            pltpu.VMEM((512, 1280), BF),
            pltpu.VMEM((512, 1664), BF),
            pltpu.SemaphoreType.DMA((SLOTS,)),
            pltpu.SemaphoreType.DMA((SLOTS,)),
        ],
        compiler_params=params(),
        name="integrals",
    )(
        table,
        own.reshape(16, 64, 1408),
        other.reshape(16, 64, 1408),
        own_next.reshape(16, 64, LANES),
        other_next.reshape(16, 64, LANES),
        pot,
    )


def combine_kernel(parts, weights, out, lines_all, sems):
    lines = [jnp.zeros((16, 640), F32), jnp.zeros((16, 640), F32)]
    for domain in range(8):
        total = parts[domain].astype(F32)
        for v in range(1, 8):
            total = total + parts[v * 8 + domain].astype(F32)
        for half in range(2):
            lines[half] = lines[half] + total * weights[8 * half + domain : 8 * half + domain + 1, :]
    _, core, _ = place()
    even = core == 0
    lane = iota((16, LANES), 1)
    tails = []
    for half in range(2):
        line = lines[half]
        lines_all[:, 512 * half : 512 * half + 512] = jnp.where(even, line[:, :512], line[:, 128:]).astype(BF)
        tail = jnp.where(even, line[:, 512:], line[:, :128])
        tails.append(jnp.where(even == (half == 0), tail, pltpu.roll(tail, 64, 1)))
    lines_all[:, 1024:] = jnp.where(lane < 64, tails[0], tails[1]).astype(BF)
    copies = [pltpu.make_async_copy(lines_all, out.at[peer], sems.at[peer]) for peer in range(64)]
    for copy in copies:
        copy.start()
    for copy in copies:
        copy.wait()


def combine(parts, weights):
    vmem = pl.BlockSpec(memory_space=pltpu.VMEM)
    return pl.pallas_call(
        combine_kernel,
        out_shape=jax.ShapeDtypeStruct((64, 16, 1152), BF),
        in_specs=[vmem, vmem],
        out_specs=pl.BlockSpec(memory_space=pl.ANY),
        scratch_shapes=[pltpu.VMEM((16, 1152), BF), pltpu.SemaphoreType.DMA((64,))],
        compiler_params=params(),
        name="combine",
    )(parts, weights)


def regroup(table, source, target):
    lane = iota((256, LANES), 1)
    for tile in range(16):
        halves = []
        for half in range(2):
            block = table[1, 2 * tile + half]
            part = source[:, pl.ds(pl.multiple_of((block >> 1) * 128, 128), 128)].astype(F32)
            halves.append(jnp.where((block & 1) == half, part, pltpu.roll(part, 64, 1)))
        both = jnp.where(lane < 64, halves[0], halves[1])
        target[:, tile * 128 : tile * 128 + 128] = both.astype(BF)


def chain_kernel(
    table, mask, mine, theirs, k_low, k_high, k_own, out, band, full, k_all, rows_i, rows_j, raw, first, second, sems, band_sems
):
    gx, core, gy = place()
    arrivals = []
    for part, (held, parity) in enumerate(((mine, core), (theirs, 1 - core))):
        arrivals.append(pltpu.make_async_copy(held, band.at[parity], band_sems.at[part]))
        arrivals[part].start()
    copies = []

    def fetch(rank):
        source = pl.multiple_of(table[1, rank] * 64, 64)
        for held, start, width in ((k_low, 0, CUT), (k_high, CUT, 2048 - CUT)):
            copy = pltpu.make_async_copy(
                held.at[pl.ds(source, 64), :],
                k_all.at[rank * 64 : rank * 64 + 64, start : start + width],
                sems.at[len(copies)],
            )
            copy.start()
            copies.append(copy)

    a, b = iota((256, 256), 0), iota((256, 256), 1)
    same_block = (a >> 6) == (b >> 6)
    eye = (a == b).astype(F32).astype(BF)
    empty = jnp.zeros((64, 128), BF)
    lane = iota((64, LANES), 1)

    def line(mat, rank):
        half, v, parity = rank // 16, rank % 16 // 2, rank % 2
        block = band[parity, v * 8 + 4 * mat : v * 8 + 4 * mat + 4].reshape(64, 1152)
        body = block[:, 512 * half : 512 * half + 512]
        tail = block[:, 1024:].astype(F32)
        tail = tail if half == parity else pltpu.roll(tail, 64, 1)
        tail = jnp.where((lane < 64) == (parity == 0), tail, 0.0).astype(BF)
        parts = [body, tail] if parity == 0 else [tail, body]
        return jnp.concatenate(parts + [empty] if rank % 4 < 2 else [empty] + parts, axis=1)

    for arrival in arrivals:
        arrival.wait()
    for mat in range(2):
        for quad in range(8):
            at = quad * 256
            wide = jnp.concatenate([line(mat, 4 * quad + i) for i in range(4)], axis=0)
            if mat == 0:
                for i in range(4):
                    fetch(4 * quad + i)
            own = wide[:, :256]
            strict = jnp.where(same_block, 0.0, own.astype(F32)).astype(BF)
            own = (own.astype(F32) + dot_t(eye, strict)).astype(BF)
            full[mat, at : at + 256, at : at + 256] = own
            for step in (1, 2):
                to = ((quad + step) % 8) * 256
                part = wide[:, step * 256 : step * 256 + 256]
                full[mat, at : at + 256, to : to + 256] = part
                full[mat, to : to + 256, at : at + 256] = dot_t(eye, part).astype(BF)
            for step in (3, 4, 5):
                to = ((quad + step) % 8) * 256
                full[mat, at : at + 256, to : to + 256] = jnp.zeros((256, 256), BF)
    for mat in range(2):
        for i in range(2):
            rank = pl.multiple_of(table[2, 2 * gx + i] * 64, 64)
            rows_i[mat * 128 + i * 64 : mat * 128 + i * 64 + 64, :] = full[mat, pl.ds(rank, 64), :]
        for j in range(4):
            rank = pl.multiple_of(table[2, 4 * gy + j] * 64, 64)
            rows_j[mat, j * 64 : j * 64 + 64, :] = full[mat, pl.ds(rank, 64), :]
    for copy in copies:
        copy.wait()
    for n in range(8):
        raw[:, n * 256 : n * 256 + 256] = dot(rows_i[...], k_all[:, n * 256 : n * 256 + 256]).astype(BF)
    regroup(table, raw, first)
    for quad in range(8):
        at = quad * 256
        both = jnp.zeros((256, 256), F32)
        cross = jnp.zeros((128, 256), F32)
        for step in (-2, -1, 0, 1, 2):
            k = ((quad + step) % 8) * 256
            both = both + dot(first[:, k : k + 256], full[0, k : k + 256, at : at + 256])
            cross = cross + dot(first[:128, k : k + 256], full[1, k : k + 256, at : at + 256])
        second[:128, at : at + 256] = (both[128:] + cross).astype(BF)
        second[128:, at : at + 256] = both[:128].astype(BF)
    pair = dot_t(first[128:, :], rows_j[0]) + dot_t(first[:128, :], rows_j[1])
    for n in range(8):
        raw[:, n * 256 : n * 256 + 256] = dot(second[...], k_all[:, n * 256 : n * 256 + 256]).astype(BF)
    regroup(table, raw, first)
    cubic = dot_t(first[:128, :], rows_j[0]) + dot_t(first[128:, :], rows_j[1])
    grad = 3.0 * pair - 2.0 * cubic
    kernel = k_own[:, pl.ds(pl.multiple_of(gy * 256, 256), 256)].astype(F32)
    r, l = iota((128, 256), 0), iota((128, 256), 1)
    keep = jnp.zeros((128, 256), F32)
    for i in range(2):
        for j in range(4):
            here = ((r >> 6) == i) & ((l >> 6) == j)
            keep = keep + jnp.where(here, mask[i, 4 * gy + j].astype(F32), 0.0)
    out[...] = kernel - 0.5 * (keep * grad)


def chain(table, mask, mine, theirs, k_low, k_high, k_own):
    vmem = pl.BlockSpec(memory_space=pltpu.VMEM)
    smem = pl.BlockSpec(memory_space=pltpu.SMEM)
    anywhere = pl.BlockSpec(memory_space=pl.ANY)
    return pl.pallas_call(
        chain_kernel,
        out_shape=jax.ShapeDtypeStruct((128, 256), F32),
        in_specs=[smem, smem, anywhere, anywhere, anywhere, anywhere, vmem],
        out_specs=vmem,
        scratch_shapes=[
            pltpu.VMEM((2, 64, 16, 1152), BF),
            pltpu.VMEM((2, 2048, 2048), BF),
            pltpu.VMEM((2048, 2048), BF),
            pltpu.VMEM((256, 2048), BF),
            pltpu.VMEM((2, 256, 2048), BF),
            pltpu.VMEM((256, 2048), BF),
            pltpu.VMEM((256, 2048), BF),
            pltpu.VMEM((256, 2048), BF),
            pltpu.SemaphoreType.DMA((2 * NB,)),
            pltpu.SemaphoreType.DMA((2,)),
        ],
        compiler_params=params(),
        name="chain",
    )(table, mask, mine, theirs, k_low, k_high, k_own)


def extended(block):
    forward = [(i, (i + 1) % 8) for i in range(8)]
    backward = [(target, source) for source, target in forward]
    low = lax.ppermute(block[:, -1:], GY, forward)
    high = lax.ppermute(block[:, :1], GY, backward)
    return jnp.concatenate([low, block, high], axis=1)


def spread(values, mask):
    rows, cols = (values.shape[-2], values.shape[-1])
    grid = values.reshape(values.shape[:-2] + (rows // BLOCK, BLOCK, cols // BLOCK, BLOCK))
    return (grid * mask.astype(values.dtype)[:, None, :, None]).reshape(values.shape)


def matmul(left, right):
    return jnp.dot(left, right, preferred_element_type=F32)


def general(phi, potential, kernel, mask_s, mask_k):
    nrows = phi.shape[0]
    width = kernel.shape[1] // 8
    col_start = lax.axis_index(GY) * width
    padded = extended(phi).astype(F32)
    center = padded[:, 1:-1]
    lap = padded[:, 2:] + padded[:, :-2] - 6.0 * center
    for axis in (2, 3):
        lap = lap + jnp.roll(center, 1, axis) + jnp.roll(center, -1, axis)
    hphi = (-0.5 * lap + potential[None] * center).astype(BF)
    flat_phi = phi.reshape(nrows, -1)
    flat_h = hphi.reshape(nrows, -1)
    piece = lax.all_gather(phi, ROWS, axis=0, tiled=True)
    other = piece.reshape(piece.shape[0], -1)
    s_part = jnp.einsum("ap,bp->ab", flat_phi, other, preferred_element_type=F32)
    h_part = jnp.einsum("ap,bp->ab", flat_h, other, preferred_element_type=F32)
    partial_sums = jnp.stack([s_part, h_part])
    mask_cols = lax.dynamic_slice_in_dim(mask_s, col_start // BLOCK, width // BLOCK, 1)
    local = lax.psum_scatter(partial_sums, GY, scatter_dimension=2, tiled=True)
    block_pair = spread(local, mask_cols).astype(BF)
    rows = lax.all_gather(block_pair, GY, axis=2, tiled=True)
    k_mat = spread(kernel, mask_k)
    pieces = lax.all_gather(block_pair, ROWS, axis=1, tiled=True)
    x_acc = matmul(k_mat, pieces[0])
    y_acc = matmul(k_mat, pieces[1])
    pair = jnp.stack([x_acc.astype(BF), y_acc.astype(BF)])
    columns = lax.all_gather(pair, ROWS, axis=1, tiled=True)
    p_one = matmul(rows[1], columns[0])
    p_two = matmul(rows[0], columns[1])
    z_mat = matmul(rows[0], columns[0])
    trio = jnp.stack([p_one, z_mat, p_two]).astype(BF)
    trio_rows = lax.all_gather(trio, GY, axis=2, tiled=True)
    q_mat = (
        matmul(trio_rows[0], columns[0])
        + matmul(trio_rows[1], columns[1])
        + matmul(trio_rows[2], columns[0])
    )
    grad = 3.0 * (trio[0].astype(F32) + trio[2].astype(F32)) - 2.0 * q_mat
    mask_kcols = lax.dynamic_slice_in_dim(mask_k, col_start // BLOCK, width // BLOCK, 1)
    kernel_cols = lax.dynamic_slice_in_dim(kernel, col_start, width, 1).astype(F32)
    return kernel_cols - 0.5 * spread(grad, mask_kcols)


def sparse(phi, potential, kernel, mask_s, mask_k):
    swap = [(0, 1), (1, 0)]
    k_low, k_high = trim(mask_k, kernel)
    k_low = lax.all_gather(k_low, ROWS, axis=0, tiled=True)
    packed = pack(phi.reshape(128, 10240), mask_s)
    own = lax.all_to_all(packed, "v", 0, 0, tiled=True)
    own, k_high = lax.optimization_barrier((own, k_high))
    k_high = lax.all_gather(k_high, ROWS, axis=0, tiled=True)
    other = lax.ppermute(own, "c", swap)
    own_next = lax.ppermute(own[:, :, :LANES], GY, [((i + 1) % 8, i) for i in range(8)])
    notes = own.reshape(16, 64, 1408)[:, 0, 1280:1408]
    notes = lax.all_to_all(jnp.broadcast_to(notes[None], (16, 16, LANES)), ("c",) + GY, 0, 0, tiled=True)
    notes, own_next = lax.optimization_barrier((notes, own_next))
    other_next = lax.ppermute(own_next, "c", swap)
    pot = lax.dynamic_index_in_dim(potential.reshape(10, 4, 8, 32), lax.axis_index("v"), 2, keepdims=False)
    pot = jnp.pad(pot.reshape(10, LANES), ((0, 6), (0, 0)))
    table, weights = plan(notes)
    part = integrals(table, own, other, own_next, other_next, pot)
    parts = lax.all_to_all(part, PEERS, 0, 0, tiled=True)
    mine = lax.all_to_all(combine(parts, weights), PEERS, 0, 0, tiled=True)
    theirs = lax.ppermute(mine, "c", swap)
    result = chain(table, mask_k, mine, theirs, k_low, k_high, kernel)
    return result, table[3, 0] == 1


def shards(*args):
    result, fits = sparse(*args)
    return lax.cond(fits, lambda *_: result, general, *args)


def solution(mesh):
    fine = Mesh(mesh.devices.reshape(8, 2, 4, 2), ("v", "c", "x", "yh"))
    in_specs = (
        P(ROWS, GY, None, None),
        P(GY, None, None),
        P(ROWS, None),
        P(ROWS, None),
        P(ROWS, None),
    )
    out_specs = P(ROWS, GY)
    return jax.shard_map(shards, mesh=fine, in_specs=in_specs, out_specs=out_specs, check_vma=False)
```

```python
import jax
import jax.numpy as jnp
from jax import lax
from jax.experimental import pallas as pl
from jax.experimental.pallas import tpu as pltpu
from jax.sharding import Mesh, PartitionSpec as P

BLOCK = 64
NB = 32
SLOTS = 16
REACH = 8
CUT = 512
LANES = 128
ROWS = ("v", "c")
GY = ("x", "yh")
PEERS = ("v", "x", "yh")
BF = jnp.bfloat16
F32 = jnp.float32
I32 = jnp.int32
VMEM_LIMIT = 56 * 1024 * 1024


def iota(shape, dim):
    return lax.broadcasted_iota(I32, shape, dim)


def dot(left, right):
    return lax.dot_general(left, right, (((1,), (0,)), ((), ())), preferred_element_type=F32)


def dot_t(left, right):
    return lax.dot_general(left, right, (((1,), (1,)), ((), ())), preferred_element_type=F32)


def exact(left, right):
    return dot(left.astype(BF), right.astype(BF))


def exact_t(left, right):
    return dot_t(left.astype(BF), right.astype(BF))


def place():
    core = lax.axis_index("c")
    return 2 * lax.axis_index("v") + core, core, 2 * lax.axis_index("x") + lax.axis_index("yh")


def params(**more):
    return pltpu.CompilerParams(vmem_limit_bytes=VMEM_LIMIT, **more)


def spare_lanes():
    note, lane = iota((LANES, LANES), 0), iota((LANES, LANES), 1)
    group, at = lane >> 5, lane & 31
    index = group * 12 + jnp.where(at >= 16, at - 20, at - 10)
    spare = ((at & 15) >= 10) & (index < 42)
    wanted = jnp.where(index < 10, index, index + 22)
    return (spare & (note == wanted)).astype(F32)


def pack_kernel(flat, mask, packed):
    src, dst = iota((512, 512), 0), iota((512, 512), 1)
    wanted = ((dst >> 5) & 3) * 128 + (dst >> 7) * 32 + (dst & 31)
    perm = (src == wanted).astype(F32).astype(BF)
    for x in range(10):
        for half in range(2):
            pieces = []
            for y in range(4):
                at = y * 256 + half * 128
                pieces.append(flat[:, x * 1024 + at : x * 1024 + at + 128])
            out = dot(jnp.concatenate(pieces, axis=1), perm).astype(BF)
            for j in range(4):
                packed[4 * half + j, :, x * 128 : x * 128 + 128] = out[:, j * 128 : j * 128 + 128]
    src, dst = iota((1280, 256), 0), iota((1280, 256), 1)
    plane, lane = src >> 7, src & 127
    low = (dst < 128) & ((lane & 31) == 31) & ((dst & 127) == (lane & 96) + plane)
    high = (dst >= 128) & ((lane & 31) == 0) & ((dst & 127) == (lane & 96) + 16 + plane)
    edges = (low | high).astype(F32).astype(BF)
    lane, row = iota((2, LANES), 1), iota((2, LANES), 0)
    meta = jnp.zeros((2, LANES), F32)
    for block in range(2):
        for x in range(10):
            part = jnp.abs(flat[block * 64 : block * 64 + 64, x * 1024 : x * 1024 + 1024].astype(F32))
            top = jnp.max(jnp.max(part, axis=0, keepdims=True), axis=1, keepdims=True)
            used = (top > 0.0).astype(F32)
            meta = meta + jnp.where((row == block) & (lane == x), used, 0.0)
    spare = spare_lanes()
    meta = exact(meta, spare) + exact(mask[...].astype(F32), spare[NB : 2 * NB])
    row = iota((128, LANES), 0)
    notes = jnp.where(row == 0, meta[0:1], 0.0) + jnp.where(row == 64, meta[1:2], 0.0)
    found = [dot(packed[v, :, :1280], edges) for v in range(8)]
    for v in range(8):
        tile = found[v][:, :128] + found[(v + 1) % 8][:, 128:]
        packed[v, :, 1280:1408] = (tile + notes).astype(BF)


def pack(flat, mask):
    vmem = pl.BlockSpec(memory_space=pltpu.VMEM)
    return pl.pallas_call(
        pack_kernel,
        out_shape=jax.ShapeDtypeStruct((8, 128, 1408), BF),
        in_specs=[vmem, vmem],
        out_specs=vmem,
        compiler_params=params(),
        name="pack",
    )(flat, mask)


def plan_kernel(notes, table, weights):
    gx, core, gy = place()
    square = (LANES, LANES)
    zeros = jnp.zeros((96, LANES), F32)
    found = dot_t(notes[...].reshape(256, LANES), spare_lanes().astype(BF))
    lane = iota((16, LANES), 1)
    planes, masks = [], []
    for c in range(2):
        total = jnp.zeros((16, LANES), F32)
        for domain in range(8):
            at = (c * 8 + domain) * 16
            part = jnp.where(lane < 10, found[at : at + 16], 0.0)
            total = total + (pltpu.roll(part, 10 * domain, 1) if domain else part)
        planes.append(total)
        part = pltpu.roll(found[c * 128 : c * 128 + 16], 96, 1)
        masks.append(jnp.where(lane < NB, part, 0.0))
    block, at = iota((NB, NB), 0), iota((NB, NB), 1)
    spot = (block == 4 * ((at & 15) >> 1) + 2 * (at >> 4) + (at & 1)).astype(F32)
    used = exact(spot, jnp.concatenate(planes, axis=0))
    near = exact(spot, jnp.concatenate(masks, axis=0))
    tall_used = jnp.concatenate([used, zeros], axis=0)
    tall_near = jnp.concatenate([near, zeros], axis=0)
    a, b = iota(square, 0), iota(square, 1)
    apart = jnp.abs(a - b)
    apart = jnp.minimum(apart, 80 - apart)
    far = ((a < 80) & (b < 80) & (apart > 13)).astype(F32)
    row, lane = iota((NB, LANES), 0), iota((NB, LANES), 1)
    outside = exact(used, far)
    fits = (outside < 0.5) & (lane < 80)
    centre = jnp.min(jnp.where(fits, lane.astype(F32), 127.0), axis=1, keepdims=True)
    key_col = centre * 32.0 + row[:, :1].astype(F32)
    key_row = jnp.sum(jnp.where(row == lane, key_col, 0.0), axis=0, keepdims=True)
    rank_col = jnp.sum(((lane < NB) & (key_row < key_col)).astype(F32), axis=1, keepdims=True)
    rank_row = jnp.sum((key_col < key_row).astype(F32), axis=0, keepdims=True)
    lane_f = lane.astype(F32)
    block_row = jnp.sum(jnp.where(rank_col == lane_f, row.astype(F32), 0.0), axis=0, keepdims=True)
    order = ((rank_row == a.astype(F32)) & (b < NB) & (a < NB)).astype(F32)
    order_rows = order[:NB]
    d8, l8 = iota((8, LANES), 0), iota((8, LANES), 1)
    ahead = l8 - 10 * d8
    ahead = jnp.where(ahead < 0, ahead + 80, ahead)
    touch = ((ahead <= 10) & (l8 < 80)).astype(F32)
    flags = (exact_t(touch, tall_used) > 0.5).astype(F32)
    flags = exact_t(flags, order)
    upper = jnp.where(l8 < SLOTS, pltpu.roll(flags, LANES - SLOTS, 1), 0.0)
    clash = jnp.max(upper * flags)
    sorted_near = exact_t(exact(order_rows, tall_near), order)
    gap = (lane - row) & 31
    stray = (sorted_near > 0.5) & (lane < NB) & (gap > REACH) & (gap < NB - REACH)
    good = (clash < 0.5) & (jnp.max(stray.astype(F32)) < 0.5)
    shift = b - core
    pick = ((a == ((gx + shift) & 15)) & (a < SLOTS)).astype(F32)
    col_half = exact(upper, pick)
    row_half = jnp.sum(jnp.where(l8 == gx, upper, 0.0), axis=1, keepdims=True)
    step = l8 - core
    allowed = ((step >= 0) & (step <= REACH)).astype(F32)
    j, lanes = iota((LANES, 640), 0), iota((LANES, 640), 1)
    widen = ((lanes >> 6) == j).astype(F32)
    for half in range(2):
        mine = gx + 16 * half
        line = jnp.sum(jnp.where(row == mine, sorted_near, 0.0), axis=0, keepdims=True)
        pick = ((a == ((mine + shift) & 31)) & (a < NB)).astype(F32)
        line = exact(jnp.broadcast_to(line, (8, LANES)), pick)
        other = (((mine + step) & 31) >> 4).astype(F32)
        same = (row_half == float(half)) & (col_half == other)
        small = jnp.where(same, line * allowed, 0.0)
        weights[8 * half : 8 * half + 8, :] = exact(small, widen)
    own = jnp.sum(jnp.where(d8 == gy, upper, 0.0), axis=0, keepdims=True)
    source = jnp.where(own > 0.5, pltpu.roll(block_row, LANES - SLOTS, 1), block_row)
    ok = jnp.where(good, 1.0, 0.0)
    out = jnp.where(d8 == 0, source, 0.0) + jnp.where(d8 == 1, block_row, 0.0)
    out = out + jnp.where(d8 == 2, rank_row, 0.0) + jnp.where(d8 == 3, ok, 0.0)
    table[...] = jnp.where(l8 < NB, out, 0.0).astype(I32)


def plan(notes):
    vmem = pl.BlockSpec(memory_space=pltpu.VMEM)
    return pl.pallas_call(
        plan_kernel,
        out_shape=(
            jax.ShapeDtypeStruct((8, LANES), I32),
            jax.ShapeDtypeStruct((16, 640), F32),
        ),
        in_specs=[vmem],
        out_specs=(vmem, vmem),
        compiler_params=params(),
        name="plan",
    )(notes)


def trim_kernel(mask, kernel, *parts):
    lane = iota((64, LANES), 1)
    for rows in range(2):
        for tile in range(16):
            part = kernel[rows * 64 : rows * 64 + 64, tile * 128 : tile * 128 + 128].astype(F32)
            keep = jnp.where(lane < 64, mask[rows, 2 * tile], mask[rows, 2 * tile + 1]).astype(F32)
            at = tile * 128 - (0 if tile * 128 < CUT else CUT)
            parts[tile * 128 >= CUT][rows * 64 : rows * 64 + 64, at : at + 128] = (part * keep).astype(BF)


def trim(mask, kernel):
    vmem = pl.BlockSpec(memory_space=pltpu.VMEM)
    smem = pl.BlockSpec(memory_space=pltpu.SMEM)
    return pl.pallas_call(
        trim_kernel,
        out_shape=tuple(jax.ShapeDtypeStruct((128, width), BF) for width in (CUT, 2048 - CUT)),
        in_specs=[smem, vmem],
        out_specs=(vmem, vmem),
        compiler_params=params(),
        name="trim",
    )(mask, kernel)


def integrals_kernel(
    table, own, other, own_next, other_next, potential, out, right, left_s, left_h, sems, next_sems
):
    _, core, _ = place()
    for slot in range(SLOTS):
        block = table[0, slot]
        at = (block >> 2) * 2 + (block & 1)
        mine = ((block >> 1) & 1) == core
        to = right.at[slot * 64 : slot * 64 + 64, :1408]
        after = right.at[slot * 64 : slot * 64 + 64, 1408:]

        @pl.when(mine)
        def _():
            pltpu.make_async_copy(own.at[at], to, sems.at[slot]).start()
            pltpu.make_async_copy(own_next.at[at], after, next_sems.at[slot]).start()

        @pl.when(jnp.logical_not(mine))
        def _():
            pltpu.make_async_copy(other.at[at], to, sems.at[slot]).start()
            pltpu.make_async_copy(other_next.at[at], after, next_sems.at[slot]).start()

    lane = iota((64, LANES), 1)
    low, high = (lane & 31) == 0, (lane & 31) == 31
    v = lax.axis_index("v")
    half = pl.ds(pl.multiple_of((v >> 2) * 128, 128), 128)
    group = iota((10, LANES), 1) >> 5
    pot = jnp.zeros((10, LANES), F32)
    for y in range(4):
        turned = pltpu.roll(potential[:, y, half], (32 * (y + 4 - (v & 3))) & 127, 1)
        pot = jnp.where(group == y, turned, pot)
    for pair in range(8):
        for side in range(2):
            slot = 2 * pair + side
            rows = right.at[slot * 64 : slot * 64 + 64, :1408]
            after = right.at[slot * 64 : slot * 64 + 64, 1408:]
            pltpu.make_async_copy(own.at[0], rows, sems.at[slot]).wait()
            pltpu.make_async_copy(own_next.at[0], after, next_sems.at[slot]).wait()
        to = pair * 64
        source = pl.multiple_of((2 * pair + core) * 64, 64)
        data = right[pl.ds(source, 64), :]
        left_s[to : to + 64, :] = data[:, :1280]
        before = jnp.zeros((64, LANES), F32)
        here = data[:, :128].astype(F32)
        for x in range(10):
            after = data[:, x * 128 + 128 : x * 128 + 256].astype(F32) if x < 9 else jnp.zeros((64, LANES), F32)
            near = before + after
            near = near + pltpu.roll(here, 32, 1) + pltpu.roll(here, 96, 1)
            near = near + jnp.where(low, 0.0, pltpu.roll(here, 1, 1))
            near = near + jnp.where(high, 0.0, pltpu.roll(here, 127, 1))
            value = (3.0 + pot[x : x + 1, :]) * here - 0.5 * near
            left_h[to : to + 64, x * 128 : x * 128 + 128] = value.astype(BF)
            before, here = here, after
        edge = jnp.where((lane & 15) < 10, data[:, 1280:1408].astype(F32), 0.0)
        left_h[to : to + 64, 1280:1408] = (-0.5 * edge).astype(BF)
        left_h[to : to + 64, 1408:1536] = (-0.5 * data[:, 1152:1280].astype(F32)).astype(BF)
        left_h[to : to + 64, 1536:1664] = (-0.5 * data[:, 1408:1536].astype(F32)).astype(BF)
        for side in range(2):
            at = (2 * pair + side) * 64
            edge = right[at : at + 64, 1280:1408].astype(F32)
            edge = jnp.where((lane & 31) < 16, pltpu.roll(edge, 112, 1), pltpu.roll(edge, 16, 1))
            edge = jnp.where((lane & 15) < 10, edge, 0.0)
            right[at : at + 64, 1280:1408] = edge.astype(BF)
    for chunk in range(4):
        cols = right[chunk * 256 : chunk * 256 + 256, :]
        found = (
            dot_t(left_s[...], cols[:, :1280]),
            dot_t(left_h[:, :1536], cols) + dot_t(left_h[:, 1536:], cols[:, 1152:1280]),
        )
        for mat in range(2):
            value = found[mat].astype(BF)
            for rows in range(8):
                for side in range(2):
                    step = (2 * chunk + side - rows) % 8
                    if step < 5:
                        for part in range(4):
                            at = rows * 64 + part * 16
                            out[rows * 8 + mat * 4 + part, :, step * 128 : step * 128 + 128] = value[
                                at : at + 16, side * 128 : side * 128 + 128
                            ]


def integrals(table, own, other, own_next, other_next, potential):
    vmem = pl.BlockSpec(memory_space=pltpu.VMEM)
    anywhere = pl.BlockSpec(memory_space=pl.ANY)
    return pl.pallas_call(
        integrals_kernel,
        out_shape=jax.ShapeDtypeStruct((64, 16, 640), BF),
        in_specs=[pl.BlockSpec(memory_space=pltpu.SMEM), anywhere, anywhere, anywhere, anywhere, vmem],
        out_specs=vmem,
        scratch_shapes=[
            pltpu.VMEM((1024, 1536), BF),
            pltpu.VMEM((512, 1280), BF),
            pltpu.VMEM((512, 1664), BF),
            pltpu.SemaphoreType.DMA((SLOTS,)),
            pltpu.SemaphoreType.DMA((SLOTS,)),
        ],
        compiler_params=params(),
        name="integrals",
    )(
        table,
        own.reshape(16, 64, 1408),
        other.reshape(16, 64, 1408),
        own_next.reshape(16, 64, LANES),
        other_next.reshape(16, 64, LANES),
        potential,
    )


def combine_kernel(parts, weights, out, lines_all, sems):
    lines = [jnp.zeros((16, 640), F32), jnp.zeros((16, 640), F32)]
    for domain in range(8):
        total = parts[domain].astype(F32)
        for v in range(1, 8):
            total = total + parts[v * 8 + domain].astype(F32)
        for half in range(2):
            lines[half] = lines[half] + total * weights[8 * half + domain : 8 * half + domain + 1, :]
    _, core, _ = place()
    even = core == 0
    lane = iota((16, LANES), 1)
    tails = []
    for half in range(2):
        line = lines[half]
        lines_all[:, 512 * half : 512 * half + 512] = jnp.where(even, line[:, :512], line[:, 128:]).astype(BF)
        tail = jnp.where(even, line[:, 512:], line[:, :128])
        tails.append(jnp.where(even == (half == 0), tail, pltpu.roll(tail, 64, 1)))
    lines_all[:, 1024:] = jnp.where(lane < 64, tails[0], tails[1]).astype(BF)

    def start(peer, _):
        pltpu.make_async_copy(lines_all, out.at[peer], sems.at[peer]).start()
        return 0

    def finish(peer, _):
        pltpu.make_async_copy(lines_all, out.at[peer], sems.at[peer]).wait()
        return 0

    lax.fori_loop(0, 64, start, 0)
    lax.fori_loop(0, 64, finish, 0)


def combine(parts, weights):
    vmem = pl.BlockSpec(memory_space=pltpu.VMEM)
    return pl.pallas_call(
        combine_kernel,
        out_shape=jax.ShapeDtypeStruct((64, 16, 1152), BF),
        in_specs=[vmem, vmem],
        out_specs=pl.BlockSpec(memory_space=pl.ANY),
        scratch_shapes=[pltpu.VMEM((16, 1152), BF), pltpu.SemaphoreType.DMA((64,))],
        compiler_params=params(),
        name="combine",
    )(parts, weights)


def regroup(table, source, target):
    lane = iota((256, LANES), 1)
    for tile in range(16):
        halves = []
        for half in range(2):
            block = table[1, 2 * tile + half]
            part = source[:, pl.ds(pl.multiple_of((block >> 1) * 128, 128), 128)].astype(F32)
            halves.append(jnp.where((block & 1) == half, part, pltpu.roll(part, 64, 1)))
        both = jnp.where(lane < 64, halves[0], halves[1])
        target[:, tile * 128 : tile * 128 + 128] = both.astype(BF)


def chain_kernel(
    table, mask, mine, theirs, k_low, k_high, k_own, out, band, full, k_all, rows_i, rows_j, raw, first, second, sems, band_sems
):
    gx, core, gy = place()
    arrivals = []
    for part, (held, parity) in enumerate(((mine, core), (theirs, 1 - core))):
        arrivals.append(pltpu.make_async_copy(held, band.at[parity], band_sems.at[part]))
        arrivals[part].start()
    copies = []

    def fetch(rank):
        source = pl.multiple_of(table[1, rank] * 64, 64)
        for held, start, width in ((k_low, 0, CUT), (k_high, CUT, 2048 - CUT)):
            copy = pltpu.make_async_copy(
                held.at[pl.ds(source, 64), :],
                k_all.at[rank * 64 : rank * 64 + 64, start : start + width],
                sems.at[len(copies)],
            )
            copy.start()
            copies.append(copy)

    a, b = iota((256, 256), 0), iota((256, 256), 1)
    same_block = (a >> 6) == (b >> 6)
    eye = (a == b).astype(F32).astype(BF)
    empty = jnp.zeros((64, 128), BF)
    lane = iota((64, LANES), 1)

    def line(mat, rank):
        half, v, parity = rank // 16, rank % 16 // 2, rank % 2
        block = band[parity, v * 8 + 4 * mat : v * 8 + 4 * mat + 4].reshape(64, 1152)
        body = block[:, 512 * half : 512 * half + 512]
        tail = block[:, 1024:].astype(F32)
        tail = tail if half == parity else pltpu.roll(tail, 64, 1)
        tail = jnp.where((lane < 64) == (parity == 0), tail, 0.0).astype(BF)
        parts = [body, tail] if parity == 0 else [tail, body]
        return jnp.concatenate(parts + [empty] if rank % 4 < 2 else [empty] + parts, axis=1)

    for arrival in arrivals:
        arrival.wait()
    for mat in range(2):
        for quad in range(8):
            at = quad * 256
            wide = jnp.concatenate([line(mat, 4 * quad + i) for i in range(4)], axis=0)
            if mat == 0:
                for i in range(4):
                    fetch(4 * quad + i)
            own = wide[:, :256]
            strict = jnp.where(same_block, 0.0, own.astype(F32)).astype(BF)
            own = (own.astype(F32) + dot_t(eye, strict)).astype(BF)
            full[mat, at : at + 256, at : at + 256] = own
            for step in (1, 2):
                to = ((quad + step) % 8) * 256
                part = wide[:, step * 256 : step * 256 + 256]
                full[mat, at : at + 256, to : to + 256] = part
                full[mat, to : to + 256, at : at + 256] = dot_t(eye, part).astype(BF)
            for step in (3, 4, 5):
                to = ((quad + step) % 8) * 256
                full[mat, at : at + 256, to : to + 256] = jnp.zeros((256, 256), BF)
    for mat in range(2):
        for i in range(2):
            rank = pl.multiple_of(table[2, 2 * gx + i] * 64, 64)
            rows_i[mat * 128 + i * 64 : mat * 128 + i * 64 + 64, :] = full[mat, pl.ds(rank, 64), :]
        for j in range(4):
            rank = pl.multiple_of(table[2, 4 * gy + j] * 64, 64)
            rows_j[mat, j * 64 : j * 64 + 64, :] = full[mat, pl.ds(rank, 64), :]
    for copy in copies:
        copy.wait()
    for n in range(8):
        raw[:, n * 256 : n * 256 + 256] = dot(rows_i[...], k_all[:, n * 256 : n * 256 + 256]).astype(BF)
    regroup(table, raw, first)
    for quad in range(8):
        at = quad * 256
        both = jnp.zeros((256, 256), F32)
        cross = jnp.zeros((128, 256), F32)
        for step in (-2, -1, 0, 1, 2):
            k = ((quad + step) % 8) * 256
            both = both + dot(first[:, k : k + 256], full[0, k : k + 256, at : at + 256])
            cross = cross + dot(first[:128, k : k + 256], full[1, k : k + 256, at : at + 256])
        second[:128, at : at + 256] = (both[128:] + cross).astype(BF)
        second[128:, at : at + 256] = both[:128].astype(BF)
    pair = dot_t(first[128:, :], rows_j[0]) + dot_t(first[:128, :], rows_j[1])
    for n in range(8):
        raw[:, n * 256 : n * 256 + 256] = dot(second[...], k_all[:, n * 256 : n * 256 + 256]).astype(BF)
    regroup(table, raw, first)
    cubic = dot_t(first[:128, :], rows_j[0]) + dot_t(first[128:, :], rows_j[1])
    grad = 3.0 * pair - 2.0 * cubic
    kernel = k_own[:, pl.ds(pl.multiple_of(gy * 256, 256), 256)].astype(F32)
    r, l = iota((128, 256), 0), iota((128, 256), 1)
    keep = jnp.zeros((128, 256), F32)
    for i in range(2):
        for j in range(4):
            here = ((r >> 6) == i) & ((l >> 6) == j)
            keep = keep + jnp.where(here, mask[i, 4 * gy + j].astype(F32), 0.0)
    out[...] = kernel - 0.5 * (keep * grad)


def chain(table, mask, mine, theirs, k_low, k_high, k_own):
    vmem = pl.BlockSpec(memory_space=pltpu.VMEM)
    smem = pl.BlockSpec(memory_space=pltpu.SMEM)
    anywhere = pl.BlockSpec(memory_space=pl.ANY)
    return pl.pallas_call(
        chain_kernel,
        out_shape=jax.ShapeDtypeStruct((128, 256), F32),
        in_specs=[smem, smem, anywhere, anywhere, anywhere, anywhere, vmem],
        out_specs=vmem,
        scratch_shapes=[
            pltpu.VMEM((2, 64, 16, 1152), BF),
            pltpu.VMEM((2, 2048, 2048), BF),
            pltpu.VMEM((2048, 2048), BF),
            pltpu.VMEM((256, 2048), BF),
            pltpu.VMEM((2, 256, 2048), BF),
            pltpu.VMEM((256, 2048), BF),
            pltpu.VMEM((256, 2048), BF),
            pltpu.VMEM((256, 2048), BF),
            pltpu.SemaphoreType.DMA((2 * NB,)),
            pltpu.SemaphoreType.DMA((2,)),
        ],
        compiler_params=params(),
        name="chain",
    )(table, mask, mine, theirs, k_low, k_high, k_own)


def extended(block):
    forward = [(i, (i + 1) % 8) for i in range(8)]
    backward = [(target, source) for source, target in forward]
    low = lax.ppermute(block[:, -1:], GY, forward)
    high = lax.ppermute(block[:, :1], GY, backward)
    return jnp.concatenate([low, block, high], axis=1)


def spread(values, mask):
    rows, cols = (values.shape[-2], values.shape[-1])
    grid = values.reshape(values.shape[:-2] + (rows // BLOCK, BLOCK, cols // BLOCK, BLOCK))
    return (grid * mask.astype(values.dtype)[:, None, :, None]).reshape(values.shape)


def matmul(left, right):
    return jnp.dot(left, right, preferred_element_type=F32)


def general(phi, potential, kernel, mask_s, mask_k):
    nrows = phi.shape[0]
    width = kernel.shape[1] // 8
    col_start = lax.axis_index(GY) * width
    padded = extended(phi).astype(F32)
    center = padded[:, 1:-1]
    lap = padded[:, 2:] + padded[:, :-2] - 6.0 * center
    for axis in (2, 3):
        lap = lap + jnp.roll(center, 1, axis) + jnp.roll(center, -1, axis)
    hphi = (-0.5 * lap + potential[None] * center).astype(BF)
    flat_phi = phi.reshape(nrows, -1)
    flat_h = hphi.reshape(nrows, -1)
    piece = lax.all_gather(phi, ROWS, axis=0, tiled=True)
    other = piece.reshape(piece.shape[0], -1)
    s_part = jnp.einsum("ap,bp->ab", flat_phi, other, preferred_element_type=F32)
    h_part = jnp.einsum("ap,bp->ab", flat_h, other, preferred_element_type=F32)
    partial_sums = jnp.stack([s_part, h_part])
    mask_cols = lax.dynamic_slice_in_dim(mask_s, col_start // BLOCK, width // BLOCK, 1)
    local = lax.psum_scatter(partial_sums, GY, scatter_dimension=2, tiled=True)
    block_pair = spread(local, mask_cols).astype(BF)
    rows = lax.all_gather(block_pair, GY, axis=2, tiled=True)
    k_mat = spread(kernel, mask_k)
    pieces = lax.all_gather(block_pair, ROWS, axis=1, tiled=True)
    x_acc = matmul(k_mat, pieces[0])
    y_acc = matmul(k_mat, pieces[1])
    pair = jnp.stack([x_acc.astype(BF), y_acc.astype(BF)])
    columns = lax.all_gather(pair, ROWS, axis=1, tiled=True)
    p_one = matmul(rows[1], columns[0])
    p_two = matmul(rows[0], columns[1])
    z_mat = matmul(rows[0], columns[0])
    trio = jnp.stack([p_one, z_mat, p_two]).astype(BF)
    trio_rows = lax.all_gather(trio, GY, axis=2, tiled=True)
    q_mat = (
        matmul(trio_rows[0], columns[0])
        + matmul(trio_rows[1], columns[1])
        + matmul(trio_rows[2], columns[0])
    )
    grad = 3.0 * (trio[0].astype(F32) + trio[2].astype(F32)) - 2.0 * q_mat
    mask_kcols = lax.dynamic_slice_in_dim(mask_k, col_start // BLOCK, width // BLOCK, 1)
    kernel_cols = lax.dynamic_slice_in_dim(kernel, col_start, width, 1).astype(F32)
    return kernel_cols - 0.5 * spread(grad, mask_kcols)


def sparse(phi, potential, kernel, mask_s, mask_k):
    swap = [(0, 1), (1, 0)]
    k_low, k_high = trim(mask_k, kernel)
    k_low = lax.all_gather(k_low, ROWS, axis=0, tiled=True)
    packed = pack(phi.reshape(128, 10240), mask_s)
    own = lax.all_to_all(packed, "v", 0, 0, tiled=True)
    own, k_high = lax.optimization_barrier((own, k_high))
    k_high = lax.all_gather(k_high, ROWS, axis=0, tiled=True)
    other = lax.ppermute(own, "c", swap)
    own_next = lax.ppermute(own[:, :, :LANES], GY, [((i + 1) % 8, i) for i in range(8)])
    notes = own.reshape(16, 64, 1408)[:, 0, 1280:1408]
    notes = lax.all_to_all(jnp.broadcast_to(notes[None], (16, 16, LANES)), ("c",) + GY, 0, 0, tiled=True)
    notes, own_next = lax.optimization_barrier((notes, own_next))
    other_next = lax.ppermute(own_next, "c", swap)
    table, weights = plan(notes)
    part = integrals(table, own, other, own_next, other_next, potential)
    parts = lax.all_to_all(part, PEERS, 0, 0, tiled=True)
    mine = lax.all_to_all(combine(parts, weights), PEERS, 0, 0, tiled=True)
    theirs = lax.ppermute(mine, "c", swap)
    result = chain(table, mask_k, mine, theirs, k_low, k_high, kernel)
    return result, table[3, 0] == 1


def shards(*args):
    result, fits = sparse(*args)
    return lax.cond(fits, lambda *_: result, general, *args)


def solution(mesh):
    fine = Mesh(mesh.devices.reshape(8, 2, 4, 2), ("v", "c", "x", "yh"))
    in_specs = (
        P(ROWS, GY, None, None),
        P(GY, None, None),
        P(ROWS, None),
        P(ROWS, None),
        P(ROWS, None),
    )
    out_specs = P(ROWS, GY)
    return jax.shard_map(shards, mesh=fine, in_specs=in_specs, out_specs=out_specs, check_vma=False)
```

```python
import jax
import jax.numpy as jnp
from jax import lax
from jax.experimental import pallas as pl
from jax.experimental.pallas import tpu as pltpu
from jax.sharding import Mesh, PartitionSpec as P

BLOCK = 64
NB = 32
SLOTS = 16
REACH = 8
CUT = 512
LANES = 128
ROWS = ("v", "c")
GY = ("x", "yh")
PEERS = ("v", "x", "yh")
BF = jnp.bfloat16
F32 = jnp.float32
I32 = jnp.int32
VMEM_LIMIT = 56 * 1024 * 1024


def iota(shape, dim):
    return lax.broadcasted_iota(I32, shape, dim)


def dot(left, right):
    return lax.dot_general(left, right, (((1,), (0,)), ((), ())), preferred_element_type=F32)


def dot_t(left, right):
    return lax.dot_general(left, right, (((1,), (1,)), ((), ())), preferred_element_type=F32)


def exact(left, right):
    return dot(left.astype(BF), right.astype(BF))


def exact_t(left, right):
    return dot_t(left.astype(BF), right.astype(BF))


def place():
    core = lax.axis_index("c")
    return 2 * lax.axis_index("v") + core, core, 2 * lax.axis_index("x") + lax.axis_index("yh")


def params(**more):
    return pltpu.CompilerParams(vmem_limit_bytes=VMEM_LIMIT, **more)


def spare_lanes():
    note, lane = iota((LANES, LANES), 0), iota((LANES, LANES), 1)
    group, at = lane >> 5, lane & 31
    index = group * 12 + jnp.where(at >= 16, at - 20, at - 10)
    spare = ((at & 15) >= 10) & (index < 42)
    wanted = jnp.where(index < 10, index, index + 22)
    return (spare & (note == wanted)).astype(F32)


def pack_kernel(source, mask, packed):
    src, dst = iota((512, 512), 0), iota((512, 512), 1)
    wanted = ((dst >> 5) & 3) * 128 + (dst >> 7) * 32 + (dst & 31)
    perm = (src == wanted).astype(F32).astype(BF)
    lane, row = iota((2, LANES), 1), iota((2, LANES), 0)
    meta = jnp.zeros((2, LANES), F32)
    for x in range(10):
        slab = source[:, x].reshape(128, 1024)
        for block in range(2):
            part = jnp.abs(slab[block * 64 : block * 64 + 64].astype(F32))
            top = jnp.max(jnp.max(part, axis=0, keepdims=True), axis=1, keepdims=True)
            used = (top > 0.0).astype(F32)
            meta = meta + jnp.where((row == block) & (lane == x), used, 0.0)
        for half in range(2):
            pieces = []
            for y in range(4):
                at = y * 256 + half * 128
                pieces.append(slab[:, at : at + 128])
            out = dot(jnp.concatenate(pieces, axis=1), perm).astype(BF)
            for j in range(4):
                packed[4 * half + j, :, x * 128 : x * 128 + 128] = out[:, j * 128 : j * 128 + 128]
    src, dst = iota((1280, 256), 0), iota((1280, 256), 1)
    plane, lane = src >> 7, src & 127
    low = (dst < 128) & ((lane & 31) == 31) & ((dst & 127) == (lane & 96) + plane)
    high = (dst >= 128) & ((lane & 31) == 0) & ((dst & 127) == (lane & 96) + 16 + plane)
    edges = (low | high).astype(F32).astype(BF)
    spare = spare_lanes()
    meta = exact(meta, spare) + exact(mask[...].astype(F32), spare[NB : 2 * NB])
    row = iota((128, LANES), 0)
    notes = jnp.where(row == 0, meta[0:1], 0.0) + jnp.where(row == 64, meta[1:2], 0.0)
    found = [dot(packed[v, :, :1280], edges) for v in range(8)]
    for v in range(8):
        tile = found[v][:, :128] + found[(v + 1) % 8][:, 128:]
        packed[v, :, 1280:1408] = (tile + notes).astype(BF)


def pack(phi, mask):
    vmem = pl.BlockSpec(memory_space=pltpu.VMEM)
    return pl.pallas_call(
        pack_kernel,
        out_shape=jax.ShapeDtypeStruct((8, 128, 1408), BF),
        in_specs=[vmem, vmem],
        out_specs=vmem,
        compiler_params=params(),
        name="pack",
    )(phi, mask)


def plan_kernel(notes, table, weights):
    gx, core, gy = place()
    square = (LANES, LANES)
    zeros = jnp.zeros((96, LANES), F32)
    found = dot_t(notes[...].reshape(256, LANES), spare_lanes().astype(BF))
    lane = iota((16, LANES), 1)
    planes, masks = [], []
    for c in range(2):
        total = jnp.zeros((16, LANES), F32)
        for domain in range(8):
            at = (c * 8 + domain) * 16
            part = jnp.where(lane < 10, found[at : at + 16], 0.0)
            total = total + (pltpu.roll(part, 10 * domain, 1) if domain else part)
        planes.append(total)
        part = pltpu.roll(found[c * 128 : c * 128 + 16], 96, 1)
        masks.append(jnp.where(lane < NB, part, 0.0))
    block, at = iota((NB, NB), 0), iota((NB, NB), 1)
    spot = (block == 4 * ((at & 15) >> 1) + 2 * (at >> 4) + (at & 1)).astype(F32)
    used = exact(spot, jnp.concatenate(planes, axis=0))
    near = exact(spot, jnp.concatenate(masks, axis=0))
    tall_used = jnp.concatenate([used, zeros], axis=0)
    tall_near = jnp.concatenate([near, zeros], axis=0)
    a, b = iota(square, 0), iota(square, 1)
    apart = jnp.abs(a - b)
    apart = jnp.minimum(apart, 80 - apart)
    far = ((a < 80) & (b < 80) & (apart > 13)).astype(F32)
    row, lane = iota((NB, LANES), 0), iota((NB, LANES), 1)
    outside = exact(used, far)
    fits = (outside < 0.5) & (lane < 80)
    centre = jnp.min(jnp.where(fits, lane.astype(F32), 127.0), axis=1, keepdims=True)
    key_col = centre * 32.0 + row[:, :1].astype(F32)
    key_row = jnp.sum(jnp.where(row == lane, key_col, 0.0), axis=0, keepdims=True)
    rank_col = jnp.sum(((lane < NB) & (key_row < key_col)).astype(F32), axis=1, keepdims=True)
    rank_row = jnp.sum((key_col < key_row).astype(F32), axis=0, keepdims=True)
    lane_f = lane.astype(F32)
    block_row = jnp.sum(jnp.where(rank_col == lane_f, row.astype(F32), 0.0), axis=0, keepdims=True)
    order = ((rank_row == a.astype(F32)) & (b < NB) & (a < NB)).astype(F32)
    order_rows = order[:NB]
    d8, l8 = iota((8, LANES), 0), iota((8, LANES), 1)
    ahead = l8 - 10 * d8
    ahead = jnp.where(ahead < 0, ahead + 80, ahead)
    touch = ((ahead <= 10) & (l8 < 80)).astype(F32)
    flags = (exact_t(touch, tall_used) > 0.5).astype(F32)
    flags = exact_t(flags, order)
    upper = jnp.where(l8 < SLOTS, pltpu.roll(flags, LANES - SLOTS, 1), 0.0)
    clash = jnp.max(upper * flags)
    sorted_near = exact_t(exact(order_rows, tall_near), order)
    gap = (lane - row) & 31
    stray = (sorted_near > 0.5) & (lane < NB) & (gap > REACH) & (gap < NB - REACH)
    good = (clash < 0.5) & (jnp.max(stray.astype(F32)) < 0.5)
    shift = b - core
    pick = ((a == ((gx + shift) & 15)) & (a < SLOTS)).astype(F32)
    col_half = exact(upper, pick)
    row_half = jnp.sum(jnp.where(l8 == gx, upper, 0.0), axis=1, keepdims=True)
    step = l8 - core
    allowed = ((step >= 0) & (step <= REACH)).astype(F32)
    j, lanes = iota((LANES, 640), 0), iota((LANES, 640), 1)
    widen = ((lanes >> 6) == j).astype(F32)
    for half in range(2):
        mine = gx + 16 * half
        line = jnp.sum(jnp.where(row == mine, sorted_near, 0.0), axis=0, keepdims=True)
        pick = ((a == ((mine + shift) & 31)) & (a < NB)).astype(F32)
        line = exact(jnp.broadcast_to(line, (8, LANES)), pick)
        other = (((mine + step) & 31) >> 4).astype(F32)
        same = (row_half == float(half)) & (col_half == other)
        small = jnp.where(same, line * allowed, 0.0)
        weights[8 * half : 8 * half + 8, :] = exact(small, widen)
    own = jnp.sum(jnp.where(d8 == gy, upper, 0.0), axis=0, keepdims=True)
    source = jnp.where(own > 0.5, pltpu.roll(block_row, LANES - SLOTS, 1), block_row)
    ok = jnp.where(good, 1.0, 0.0)
    out = jnp.where(d8 == 0, source, 0.0) + jnp.where(d8 == 1, block_row, 0.0)
    out = out + jnp.where(d8 == 2, rank_row, 0.0) + jnp.where(d8 == 3, ok, 0.0)
    table[...] = jnp.where(l8 < NB, out, 0.0).astype(I32)


def plan(notes):
    vmem = pl.BlockSpec(memory_space=pltpu.VMEM)
    return pl.pallas_call(
        plan_kernel,
        out_shape=(
            jax.ShapeDtypeStruct((8, LANES), I32),
            jax.ShapeDtypeStruct((16, 640), F32),
        ),
        in_specs=[vmem],
        out_specs=(vmem, vmem),
        compiler_params=params(),
        name="plan",
    )(notes)


def trim_kernel(mask, kernel, *parts):
    lane = iota((64, LANES), 1)
    for rows in range(2):
        for tile in range(16):
            part = kernel[rows * 64 : rows * 64 + 64, tile * 128 : tile * 128 + 128].astype(F32)
            keep = jnp.where(lane < 64, mask[rows, 2 * tile], mask[rows, 2 * tile + 1]).astype(F32)
            at = tile * 128 - (0 if tile * 128 < CUT else CUT)
            parts[tile * 128 >= CUT][rows * 64 : rows * 64 + 64, at : at + 128] = (part * keep).astype(BF)


def trim(mask, kernel):
    vmem = pl.BlockSpec(memory_space=pltpu.VMEM)
    smem = pl.BlockSpec(memory_space=pltpu.SMEM)
    return pl.pallas_call(
        trim_kernel,
        out_shape=tuple(jax.ShapeDtypeStruct((128, width), BF) for width in (CUT, 2048 - CUT)),
        in_specs=[smem, vmem],
        out_specs=(vmem, vmem),
        compiler_params=params(),
        name="trim",
    )(mask, kernel)


def integrals_kernel(
    table, own, other, own_next, other_next, potential, out, right, left_s, left_h, sems, next_sems
):
    _, core, _ = place()
    for slot in range(SLOTS):
        block = table[0, slot]
        at = (block >> 2) * 2 + (block & 1)
        mine = ((block >> 1) & 1) == core
        to = right.at[slot * 64 : slot * 64 + 64, :1408]
        after = right.at[slot * 64 : slot * 64 + 64, 1408:]

        @pl.when(mine)
        def _():
            pltpu.make_async_copy(own.at[at], to, sems.at[slot]).start()
            pltpu.make_async_copy(own_next.at[at], after, next_sems.at[slot]).start()

        @pl.when(jnp.logical_not(mine))
        def _():
            pltpu.make_async_copy(other.at[at], to, sems.at[slot]).start()
            pltpu.make_async_copy(other_next.at[at], after, next_sems.at[slot]).start()

    lane = iota((64, LANES), 1)
    low, high = (lane & 31) == 0, (lane & 31) == 31
    v = lax.axis_index("v")
    half = pl.ds(pl.multiple_of((v >> 2) * 128, 128), 128)
    group = iota((10, LANES), 1) >> 5
    pot = jnp.zeros((10, LANES), F32)
    for y in range(4):
        turned = pltpu.roll(potential[:, y, half], (32 * (y + 4 - (v & 3))) & 127, 1)
        pot = jnp.where(group == y, turned, pot)
    for pair in range(8):
        for side in range(2):
            slot = 2 * pair + side
            rows = right.at[slot * 64 : slot * 64 + 64, :1408]
            after = right.at[slot * 64 : slot * 64 + 64, 1408:]
            pltpu.make_async_copy(own.at[0], rows, sems.at[slot]).wait()
            pltpu.make_async_copy(own_next.at[0], after, next_sems.at[slot]).wait()
        to = pair * 64
        source = pl.multiple_of((2 * pair + core) * 64, 64)
        data = right[pl.ds(source, 64), :]
        left_s[to : to + 64, :] = data[:, :1280]
        before = jnp.zeros((64, LANES), F32)
        here = data[:, :128].astype(F32)
        for x in range(10):
            after = data[:, x * 128 + 128 : x * 128 + 256].astype(F32) if x < 9 else jnp.zeros((64, LANES), F32)
            near = before + after
            near = near + pltpu.roll(here, 32, 1) + pltpu.roll(here, 96, 1)
            near = near + jnp.where(low, 0.0, pltpu.roll(here, 1, 1))
            near = near + jnp.where(high, 0.0, pltpu.roll(here, 127, 1))
            value = (3.0 + pot[x : x + 1, :]) * here - 0.5 * near
            left_h[to : to + 64, x * 128 : x * 128 + 128] = value.astype(BF)
            before, here = here, after
        edge = jnp.where((lane & 15) < 10, data[:, 1280:1408].astype(F32), 0.0)
        left_h[to : to + 64, 1280:1408] = (-0.5 * edge).astype(BF)
        left_h[to : to + 64, 1408:1536] = (-0.5 * data[:, 1152:1280].astype(F32)).astype(BF)
        left_h[to : to + 64, 1536:1664] = (-0.5 * data[:, 1408:1536].astype(F32)).astype(BF)
        for side in range(2):
            at = (2 * pair + side) * 64
            edge = right[at : at + 64, 1280:1408].astype(F32)
            edge = jnp.where((lane & 31) < 16, pltpu.roll(edge, 112, 1), pltpu.roll(edge, 16, 1))
            edge = jnp.where((lane & 15) < 10, edge, 0.0)
            right[at : at + 64, 1280:1408] = edge.astype(BF)
    for chunk in range(4):
        cols = right[chunk * 256 : chunk * 256 + 256, :]
        found = (
            dot_t(left_s[...], cols[:, :1280]),
            dot_t(left_h[:, :1536], cols) + dot_t(left_h[:, 1536:], cols[:, 1152:1280]),
        )
        for mat in range(2):
            value = found[mat].astype(BF)
            for rows in range(8):
                for side in range(2):
                    step = (2 * chunk + side - rows) % 8
                    if step < 5:
                        for part in range(4):
                            at = rows * 64 + part * 16
                            out[rows * 8 + mat * 4 + part, :, step * 128 : step * 128 + 128] = value[
                                at : at + 16, side * 128 : side * 128 + 128
                            ]


def integrals(table, own, other, own_next, other_next, potential):
    vmem = pl.BlockSpec(memory_space=pltpu.VMEM)
    anywhere = pl.BlockSpec(memory_space=pl.ANY)
    return pl.pallas_call(
        integrals_kernel,
        out_shape=jax.ShapeDtypeStruct((64, 16, 640), BF),
        in_specs=[pl.BlockSpec(memory_space=pltpu.SMEM), anywhere, anywhere, anywhere, anywhere, vmem],
        out_specs=vmem,
        scratch_shapes=[
            pltpu.VMEM((1024, 1536), BF),
            pltpu.VMEM((512, 1280), BF),
            pltpu.VMEM((512, 1664), BF),
            pltpu.SemaphoreType.DMA((SLOTS,)),
            pltpu.SemaphoreType.DMA((SLOTS,)),
        ],
        compiler_params=params(),
        name="integrals",
    )(
        table,
        own.reshape(16, 64, 1408),
        other.reshape(16, 64, 1408),
        own_next.reshape(16, 64, LANES),
        other_next.reshape(16, 64, LANES),
        potential,
    )


def combine_kernel(parts, weights, out, lines_all, sems):
    lines = [jnp.zeros((16, 640), F32), jnp.zeros((16, 640), F32)]
    for domain in range(8):
        total = parts[domain].astype(F32)
        for v in range(1, 8):
            total = total + parts[v * 8 + domain].astype(F32)
        for half in range(2):
            lines[half] = lines[half] + total * weights[8 * half + domain : 8 * half + domain + 1, :]
    _, core, _ = place()
    even = core == 0
    lane = iota((16, LANES), 1)
    tails = []
    for half in range(2):
        line = lines[half]
        lines_all[:, 512 * half : 512 * half + 512] = jnp.where(even, line[:, :512], line[:, 128:]).astype(BF)
        tail = jnp.where(even, line[:, 512:], line[:, :128])
        tails.append(jnp.where(even == (half == 0), tail, pltpu.roll(tail, 64, 1)))
    lines_all[:, 1024:] = jnp.where(lane < 64, tails[0], tails[1]).astype(BF)

    def start(peer, _):
        pltpu.make_async_copy(lines_all, out.at[peer], sems.at[peer]).start()
        return 0

    def finish(peer, _):
        pltpu.make_async_copy(lines_all, out.at[peer], sems.at[peer]).wait()
        return 0

    lax.fori_loop(0, 64, start, 0)
    lax.fori_loop(0, 64, finish, 0)


def combine(parts, weights):
    vmem = pl.BlockSpec(memory_space=pltpu.VMEM)
    return pl.pallas_call(
        combine_kernel,
        out_shape=jax.ShapeDtypeStruct((64, 16, 1152), BF),
        in_specs=[vmem, vmem],
        out_specs=pl.BlockSpec(memory_space=pl.ANY),
        scratch_shapes=[pltpu.VMEM((16, 1152), BF), pltpu.SemaphoreType.DMA((64,))],
        compiler_params=params(),
        name="combine",
    )(parts, weights)


def regroup(table, source, target):
    lane = iota((256, LANES), 1)
    for tile in range(16):
        halves = []
        for half in range(2):
            block = table[1, 2 * tile + half]
            part = source[:, pl.ds(pl.multiple_of((block >> 1) * 128, 128), 128)].astype(F32)
            halves.append(jnp.where((block & 1) == half, part, pltpu.roll(part, 64, 1)))
        both = jnp.where(lane < 64, halves[0], halves[1])
        target[:, tile * 128 : tile * 128 + 128] = both.astype(BF)


def chain_kernel(
    table, mask, mine, theirs, k_low, k_high, k_own, out, band, full, k_all, rows_i, rows_j, raw, first, second, sems, band_sems
):
    gx, core, gy = place()
    arrivals = []
    for part, (held, parity) in enumerate(((mine, core), (theirs, 1 - core))):
        arrivals.append(pltpu.make_async_copy(held, band.at[parity], band_sems.at[part]))
        arrivals[part].start()
    copies = []

    def fetch(rank):
        source = pl.multiple_of(table[1, rank] * 64, 64)
        for held, start, width in ((k_low, 0, CUT), (k_high, CUT, 2048 - CUT)):
            copy = pltpu.make_async_copy(
                held.at[pl.ds(source, 64), :],
                k_all.at[rank * 64 : rank * 64 + 64, start : start + width],
                sems.at[len(copies)],
            )
            copy.start()
            copies.append(copy)

    a, b = iota((256, 256), 0), iota((256, 256), 1)
    same_block = (a >> 6) == (b >> 6)
    eye = (a == b).astype(F32).astype(BF)
    empty = jnp.zeros((64, 128), BF)
    lane = iota((64, LANES), 1)

    def line(mat, rank):
        half, v, parity = rank // 16, rank % 16 // 2, rank % 2
        block = band[parity, v * 8 + 4 * mat : v * 8 + 4 * mat + 4].reshape(64, 1152)
        body = block[:, 512 * half : 512 * half + 512]
        tail = block[:, 1024:].astype(F32)
        tail = tail if half == parity else pltpu.roll(tail, 64, 1)
        tail = jnp.where((lane < 64) == (parity == 0), tail, 0.0).astype(BF)
        parts = [body, tail] if parity == 0 else [tail, body]
        return jnp.concatenate(parts + [empty] if rank % 4 < 2 else [empty] + parts, axis=1)

    for arrival in arrivals:
        arrival.wait()
    for mat in range(2):
        for quad in range(8):
            at = quad * 256
            wide = jnp.concatenate([line(mat, 4 * quad + i) for i in range(4)], axis=0)
            if mat == 0:
                for i in range(4):
                    fetch(4 * quad + i)
            own = wide[:, :256]
            strict = jnp.where(same_block, 0.0, own.astype(F32)).astype(BF)
            own = (own.astype(F32) + dot_t(eye, strict)).astype(BF)
            full[mat, at : at + 256, at : at + 256] = own
            for step in (1, 2):
                to = ((quad + step) % 8) * 256
                part = wide[:, step * 256 : step * 256 + 256]
                full[mat, at : at + 256, to : to + 256] = part
                full[mat, to : to + 256, at : at + 256] = dot_t(eye, part).astype(BF)
            for step in (3, 4, 5):
                to = ((quad + step) % 8) * 256
                full[mat, at : at + 256, to : to + 256] = jnp.zeros((256, 256), BF)
    for mat in range(2):
        for i in range(2):
            rank = pl.multiple_of(table[2, 2 * gx + i] * 64, 64)
            rows_i[mat * 128 + i * 64 : mat * 128 + i * 64 + 64, :] = full[mat, pl.ds(rank, 64), :]
        for j in range(4):
            rank = pl.multiple_of(table[2, 4 * gy + j] * 64, 64)
            rows_j[mat, j * 64 : j * 64 + 64, :] = full[mat, pl.ds(rank, 64), :]
    for copy in copies:
        copy.wait()
    for n in range(8):
        raw[:, n * 256 : n * 256 + 256] = dot(rows_i[...], k_all[:, n * 256 : n * 256 + 256]).astype(BF)
    regroup(table, raw, first)
    for quad in range(8):
        at = quad * 256
        both = jnp.zeros((256, 256), F32)
        cross = jnp.zeros((128, 256), F32)
        for step in (-2, -1, 0, 1, 2):
            k = ((quad + step) % 8) * 256
            both = both + dot(first[:, k : k + 256], full[0, k : k + 256, at : at + 256])
            cross = cross + dot(first[:128, k : k + 256], full[1, k : k + 256, at : at + 256])
        second[:128, at : at + 256] = (both[128:] + cross).astype(BF)
        second[128:, at : at + 256] = both[:128].astype(BF)
    pair = dot_t(first[128:, :], rows_j[0]) + dot_t(first[:128, :], rows_j[1])
    for n in range(8):
        raw[:, n * 256 : n * 256 + 256] = dot(second[...], k_all[:, n * 256 : n * 256 + 256]).astype(BF)
    regroup(table, raw, first)
    cubic = dot_t(first[:128, :], rows_j[0]) + dot_t(first[128:, :], rows_j[1])
    grad = 3.0 * pair - 2.0 * cubic
    kernel = k_own[:, pl.ds(pl.multiple_of(gy * 256, 256), 256)].astype(F32)
    r, l = iota((128, 256), 0), iota((128, 256), 1)
    keep = jnp.zeros((128, 256), F32)
    for i in range(2):
        for j in range(4):
            here = ((r >> 6) == i) & ((l >> 6) == j)
            keep = keep + jnp.where(here, mask[i, 4 * gy + j].astype(F32), 0.0)
    out[...] = kernel - 0.5 * (keep * grad)


def chain(table, mask, mine, theirs, k_low, k_high, k_own):
    vmem = pl.BlockSpec(memory_space=pltpu.VMEM)
    smem = pl.BlockSpec(memory_space=pltpu.SMEM)
    anywhere = pl.BlockSpec(memory_space=pl.ANY)
    return pl.pallas_call(
        chain_kernel,
        out_shape=jax.ShapeDtypeStruct((128, 256), F32),
        in_specs=[smem, smem, anywhere, anywhere, anywhere, anywhere, vmem],
        out_specs=vmem,
        scratch_shapes=[
            pltpu.VMEM((2, 64, 16, 1152), BF),
            pltpu.VMEM((2, 2048, 2048), BF),
            pltpu.VMEM((2048, 2048), BF),
            pltpu.VMEM((256, 2048), BF),
            pltpu.VMEM((2, 256, 2048), BF),
            pltpu.VMEM((256, 2048), BF),
            pltpu.VMEM((256, 2048), BF),
            pltpu.VMEM((256, 2048), BF),
            pltpu.SemaphoreType.DMA((2 * NB,)),
            pltpu.SemaphoreType.DMA((2,)),
        ],
        compiler_params=params(),
        name="chain",
    )(table, mask, mine, theirs, k_low, k_high, k_own)


def extended(block):
    forward = [(i, (i + 1) % 8) for i in range(8)]
    backward = [(target, source) for source, target in forward]
    low = lax.ppermute(block[:, -1:], GY, forward)
    high = lax.ppermute(block[:, :1], GY, backward)
    return jnp.concatenate([low, block, high], axis=1)


def spread(values, mask):
    rows, cols = (values.shape[-2], values.shape[-1])
    grid = values.reshape(values.shape[:-2] + (rows // BLOCK, BLOCK, cols // BLOCK, BLOCK))
    return (grid * mask.astype(values.dtype)[:, None, :, None]).reshape(values.shape)


def matmul(left, right):
    return jnp.dot(left, right, preferred_element_type=F32)


def general(phi, potential, kernel, mask_s, mask_k):
    nrows = phi.shape[0]
    width = kernel.shape[1] // 8
    col_start = lax.axis_index(GY) * width
    padded = extended(phi).astype(F32)
    center = padded[:, 1:-1]
    lap = padded[:, 2:] + padded[:, :-2] - 6.0 * center
    for axis in (2, 3):
        lap = lap + jnp.roll(center, 1, axis) + jnp.roll(center, -1, axis)
    hphi = (-0.5 * lap + potential[None] * center).astype(BF)
    flat_phi = phi.reshape(nrows, -1)
    flat_h = hphi.reshape(nrows, -1)
    piece = lax.all_gather(phi, ROWS, axis=0, tiled=True)
    other = piece.reshape(piece.shape[0], -1)
    s_part = jnp.einsum("ap,bp->ab", flat_phi, other, preferred_element_type=F32)
    h_part = jnp.einsum("ap,bp->ab", flat_h, other, preferred_element_type=F32)
    partial_sums = jnp.stack([s_part, h_part])
    mask_cols = lax.dynamic_slice_in_dim(mask_s, col_start // BLOCK, width // BLOCK, 1)
    local = lax.psum_scatter(partial_sums, GY, scatter_dimension=2, tiled=True)
    block_pair = spread(local, mask_cols).astype(BF)
    rows = lax.all_gather(block_pair, GY, axis=2, tiled=True)
    k_mat = spread(kernel, mask_k)
    pieces = lax.all_gather(block_pair, ROWS, axis=1, tiled=True)
    x_acc = matmul(k_mat, pieces[0])
    y_acc = matmul(k_mat, pieces[1])
    pair = jnp.stack([x_acc.astype(BF), y_acc.astype(BF)])
    columns = lax.all_gather(pair, ROWS, axis=1, tiled=True)
    p_one = matmul(rows[1], columns[0])
    p_two = matmul(rows[0], columns[1])
    z_mat = matmul(rows[0], columns[0])
    trio = jnp.stack([p_one, z_mat, p_two]).astype(BF)
    trio_rows = lax.all_gather(trio, GY, axis=2, tiled=True)
    q_mat = (
        matmul(trio_rows[0], columns[0])
        + matmul(trio_rows[1], columns[1])
        + matmul(trio_rows[2], columns[0])
    )
    grad = 3.0 * (trio[0].astype(F32) + trio[2].astype(F32)) - 2.0 * q_mat
    mask_kcols = lax.dynamic_slice_in_dim(mask_k, col_start // BLOCK, width // BLOCK, 1)
    kernel_cols = lax.dynamic_slice_in_dim(kernel, col_start, width, 1).astype(F32)
    return kernel_cols - 0.5 * spread(grad, mask_kcols)


def sparse(phi, potential, kernel, mask_s, mask_k):
    swap = [(0, 1), (1, 0)]
    k_low, k_high = trim(mask_k, kernel)
    k_low = lax.all_gather(k_low, ROWS, axis=0, tiled=True)
    packed = pack(phi, mask_s)
    own = lax.all_to_all(packed, "v", 0, 0, tiled=True)
    own, k_high = lax.optimization_barrier((own, k_high))
    k_high = lax.all_gather(k_high, ROWS, axis=0, tiled=True)
    other = lax.ppermute(own, "c", swap)
    own_next = lax.ppermute(own[:, :, :LANES], GY, [((i + 1) % 8, i) for i in range(8)])
    notes = own.reshape(16, 64, 1408)[:, 0, 1280:1408]
    notes = lax.all_to_all(jnp.broadcast_to(notes[None], (16, 16, LANES)), ("c",) + GY, 0, 0, tiled=True)
    notes, own_next = lax.optimization_barrier((notes, own_next))
    other_next = lax.ppermute(own_next, "c", swap)
    table, weights = plan(notes)
    part = integrals(table, own, other, own_next, other_next, potential)
    parts = lax.all_to_all(part, PEERS, 0, 0, tiled=True)
    mine = lax.all_to_all(combine(parts, weights), PEERS, 0, 0, tiled=True)
    theirs = lax.ppermute(mine, "c", swap)
    result = chain(table, mask_k, mine, theirs, k_low, k_high, kernel)
    return result, table[3, 0] == 1


def shards(*args):
    result, fits = sparse(*args)
    return lax.cond(fits, lambda *_: result, general, *args)


def solution(mesh):
    fine = Mesh(mesh.devices.reshape(8, 2, 4, 2), ("v", "c", "x", "yh"))
    in_specs = (
        P(ROWS, GY, None, None),
        P(GY, None, None),
        P(ROWS, None),
        P(ROWS, None),
        P(ROWS, None),
    )
    out_specs = P(ROWS, GY)
    return jax.shard_map(shards, mesh=fine, in_specs=in_specs, out_specs=out_specs, check_vma=False)
```

```python
import jax
import jax.numpy as jnp
from jax import lax
from jax.experimental import pallas as pl
from jax.experimental.pallas import tpu as pltpu
from jax.sharding import Mesh, PartitionSpec as P

BLOCK = 64
NB = 32
SLOTS = 16
REACH = 8
CUT = 512
LANES = 128
ROWS = ("v", "c")
GY = ("x", "yh")
PEERS = ("v", "x", "yh")
BF = jnp.bfloat16
F32 = jnp.float32
I32 = jnp.int32
VMEM_LIMIT = 56 * 1024 * 1024


def iota(shape, dim):
    return lax.broadcasted_iota(I32, shape, dim)


def dot(left, right):
    return lax.dot_general(left, right, (((1,), (0,)), ((), ())), preferred_element_type=F32)


def dot_t(left, right):
    return lax.dot_general(left, right, (((1,), (1,)), ((), ())), preferred_element_type=F32)


def exact(left, right):
    return dot(left.astype(BF), right.astype(BF))


def exact_t(left, right):
    return dot_t(left.astype(BF), right.astype(BF))


def place():
    core = lax.axis_index("c")
    return 2 * lax.axis_index("v") + core, core, 2 * lax.axis_index("x") + lax.axis_index("yh")


def params(**more):
    return pltpu.CompilerParams(vmem_limit_bytes=VMEM_LIMIT, **more)


def spare_lanes():
    note, lane = iota((LANES, LANES), 0), iota((LANES, LANES), 1)
    group, at = lane >> 5, lane & 31
    index = group * 12 + jnp.where(at >= 16, at - 20, at - 10)
    spare = ((at & 15) >= 10) & (index < 42)
    wanted = jnp.where(index < 10, index, index + 22)
    return (spare & (note == wanted)).astype(F32)


def pack_kernel(source, mask, packed):
    src, dst = iota((512, 512), 0), iota((512, 512), 1)
    wanted = ((dst >> 5) & 3) * 128 + (dst >> 7) * 32 + (dst & 31)
    perm = (src == wanted).astype(F32).astype(BF)
    lane, row = iota((2, LANES), 1), iota((2, LANES), 0)
    meta = jnp.zeros((2, LANES), F32)
    for x in range(10):
        slab = source[:, x].reshape(128, 1024)
        for block in range(2):
            part = jnp.abs(slab[block * 64 : block * 64 + 64].astype(F32))
            top = jnp.max(jnp.max(part, axis=0, keepdims=True), axis=1, keepdims=True)
            used = (top > 0.0).astype(F32)
            meta = meta + jnp.where((row == block) & (lane == x), used, 0.0)
        for half in range(2):
            pieces = []
            for y in range(4):
                at = y * 256 + half * 128
                pieces.append(slab[:, at : at + 128])
            out = dot(jnp.concatenate(pieces, axis=1), perm).astype(BF)
            for j in range(4):
                packed[4 * half + j, :, x * 128 : x * 128 + 128] = out[:, j * 128 : j * 128 + 128]
    src, dst = iota((1280, 256), 0), iota((1280, 256), 1)
    plane, lane = src >> 7, src & 127
    low = (dst < 128) & ((lane & 31) == 31) & ((dst & 127) == (lane & 96) + plane)
    high = (dst >= 128) & ((lane & 31) == 0) & ((dst & 127) == (lane & 96) + 16 + plane)
    edges = (low | high).astype(F32).astype(BF)
    spare = spare_lanes()
    meta = exact(meta, spare) + exact(mask[...].astype(F32), spare[NB : 2 * NB])
    row = iota((128, LANES), 0)
    notes = jnp.where(row == 0, meta[0:1], 0.0) + jnp.where(row == 64, meta[1:2], 0.0)
    found = [dot(packed[v, :, :1280], edges) for v in range(8)]
    for v in range(8):
        tile = found[v][:, :128] + found[(v + 1) % 8][:, 128:]
        packed[v, :, 1280:1408] = (tile + notes).astype(BF)


def pack(phi, mask):
    vmem = pl.BlockSpec(memory_space=pltpu.VMEM)
    return pl.pallas_call(
        pack_kernel,
        out_shape=jax.ShapeDtypeStruct((8, 128, 1408), BF),
        in_specs=[vmem, vmem],
        out_specs=vmem,
        compiler_params=params(),
        name="pack",
    )(phi, mask)


def plan_kernel(notes, table, weights):
    gx, core, gy = place()
    square = (LANES, LANES)
    zeros = jnp.zeros((96, LANES), F32)
    found = dot_t(notes[...].reshape(256, LANES), spare_lanes().astype(BF))
    lane = iota((16, LANES), 1)
    planes, masks = [], []
    for c in range(2):
        total = jnp.zeros((16, LANES), F32)
        for domain in range(8):
            at = (c * 8 + domain) * 16
            part = jnp.where(lane < 10, found[at : at + 16], 0.0)
            total = total + (pltpu.roll(part, 10 * domain, 1) if domain else part)
        planes.append(total)
        part = pltpu.roll(found[c * 128 : c * 128 + 16], 96, 1)
        masks.append(jnp.where(lane < NB, part, 0.0))
    block, at = iota((NB, NB), 0), iota((NB, NB), 1)
    spot = (block == 4 * ((at & 15) >> 1) + 2 * (at >> 4) + (at & 1)).astype(F32)
    used = exact(spot, jnp.concatenate(planes, axis=0))
    near = exact(spot, jnp.concatenate(masks, axis=0))
    tall_used = jnp.concatenate([used, zeros], axis=0)
    tall_near = jnp.concatenate([near, zeros], axis=0)
    a, b = iota(square, 0), iota(square, 1)
    apart = jnp.abs(a - b)
    apart = jnp.minimum(apart, 80 - apart)
    far = ((a < 80) & (b < 80) & (apart > 13)).astype(F32)
    row, lane = iota((NB, LANES), 0), iota((NB, LANES), 1)
    outside = exact(used, far)
    fits = (outside < 0.5) & (lane < 80)
    centre = jnp.min(jnp.where(fits, lane.astype(F32), 127.0), axis=1, keepdims=True)
    key_col = centre * 32.0 + row[:, :1].astype(F32)
    key_row = jnp.sum(jnp.where(row == lane, key_col, 0.0), axis=0, keepdims=True)
    rank_col = jnp.sum(((lane < NB) & (key_row < key_col)).astype(F32), axis=1, keepdims=True)
    rank_row = jnp.sum((key_col < key_row).astype(F32), axis=0, keepdims=True)
    lane_f = lane.astype(F32)
    block_row = jnp.sum(jnp.where(rank_col == lane_f, row.astype(F32), 0.0), axis=0, keepdims=True)
    order = ((rank_row == a.astype(F32)) & (b < NB) & (a < NB)).astype(F32)
    order_rows = order[:NB]
    d8, l8 = iota((8, LANES), 0), iota((8, LANES), 1)
    ahead = l8 - 10 * d8
    ahead = jnp.where(ahead < 0, ahead + 80, ahead)
    touch = ((ahead <= 10) & (l8 < 80)).astype(F32)
    flags = (exact_t(touch, tall_used) > 0.5).astype(F32)
    flags = exact_t(flags, order)
    upper = jnp.where(l8 < SLOTS, pltpu.roll(flags, LANES - SLOTS, 1), 0.0)
    clash = jnp.max(upper * flags)
    sorted_near = exact_t(exact(order_rows, tall_near), order)
    gap = (lane - row) & 31
    stray = (sorted_near > 0.5) & (lane < NB) & (gap > REACH) & (gap < NB - REACH)
    good = (clash < 0.5) & (jnp.max(stray.astype(F32)) < 0.5)
    shift = b - core
    pick = ((a == ((gx + shift) & 15)) & (a < SLOTS)).astype(F32)
    col_half = exact(upper, pick)
    row_half = jnp.sum(jnp.where(l8 == gx, upper, 0.0), axis=1, keepdims=True)
    step = l8 - core
    allowed = ((step >= 0) & (step <= REACH)).astype(F32)
    j, lanes = iota((LANES, 640), 0), iota((LANES, 640), 1)
    widen = ((lanes >> 6) == j).astype(F32)
    for half in range(2):
        mine = gx + 16 * half
        line = jnp.sum(jnp.where(row == mine, sorted_near, 0.0), axis=0, keepdims=True)
        pick = ((a == ((mine + shift) & 31)) & (a < NB)).astype(F32)
        line = exact(jnp.broadcast_to(line, (8, LANES)), pick)
        other = (((mine + step) & 31) >> 4).astype(F32)
        same = (row_half == float(half)) & (col_half == other)
        small = jnp.where(same, line * allowed, 0.0)
        weights[8 * half : 8 * half + 8, :] = exact(small, widen)
    own = jnp.sum(jnp.where(d8 == gy, upper, 0.0), axis=0, keepdims=True)
    source = jnp.where(own > 0.5, pltpu.roll(block_row, LANES - SLOTS, 1), block_row)
    ok = jnp.where(good, 1.0, 0.0)
    out = jnp.where(d8 == 0, source, 0.0) + jnp.where(d8 == 1, block_row, 0.0)
    out = out + jnp.where(d8 == 2, rank_row, 0.0) + jnp.where(d8 == 3, ok, 0.0)
    table[...] = jnp.where(l8 < NB, out, 0.0).astype(I32)


def plan(notes):
    vmem = pl.BlockSpec(memory_space=pltpu.VMEM)
    return pl.pallas_call(
        plan_kernel,
        out_shape=(
            jax.ShapeDtypeStruct((8, LANES), I32),
            jax.ShapeDtypeStruct((16, 640), F32),
        ),
        in_specs=[vmem],
        out_specs=(vmem, vmem),
        compiler_params=params(),
        name="plan",
    )(notes)


def trim_kernel(mask, kernel, *parts):
    lane = iota((64, LANES), 1)
    for rows in range(2):
        for tile in range(16):
            part = kernel[rows * 64 : rows * 64 + 64, tile * 128 : tile * 128 + 128].astype(F32)
            keep = jnp.where(lane < 64, mask[rows, 2 * tile], mask[rows, 2 * tile + 1]).astype(F32)
            at = tile * 128 - (0 if tile * 128 < CUT else CUT)
            parts[tile * 128 >= CUT][rows * 64 : rows * 64 + 64, at : at + 128] = (part * keep).astype(BF)


def trim(mask, kernel):
    vmem = pl.BlockSpec(memory_space=pltpu.VMEM)
    smem = pl.BlockSpec(memory_space=pltpu.SMEM)
    return pl.pallas_call(
        trim_kernel,
        out_shape=tuple(jax.ShapeDtypeStruct((128, width), BF) for width in (CUT, 2048 - CUT)),
        in_specs=[smem, vmem],
        out_specs=(vmem, vmem),
        compiler_params=params(),
        name="trim",
    )(mask, kernel)


def integrals_kernel(
    table, own, other, own_next, other_next, potential, out, right, left_s, left_h, sems, next_sems
):
    _, core, _ = place()
    for slot in range(SLOTS):
        block = table[0, slot]
        at = (block >> 2) * 2 + (block & 1)
        mine = ((block >> 1) & 1) == core
        to = right.at[slot * 64 : slot * 64 + 64, :1408]
        after = right.at[slot * 64 : slot * 64 + 64, 1408:]

        @pl.when(mine)
        def _():
            pltpu.make_async_copy(own.at[at], to, sems.at[slot]).start()
            pltpu.make_async_copy(own_next.at[at], after, next_sems.at[slot]).start()

        @pl.when(jnp.logical_not(mine))
        def _():
            pltpu.make_async_copy(other.at[at], to, sems.at[slot]).start()
            pltpu.make_async_copy(other_next.at[at], after, next_sems.at[slot]).start()

    lane = iota((64, LANES), 1)
    low, high = (lane & 31) == 0, (lane & 31) == 31
    v = lax.axis_index("v")
    half = pl.ds(pl.multiple_of((v >> 2) * 128, 128), 128)
    group = iota((10, LANES), 1) >> 5
    pot = jnp.zeros((10, LANES), F32)
    for y in range(4):
        turned = pltpu.roll(potential[:, y, half], (32 * (y + 4 - (v & 3))) & 127, 1)
        pot = jnp.where(group == y, turned, pot)
    for pair in range(8):
        for side in range(2):
            slot = 2 * pair + side
            rows = right.at[slot * 64 : slot * 64 + 64, :1408]
            after = right.at[slot * 64 : slot * 64 + 64, 1408:]
            pltpu.make_async_copy(own.at[0], rows, sems.at[slot]).wait()
            pltpu.make_async_copy(own_next.at[0], after, next_sems.at[slot]).wait()
        to = pair * 64
        source = pl.multiple_of((2 * pair + core) * 64, 64)
        data = right[pl.ds(source, 64), :]
        left_s[to : to + 64, :] = data[:, :1280]
        before = jnp.zeros((64, LANES), F32)
        here = data[:, :128].astype(F32)
        for x in range(10):
            after = data[:, x * 128 + 128 : x * 128 + 256].astype(F32) if x < 9 else jnp.zeros((64, LANES), F32)
            near = before + after
            near = near + pltpu.roll(here, 32, 1) + pltpu.roll(here, 96, 1)
            near = near + jnp.where(low, 0.0, pltpu.roll(here, 1, 1))
            near = near + jnp.where(high, 0.0, pltpu.roll(here, 127, 1))
            value = (3.0 + pot[x : x + 1, :]) * here - 0.5 * near
            left_h[to : to + 64, x * 128 : x * 128 + 128] = value.astype(BF)
            before, here = here, after
        edge = jnp.where((lane & 15) < 10, data[:, 1280:1408].astype(F32), 0.0)
        left_h[to : to + 64, 1280:1408] = (-0.5 * edge).astype(BF)
        left_h[to : to + 64, 1408:1536] = (-0.5 * data[:, 1152:1280].astype(F32)).astype(BF)
        left_h[to : to + 64, 1536:1664] = (-0.5 * data[:, 1408:1536].astype(F32)).astype(BF)
        for side in range(2):
            at = (2 * pair + side) * 64
            edge = right[at : at + 64, 1280:1408].astype(F32)
            edge = jnp.where((lane & 31) < 16, pltpu.roll(edge, 112, 1), pltpu.roll(edge, 16, 1))
            edge = jnp.where((lane & 15) < 10, edge, 0.0)
            right[at : at + 64, 1280:1408] = edge.astype(BF)
    for chunk in range(4):
        cols = right[chunk * 256 : chunk * 256 + 256, :]
        found = (
            dot_t(left_s[...], cols[:, :1280]),
            dot_t(left_h[:, :1536], cols) + dot_t(left_h[:, 1536:], cols[:, 1152:1280]),
        )
        for mat in range(2):
            value = found[mat].astype(BF)
            for rows in range(8):
                for side in range(2):
                    step = (2 * chunk + side - rows) % 8
                    if step < 5:
                        for part in range(4):
                            at = rows * 64 + part * 16
                            out[rows * 8 + mat * 4 + part, :, step * 128 : step * 128 + 128] = value[
                                at : at + 16, side * 128 : side * 128 + 128
                            ]


def integrals(table, own, other, own_next, other_next, potential):
    vmem = pl.BlockSpec(memory_space=pltpu.VMEM)
    anywhere = pl.BlockSpec(memory_space=pl.ANY)
    return pl.pallas_call(
        integrals_kernel,
        out_shape=jax.ShapeDtypeStruct((64, 16, 640), BF),
        in_specs=[pl.BlockSpec(memory_space=pltpu.SMEM), anywhere, anywhere, anywhere, anywhere, vmem],
        out_specs=vmem,
        scratch_shapes=[
            pltpu.VMEM((1024, 1536), BF),
            pltpu.VMEM((512, 1280), BF),
            pltpu.VMEM((512, 1664), BF),
            pltpu.SemaphoreType.DMA((SLOTS,)),
            pltpu.SemaphoreType.DMA((SLOTS,)),
        ],
        compiler_params=params(),
        name="integrals",
    )(
        table,
        own.reshape(16, 64, 1408),
        other.reshape(16, 64, 1408),
        own_next.reshape(16, 64, LANES),
        other_next.reshape(16, 64, LANES),
        potential,
    )


def combine_kernel(parts, weights, out, lines_all, sems):
    lines = [jnp.zeros((16, 640), F32), jnp.zeros((16, 640), F32)]
    for domain in range(8):
        total = parts[domain].astype(F32)
        for v in range(1, 8):
            total = total + parts[v * 8 + domain].astype(F32)
        for half in range(2):
            lines[half] = lines[half] + total * weights[8 * half + domain : 8 * half + domain + 1, :]
    _, core, _ = place()
    even = core == 0
    lane = iota((16, LANES), 1)
    tails = []
    for half in range(2):
        line = lines[half]
        lines_all[:, 512 * half : 512 * half + 512] = jnp.where(even, line[:, :512], line[:, 128:]).astype(BF)
        tail = jnp.where(even, line[:, 512:], line[:, :128])
        tails.append(jnp.where(even == (half == 0), tail, pltpu.roll(tail, 64, 1)))
    lines_all[:, 1024:] = jnp.where(lane < 64, tails[0], tails[1]).astype(BF)

    def start(peer, _):
        pltpu.make_async_copy(lines_all, out.at[peer], sems.at[peer]).start()
        return 0

    def finish(peer, _):
        pltpu.make_async_copy(lines_all, out.at[peer], sems.at[peer]).wait()
        return 0

    lax.fori_loop(0, 64, start, 0)
    lax.fori_loop(0, 64, finish, 0)


def combine(parts, weights):
    vmem = pl.BlockSpec(memory_space=pltpu.VMEM)
    return pl.pallas_call(
        combine_kernel,
        out_shape=jax.ShapeDtypeStruct((64, 16, 1152), BF),
        in_specs=[vmem, vmem],
        out_specs=pl.BlockSpec(memory_space=pl.ANY),
        scratch_shapes=[pltpu.VMEM((16, 1152), BF), pltpu.SemaphoreType.DMA((64,))],
        compiler_params=params(),
        name="combine",
    )(parts, weights)


def regroup(table, source, target):
    lane = iota((256, LANES), 1)
    for tile in range(16):
        halves = []
        for half in range(2):
            block = table[1, 2 * tile + half]
            part = source[:, pl.ds(pl.multiple_of((block >> 1) * 128, 128), 128)].astype(F32)
            halves.append(jnp.where((block & 1) == half, part, pltpu.roll(part, 64, 1)))
        both = jnp.where(lane < 64, halves[0], halves[1])
        target[:, tile * 128 : tile * 128 + 128] = both.astype(BF)


def chain_kernel(
    table, mask, mine, theirs, k_low, k_high, k_own, out, band, full, k_all, rows_i, rows_j, raw, first, second, sems, band_sems
):
    gx, core, gy = place()
    arrivals = []
    for part, (held, parity) in enumerate(((mine, core), (theirs, 1 - core))):
        arrivals.append(pltpu.make_async_copy(held, band.at[parity], band_sems.at[part]))
        arrivals[part].start()
    copies = []

    def fetch(rank):
        source = pl.multiple_of(table[1, rank] * 64, 64)
        for held, start, width in ((k_low, 0, CUT), (k_high, CUT, 2048 - CUT)):
            copy = pltpu.make_async_copy(
                held.at[pl.ds(source, 64), :],
                k_all.at[rank * 64 : rank * 64 + 64, start : start + width],
                sems.at[len(copies)],
            )
            copy.start()
            copies.append(copy)

    a, b = iota((256, 256), 0), iota((256, 256), 1)
    same_block = (a >> 6) == (b >> 6)
    eye = (a == b).astype(F32).astype(BF)
    empty = jnp.zeros((64, 128), BF)
    lane = iota((64, LANES), 1)

    def line(mat, rank):
        half, v, parity = rank // 16, rank % 16 // 2, rank % 2
        block = band[parity, v * 8 + 4 * mat : v * 8 + 4 * mat + 4].reshape(64, 1152)
        body = block[:, 512 * half : 512 * half + 512]
        tail = block[:, 1024:].astype(F32)
        tail = tail if half == parity else pltpu.roll(tail, 64, 1)
        tail = jnp.where((lane < 64) == (parity == 0), tail, 0.0).astype(BF)
        parts = [body, tail] if parity == 0 else [tail, body]
        return jnp.concatenate(parts + [empty] if rank % 4 < 2 else [empty] + parts, axis=1)

    for arrival in arrivals:
        arrival.wait()
    for mat in range(2):
        for quad in range(8):
            at = quad * 256
            wide = jnp.concatenate([line(mat, 4 * quad + i) for i in range(4)], axis=0)
            if mat == 0:
                for i in range(4):
                    fetch(4 * quad + i)
            own = wide[:, :256]
            strict = jnp.where(same_block, 0.0, own.astype(F32)).astype(BF)
            own = (own.astype(F32) + dot_t(eye, strict)).astype(BF)
            full[mat, at : at + 256, at : at + 256] = own
            for step in (1, 2):
                to = ((quad + step) % 8) * 256
                part = wide[:, step * 256 : step * 256 + 256]
                full[mat, at : at + 256, to : to + 256] = part
                full[mat, to : to + 256, at : at + 256] = dot_t(eye, part).astype(BF)
    rows_i[...] = jnp.zeros((256, 2048), BF)
    rows_j[...] = jnp.zeros((2, 256, 2048), BF)

    def pick(mat, rank, target, start):
        at = pl.ds(pl.multiple_of(rank * 64, 64), 64)
        for step in (6, 7, 0, 1, 2):
            cut = pl.ds(pl.multiple_of(((rank >> 2) + step & 7) * 256, 256), 256)
            target[start : start + 64, cut] = full[mat, at, cut]

    for mat in range(2):
        for i in range(2):
            pick(mat, table[2, 2 * gx + i], rows_i, mat * 128 + i * 64)
        for j in range(4):
            pick(mat, table[2, 4 * gy + j], rows_j.at[mat], j * 64)
    for copy in copies:
        copy.wait()
    for n in range(8):
        raw[:, n * 256 : n * 256 + 256] = dot(rows_i[...], k_all[:, n * 256 : n * 256 + 256]).astype(BF)
    regroup(table, raw, first)
    for quad in range(8):
        at = quad * 256
        both = jnp.zeros((256, 256), F32)
        cross = jnp.zeros((128, 256), F32)
        for step in (-2, -1, 0, 1, 2):
            k = ((quad + step) % 8) * 256
            both = both + dot(first[:, k : k + 256], full[0, k : k + 256, at : at + 256])
            cross = cross + dot(first[:128, k : k + 256], full[1, k : k + 256, at : at + 256])
        second[:128, at : at + 256] = (both[128:] + cross).astype(BF)
        second[128:, at : at + 256] = both[:128].astype(BF)
    pair = dot_t(first[128:, :], rows_j[0]) + dot_t(first[:128, :], rows_j[1])
    for n in range(8):
        raw[:, n * 256 : n * 256 + 256] = dot(second[...], k_all[:, n * 256 : n * 256 + 256]).astype(BF)
    regroup(table, raw, first)
    cubic = dot_t(first[:128, :], rows_j[0]) + dot_t(first[128:, :], rows_j[1])
    grad = 3.0 * pair - 2.0 * cubic
    kernel = k_own[:, pl.ds(pl.multiple_of(gy * 256, 256), 256)].astype(F32)
    r, l = iota((128, 256), 0), iota((128, 256), 1)
    keep = jnp.zeros((128, 256), F32)
    for i in range(2):
        for j in range(4):
            here = ((r >> 6) == i) & ((l >> 6) == j)
            keep = keep + jnp.where(here, mask[i, 4 * gy + j].astype(F32), 0.0)
    out[...] = kernel - 0.5 * (keep * grad)


def chain(table, mask, mine, theirs, k_low, k_high, k_own):
    vmem = pl.BlockSpec(memory_space=pltpu.VMEM)
    smem = pl.BlockSpec(memory_space=pltpu.SMEM)
    anywhere = pl.BlockSpec(memory_space=pl.ANY)
    return pl.pallas_call(
        chain_kernel,
        out_shape=jax.ShapeDtypeStruct((128, 256), F32),
        in_specs=[smem, smem, anywhere, anywhere, anywhere, anywhere, vmem],
        out_specs=vmem,
        scratch_shapes=[
            pltpu.VMEM((2, 64, 16, 1152), BF),
            pltpu.VMEM((2, 2048, 2048), BF),
            pltpu.VMEM((2048, 2048), BF),
            pltpu.VMEM((256, 2048), BF),
            pltpu.VMEM((2, 256, 2048), BF),
            pltpu.VMEM((256, 2048), BF),
            pltpu.VMEM((256, 2048), BF),
            pltpu.VMEM((256, 2048), BF),
            pltpu.SemaphoreType.DMA((2 * NB,)),
            pltpu.SemaphoreType.DMA((2,)),
        ],
        compiler_params=params(),
        name="chain",
    )(table, mask, mine, theirs, k_low, k_high, k_own)


def extended(block):
    forward = [(i, (i + 1) % 8) for i in range(8)]
    backward = [(target, source) for source, target in forward]
    low = lax.ppermute(block[:, -1:], GY, forward)
    high = lax.ppermute(block[:, :1], GY, backward)
    return jnp.concatenate([low, block, high], axis=1)


def spread(values, mask):
    rows, cols = (values.shape[-2], values.shape[-1])
    grid = values.reshape(values.shape[:-2] + (rows // BLOCK, BLOCK, cols // BLOCK, BLOCK))
    return (grid * mask.astype(values.dtype)[:, None, :, None]).reshape(values.shape)


def matmul(left, right):
    return jnp.dot(left, right, preferred_element_type=F32)


def general(phi, potential, kernel, mask_s, mask_k):
    nrows = phi.shape[0]
    width = kernel.shape[1] // 8
    col_start = lax.axis_index(GY) * width
    padded = extended(phi).astype(F32)
    center = padded[:, 1:-1]
    lap = padded[:, 2:] + padded[:, :-2] - 6.0 * center
    for axis in (2, 3):
        lap = lap + jnp.roll(center, 1, axis) + jnp.roll(center, -1, axis)
    hphi = (-0.5 * lap + potential[None] * center).astype(BF)
    flat_phi = phi.reshape(nrows, -1)
    flat_h = hphi.reshape(nrows, -1)
    piece = lax.all_gather(phi, ROWS, axis=0, tiled=True)
    other = piece.reshape(piece.shape[0], -1)
    s_part = jnp.einsum("ap,bp->ab", flat_phi, other, preferred_element_type=F32)
    h_part = jnp.einsum("ap,bp->ab", flat_h, other, preferred_element_type=F32)
    partial_sums = jnp.stack([s_part, h_part])
    mask_cols = lax.dynamic_slice_in_dim(mask_s, col_start // BLOCK, width // BLOCK, 1)
    local = lax.psum_scatter(partial_sums, GY, scatter_dimension=2, tiled=True)
    block_pair = spread(local, mask_cols).astype(BF)
    rows = lax.all_gather(block_pair, GY, axis=2, tiled=True)
    k_mat = spread(kernel, mask_k)
    pieces = lax.all_gather(block_pair, ROWS, axis=1, tiled=True)
    x_acc = matmul(k_mat, pieces[0])
    y_acc = matmul(k_mat, pieces[1])
    pair = jnp.stack([x_acc.astype(BF), y_acc.astype(BF)])
    columns = lax.all_gather(pair, ROWS, axis=1, tiled=True)
    p_one = matmul(rows[1], columns[0])
    p_two = matmul(rows[0], columns[1])
    z_mat = matmul(rows[0], columns[0])
    trio = jnp.stack([p_one, z_mat, p_two]).astype(BF)
    trio_rows = lax.all_gather(trio, GY, axis=2, tiled=True)
    q_mat = (
        matmul(trio_rows[0], columns[0])
        + matmul(trio_rows[1], columns[1])
        + matmul(trio_rows[2], columns[0])
    )
    grad = 3.0 * (trio[0].astype(F32) + trio[2].astype(F32)) - 2.0 * q_mat
    mask_kcols = lax.dynamic_slice_in_dim(mask_k, col_start // BLOCK, width // BLOCK, 1)
    kernel_cols = lax.dynamic_slice_in_dim(kernel, col_start, width, 1).astype(F32)
    return kernel_cols - 0.5 * spread(grad, mask_kcols)


def sparse(phi, potential, kernel, mask_s, mask_k):
    swap = [(0, 1), (1, 0)]
    k_low, k_high = trim(mask_k, kernel)
    k_low = lax.all_gather(k_low, ROWS, axis=0, tiled=True)
    packed = pack(phi, mask_s)
    own = lax.all_to_all(packed, "v", 0, 0, tiled=True)
    own, k_high = lax.optimization_barrier((own, k_high))
    k_high = lax.all_gather(k_high, ROWS, axis=0, tiled=True)
    other = lax.ppermute(own, "c", swap)
    own_next = lax.ppermute(own[:, :, :LANES], GY, [((i + 1) % 8, i) for i in range(8)])
    notes = own.reshape(16, 64, 1408)[:, 0, 1280:1408]
    notes = lax.all_to_all(jnp.broadcast_to(notes[None], (16, 16, LANES)), ("c",) + GY, 0, 0, tiled=True)
    notes, own_next = lax.optimization_barrier((notes, own_next))
    other_next = lax.ppermute(own_next, "c", swap)
    table, weights = plan(notes)
    part = integrals(table, own, other, own_next, other_next, potential)
    parts = lax.all_to_all(part, PEERS, 0, 0, tiled=True)
    mine = lax.all_to_all(combine(parts, weights), PEERS, 0, 0, tiled=True)
    theirs = lax.ppermute(mine, "c", swap)
    result = chain(table, mask_k, mine, theirs, k_low, k_high, kernel)
    return result, table[3, 0] == 1


def shards(*args):
    result, fits = sparse(*args)
    return lax.cond(fits, lambda *_: result, general, *args)


def solution(mesh):
    fine = Mesh(mesh.devices.reshape(8, 2, 4, 2), ("v", "c", "x", "yh"))
    in_specs = (
        P(ROWS, GY, None, None),
        P(GY, None, None),
        P(ROWS, None),
        P(ROWS, None),
        P(ROWS, None),
    )
    out_specs = P(ROWS, GY)
    return jax.shard_map(shards, mesh=fine, in_specs=in_specs, out_specs=out_specs, check_vma=False)
```
